512 devices in a mesh: ctx: 128 (over z, x, core), head: 4 (over y).
Axes of the slice: x: 4, y: 4, z: 16, core: 2. Of those that a mesh axis runs over, the one named last changes fastest.
Arguments:
- queries: bfloat16 [65536, 1024], P('ctx', 'head'), may hold values from -16 to 16
- keys: bfloat16 [65536, 128], P('ctx'), may hold values from -8 to 8
- values: bfloat16 [65536, 128], P('ctx'), may hold values from -6 to 6
- d_out: bfloat16 [65536, 1024], P('ctx', 'head'), may hold values from -6 to 6
- doc_lengths: int32 [128], replicated, may hold values from 1 to 1536, 65536 in all
Outputs:
- attended: bfloat16 [65536, 1024], P('ctx', 'head')
- d_queries: bfloat16 [65536, 1024], P('ctx', 'head')
- d_keys: bfloat16 [65536, 128], P('ctx')
- d_values: bfloat16 [65536, 128], P('ctx')
The draws below stay inside these ranges and needn't reach their ends.
Inputs may be any that keep to these rules, and one draw needn't show every extreme that they name: `doc_lengths`: the documents lie end to end in order and their lengths sum to 65536; the longest is exactly 1536 tokens.
All inputs are finite; a program needn't handle non-finite values.
Results may differ from the reference program's by a relative error of at most 0.024.
Values may be sent and summed in bfloat16 or wider, within the bound.
No kernel may reach another device: no remote copies, remote signals or barrier semaphores. Data moves between devices by JAX's collectives and lax.ppermute only.
A program may use at most 64 MiB of HBM per device.

```python
import math
import jax
import jax.numpy as jnp
import numpy as np
from jax import lax

HD = 128
HEADS = 8
TOK_DEV = 512
SPAN = 3
TOKENS = 65536
DOCS = 128
N_CTX = 128


def draw_keys(key, part):
    key = jax.random.fold_in(key, 3)
    result = jnp.clip(jax.random.normal(key, (TOKENS, HD), jnp.float32), -4.0, 4.0)
    return result.astype(jnp.bfloat16)


def draw_queries(key, part):
    key = jax.random.fold_in(key, 5)
    result = jnp.clip(jax.random.normal(key, (TOKENS, HEADS, HD), jnp.float32), -4.0, 4.0)
    return result.reshape(TOKENS, HEADS * HD).astype(jnp.bfloat16)


def levels(own_key, extent, pieces, least, top_value):
    gain = 1.0
    for position, parts in pieces:
        steps = jax.random.uniform(jax.random.fold_in(jax.random.fold_in(own_key, 6), position), (parts,), jnp.float32, least / len(pieces), top_value / len(pieces))
        gain = gain * jnp.repeat(jnp.exp(steps), extent[position] // parts).reshape((-1,) + (1,) * (len(extent) - 1 - position))
    return gain


def length_profile(amount, total, most, skew):
    loads = [(1 << 20) // math.isqrt(grade ** skew) + 1 for grade in range(2, amount + 1)]
    rest, holding = total - most - (amount - 1), [1] * (amount - 1)
    while rest > 0:
        candidates = [i for i in range(amount - 1) if holding[i] < most]
        whole, budget = sum([loads[i] for i in candidates]), rest
        for i in candidates:
            extra = min(most - holding[i], max(1, budget * loads[i] // whole), rest)
            holding[i] = holding[i] + extra
            rest = rest - extra
    return np.array([most] + holding)


def uneven(rng, number_of, total, bound, slope):
    if number_of == 2:
        one = jax.random.randint(rng, (), max(1, total - bound), min(bound, total - 1) + 1)
        return jnp.stack([one, total - one])
    lengths = jnp.asarray(length_profile(number_of, total, bound, slope), jnp.int32)
    couples = (number_of - 1) // 2
    source_of, receiver = lengths[1:1 + 2 * couples:2], lengths[2:2 + 2 * couples:2]
    margin = jnp.minimum(source_of - 1, bound - receiver)
    passed = jax.random.randint(jax.random.fold_in(rng, 1), (couples,), 0, 1 << 20) % (margin + 1)
    lengths = lengths.at[1:1 + 2 * couples:2].set(source_of - passed).at[2:2 + 2 * couples:2].set(receiver + passed)
    return lengths[jax.random.permutation(jax.random.fold_in(rng, 2), number_of)]


def centred(rng, dims, spread, limit, pieces=(), kind=jnp.bfloat16):
    factor_of = levels(rng, dims, pieces, -0.22, 0.18) if pieces else 1.0
    drawn = jax.random.normal(rng, dims, jnp.float32) * spread * factor_of
    return jnp.minimum(jnp.maximum(drawn, -limit), limit).astype(kind)


def setup_inputs(seed: int = 0) -> dict:
    key_list = jax.random.split(jax.random.key(seed), 6)
    queries = draw_queries(jax.random.fold_in(key_list[5], 71), 0)
    keys = draw_keys(jax.random.fold_in(key_list[5], 71), 0)
    values = centred(key_list[2], (TOKENS, HD), 1.0, 6.0, ((0, 128),))
    d_out = centred(key_list[3], (TOKENS, HEADS * HD), 1.0, 6.0, ((0, 128), (1, 4)))
    doc_lengths = uneven(key_list[4], DOCS, TOKENS, SPAN * TOK_DEV, 2).astype(jnp.int32)
    return {"queries": queries, "keys": keys, "values": values, "d_out": d_out, "doc_lengths": doc_lengths}


def reference(queries, keys, values, d_out, doc_lengths):
    score_scale = 1.0 / math.sqrt(HD)
    doc_ends = jnp.cumsum(doc_lengths).astype(jnp.int32)
    window_rows = (SPAN + 1) * TOK_DEV
    lead_rows = SPAN * TOK_DEV
    keys_padded = jnp.concatenate([jnp.zeros((lead_rows, HD), keys.dtype), keys], 0)
    values_padded = jnp.concatenate([jnp.zeros((lead_rows, HD), values.dtype), values], 0)
    query_heads = queries.reshape(TOKENS, HEADS, HD)
    grad_heads = d_out.reshape(TOKENS, HEADS, HD)

    def one_block(state, block_index):
        key_grads, value_grads = state
        diagonal = (block_index * TOK_DEV).astype(jnp.int32)
        positions = diagonal + jnp.arange(TOK_DEV, dtype=jnp.int32)
        doc_start = lax.optimization_barrier(jnp.sum(jnp.where(doc_ends[None, :] <= positions[:, None], doc_lengths[None, :], 0), axis=1))
        key_positions = diagonal - lead_rows + jnp.arange(window_rows, dtype=jnp.int32)
        allowed = (key_positions[None, :] >= doc_start[:, None]) & (key_positions[None, :] <= positions[:, None])
        query_block = lax.dynamic_slice_in_dim(query_heads, diagonal, TOK_DEV, 0).astype(jnp.float32)
        grad_block = lax.dynamic_slice_in_dim(grad_heads, diagonal, TOK_DEV, 0).astype(jnp.float32)
        key_window = lax.dynamic_slice_in_dim(keys_padded, diagonal, window_rows, 0).astype(jnp.float32)
        value_window = lax.dynamic_slice_in_dim(values_padded, diagonal, window_rows, 0).astype(jnp.float32)
        scores = jnp.einsum('thd,jd->htj', query_block, key_window) * score_scale
        scores = jnp.where(allowed[None], scores, -jnp.inf)
        row_max = lax.optimization_barrier(jnp.max(scores, axis=2, keepdims=True))
        log_total = row_max + jnp.log(lax.optimization_barrier(jnp.sum(jnp.exp(scores - row_max), axis=2, keepdims=True)))
        exponent = jnp.exp(scores - log_total)
        weights = lax.optimization_barrier(exponent.astype(jnp.bfloat16)).astype(jnp.float32)
        attended = jnp.einsum('htj,jd->thd', weights, value_window).astype(jnp.bfloat16)
        attended_wide = lax.optimization_barrier(attended).astype(jnp.float32)
        row_dot = lax.optimization_barrier(jnp.sum(grad_block * attended_wide, axis=2))
        d_weights = jnp.einsum('thd,jd->htj', grad_block, value_window)
        d_scores = exponent * (d_weights - jnp.transpose(row_dot)[:, :, None])
        d_scores = lax.optimization_barrier(d_scores.astype(jnp.bfloat16)).astype(jnp.float32)
        d_queries = (jnp.einsum('htj,jd->thd', d_scores, key_window) * score_scale).astype(jnp.bfloat16)
        key_terms = jnp.einsum('htj,thd->jd', d_scores, query_block) * score_scale
        value_terms = jnp.einsum('htj,thd->jd', weights, grad_block)
        key_grads = lax.dynamic_update_slice_in_dim(key_grads, lax.dynamic_slice_in_dim(key_grads, diagonal, window_rows, 0) + key_terms, diagonal, 0)
        value_grads = lax.dynamic_update_slice_in_dim(value_grads, lax.dynamic_slice_in_dim(value_grads, diagonal, window_rows, 0) + value_terms, diagonal, 0)
        return ((key_grads, value_grads), (attended, d_queries))
    start_state = (jnp.zeros((TOKENS + lead_rows, HD), jnp.float32), jnp.zeros((TOKENS + lead_rows, HD), jnp.float32))
    (key_grads, value_grads), (attended, d_queries) = lax.scan(one_block, start_state, jnp.arange(N_CTX, dtype=jnp.int32))
    attended = attended.reshape(TOKENS, HEADS * HD)
    d_queries = d_queries.reshape(TOKENS, HEADS * HD)
    d_keys = key_grads[lead_rows:].astype(jnp.bfloat16)
    d_values = value_grads[lead_rows:].astype(jnp.bfloat16)
    return (attended, d_queries, d_keys, d_values)
```

```python
import functools
import math

import jax
import jax.numpy as jnp
from jax import lax
from jax.experimental import pallas as pl
from jax.experimental.pallas import tpu as pltpu
from jax.sharding import PartitionSpec as P

SPAN = 3
TILE = 256
BF = jnp.bfloat16
F32 = jnp.float32


def dot_nt(a, b):
    return lax.dot_general(a, b, (((1,), (1,)), ((), ())), preferred_element_type=F32)


def dot_nn(a, b):
    return jnp.dot(a, b, preferred_element_type=F32)


def attention_kernel(
    place_ref,
    lengths_ref,
    q_ref,
    do_ref,
    own_ref,
    two_ref,
    mixed_ref,
    swapped_ref,
    att_ref,
    dq_ref,
    own_part_ref,
    two_part_ref,
    mixed_part_ref,
    swapped_part_ref,
    window,
    parts,
    tiles,
    starts,
    top,
    total,
    out_sum,
    dq_sum,
    qt,
    dot_,
):
    rows, width = q_ref.shape
    head = own_ref.shape[1] // 2
    heads = width // head
    lead = SPAN * rows
    n_tiles = (lead + rows) // TILE
    scale = 1.0 / math.sqrt(head)
    to_exp2 = scale * math.log2(math.e)
    device = place_ref[0]
    odd = lax.rem(device, 2)
    mixed_row = pl.multiple_of(jnp.where(odd == 1, lead - rows, 0), rows)
    swapped_row = pl.multiple_of(jnp.where(odd == 1, 0, lead - rows), rows)

    window[pl.ds(lead, rows), :] = own_ref[...]
    window[pl.ds(lead - 2 * rows, rows), :] = two_ref[...]
    window[pl.ds(mixed_row, rows), :] = mixed_ref[...]
    window[pl.ds(swapped_row, rows), :] = swapped_ref[...]

    lengths = lengths_ref[...]
    docs = lengths.shape[1]
    along = jnp.broadcast_to(lengths.astype(F32), (docs, docs))
    earlier = lax.broadcasted_iota(jnp.int32, (docs, docs), 0)
    later = lax.broadcasted_iota(jnp.int32, (docs, docs), 1)
    ends = jnp.sum(jnp.where(earlier <= later, along.T, 0.0), axis=0, keepdims=True)
    first = (device * rows).astype(F32)
    positions = first + lax.broadcasted_iota(jnp.int32, (rows, docs), 0).astype(F32)
    doc_start = jnp.sum(
        jnp.where(ends <= positions, lengths.astype(F32), 0.0), axis=1, keepdims=True
    )
    start_row = (doc_start - (first - lead)).astype(jnp.int32)
    starts[...] = jnp.broadcast_to(start_row, (rows, TILE))
    low = jnp.minimum(jnp.maximum(jnp.min(start_row), 0) // TILE, n_tiles - 1)

    top[...] = jnp.full(top.shape, -jnp.inf, F32)
    total[...] = jnp.zeros(total.shape, F32)
    out_sum[...] = jnp.zeros(out_sum.shape, F32)
    dq_sum[...] = jnp.zeros(dq_sum.shape, F32)
    for h in range(heads):
        cols = pl.ds(h * head, head)
        qt[h] = q_ref[:, cols].T
        dot_[h] = do_ref[:, cols].T

    column = lax.broadcasted_iota(jnp.int32, (rows, TILE), 1)
    row = lax.broadcasted_iota(jnp.int32, (rows, TILE), 0) + lead

    def score_tile(t, carry):
        at = pl.multiple_of(t * TILE, TILE)
        keys = window[pl.ds(at, TILE), pl.ds(0, head)]
        key = column + t * TILE
        allowed = (key >= starts[...]) & (key <= row)
        for h in range(heads):
            s = dot_nt(q_ref[:, pl.ds(h * head, head)], keys)
            s = jnp.where(allowed, s, -jnp.inf)
            tiles[h, t] = s
            m = top[h]
            for c in range(0, TILE, head):
                m = jnp.maximum(m, s[:, c : c + head])
            top[h] = m
        return carry

    lax.fori_loop(low, n_tiles, score_tile, 0)

    for h in range(heads):
        top[h] = jnp.broadcast_to(jnp.max(top[h], axis=1, keepdims=True), (rows, head))

    def wide(x):
        return jnp.concatenate([x] * (TILE // head), axis=1)

    def out_tile(t, carry):
        at = pl.multiple_of(t * TILE, TILE)
        values = window[pl.ds(at, TILE), pl.ds(head, head)]
        for h in range(heads):
            e = jnp.exp2((tiles[h, t] - wide(top[h])) * to_exp2)
            tiles[h, t] = e
            m = total[h]
            for c in range(0, TILE, head):
                m = m + e[:, c : c + head]
            total[h] = m
            out_sum[h] += dot_nn(e.astype(BF), values)
        return carry

    lax.fori_loop(low, n_tiles, out_tile, 0)

    for h in range(heads):
        cols = pl.ds(h * head, head)
        inverse = 1.0 / jnp.sum(total[h], axis=1, keepdims=True)
        attended = (out_sum[h] * inverse).astype(BF)
        att_ref[:, cols] = attended
        row_dot = jnp.sum(
            do_ref[:, cols].astype(F32) * attended.astype(F32), axis=1, keepdims=True
        )
        total[h] = jnp.broadcast_to(inverse, (rows, head))
        top[h] = jnp.broadcast_to(row_dot, (rows, head))

    def zero_tile(t, carry):
        at = pl.multiple_of(t * TILE, TILE)
        parts[pl.ds(at, TILE), :] = jnp.zeros((TILE, 2 * head), BF)
        return carry

    lax.fori_loop(0, low, zero_tile, 0)

    def grad_tile(t, carry):
        at = pl.multiple_of(t * TILE, TILE)
        keys = window[pl.ds(at, TILE), pl.ds(0, head)]
        values = window[pl.ds(at, TILE), pl.ds(head, head)]
        dv = jnp.zeros((head, TILE), F32)
        dk = jnp.zeros((head, TILE), F32)
        for h in range(heads):
            dw = dot_nt(do_ref[:, pl.ds(h * head, head)], values)
            w = tiles[h, t] * wide(total[h])
            ds = (w * (dw - wide(top[h]))).astype(BF)
            dv = dv + dot_nn(dot_[h], w.astype(BF))
            dk = dk + dot_nn(qt[h], ds)
            dq_sum[h] += dot_nn(ds, keys)
        parts[pl.ds(at, TILE), pl.ds(0, head)] = (dk * scale).T.astype(BF)
        parts[pl.ds(at, TILE), pl.ds(head, head)] = dv.T.astype(BF)
        return carry

    lax.fori_loop(low, n_tiles, grad_tile, 0)

    for h in range(heads):
        dq_ref[:, pl.ds(h * head, head)] = (dq_sum[h] * scale).astype(BF)
    own_part_ref[...] = parts[pl.ds(lead, rows), :]
    two_part_ref[...] = parts[pl.ds(lead - 2 * rows, rows), :]
    mixed_part_ref[...] = parts[pl.ds(mixed_row, rows), :]
    swapped_part_ref[...] = parts[pl.ds(swapped_row, rows), :]


def attention(place, lengths, q, do, own, two, mixed, swapped):
    rows, width = q.shape
    head = own.shape[1] // 2
    heads = width // head
    span = (SPAN + 1) * rows
    vmem = pl.BlockSpec(memory_space=pltpu.VMEM)
    like_q = jax.ShapeDtypeStruct(q.shape, BF)
    like_kv = jax.ShapeDtypeStruct(own.shape, BF)
    return pl.pallas_call(
        attention_kernel,
        out_shape=(like_q, like_q) + (like_kv,) * 4,
        in_specs=[pl.BlockSpec(memory_space=pltpu.SMEM)] + [vmem] * 7,
        out_specs=(vmem,) * 6,
        scratch_shapes=[
            pltpu.VMEM((span, 2 * head), BF),
            pltpu.VMEM((span, 2 * head), BF),
            pltpu.VMEM((heads, span // TILE, rows, TILE), F32),
            pltpu.VMEM((rows, TILE), jnp.int32),
            pltpu.VMEM((heads, rows, head), F32),
            pltpu.VMEM((heads, rows, head), F32),
            pltpu.VMEM((heads, rows, head), F32),
            pltpu.VMEM((heads, rows, head), F32),
            pltpu.VMEM((heads, head, rows), BF),
            pltpu.VMEM((heads, head, rows), BF),
        ],
        compiler_params=pltpu.CompilerParams(vmem_limit_bytes=40 << 20),
        cost_estimate=pl.CostEstimate(
            flops=6_000_000_000, bytes_accessed=4 << 20, transcendentals=2 << 20
        ),
        name="attention",
    )(place, lengths, q, do, own, two, mixed, swapped)


def moved(value, pairs):
    return lax.ppermute(value, "ctx", pairs)


def on_device(queries, keys, values, d_out, doc_lengths):
    count = lax.axis_size("ctx")
    head = keys.shape[1]
    place = lax.axis_index("ctx").reshape(1).astype(jnp.int32)
    two_on = [(i, i + 2) for i in range(count - 2)]
    mixed_on = [(i, i + (3 if i % 2 else 1)) for i in range(count) if i + (3 if i % 2 else 1) < count]
    across = [(i, i ^ 1) for i in range(count)]

    def back(pairs):
        return [(there, here) for here, there in pairs]

    own = jnp.concatenate([keys, values], axis=1)
    two = moved(own, two_on)
    mixed = moved(own, mixed_on)
    swapped = moved(two, across)
    attended, d_queries, own_part, two_part, mixed_part, swapped_part = attention(
        place, doc_lengths.reshape(1, -1), queries, d_out, own, two, mixed, swapped
    )
    from_core = moved(swapped_part, across)
    from_mixed = moved(mixed_part, back(mixed_on))
    passed = (two_part.astype(F32) + from_core.astype(F32)).astype(BF)
    from_two = moved(passed, back(two_on))
    mine = (own_part.astype(F32) + from_mixed.astype(F32) + from_two.astype(F32)).astype(BF)
    everyone = lax.all_gather(mine, "head", axis=0)
    summed = jnp.sum(everyone.astype(F32), axis=0).astype(BF)
    return (attended, d_queries, summed[:, :head], summed[:, head:])


def solution(mesh):
    in_specs = (P("ctx", "head"), P("ctx", None), P("ctx", None), P("ctx", "head"), P())
    out_specs = (P("ctx", "head"), P("ctx", "head"), P("ctx", None), P("ctx", None))
    return jax.shard_map(
        on_device, mesh=mesh, in_specs=in_specs, out_specs=out_specs, check_vma=False
    )
```

```python
import functools
import math

import jax
import jax.numpy as jnp
from jax import lax
from jax.experimental import pallas as pl
from jax.experimental.pallas import tpu as pltpu
from jax.sharding import PartitionSpec as P

SPAN = 3
TILE = 256
BF = jnp.bfloat16
F32 = jnp.float32


def dot_nt(a, b):
    return lax.dot_general(a, b, (((1,), (1,)), ((), ())), preferred_element_type=F32)


def dot_nn(a, b):
    return jnp.dot(a, b, preferred_element_type=F32)


def attention_kernel(
    place_ref,
    lengths_ref,
    q_ref,
    do_ref,
    own_ref,
    two_ref,
    mixed_ref,
    swapped_ref,
    att_ref,
    dq_ref,
    own_part_ref,
    two_part_ref,
    mixed_part_ref,
    swapped_part_ref,
    key_window,
    value_window,
    key_parts,
    value_parts,
    tiles,
    starts,
    top,
    total,
    out_sum,
    dq_sum,
    qt,
    dot_,
):
    rows, width = q_ref.shape
    head = own_ref.shape[1]
    heads = width // head
    lead = SPAN * rows
    n_tiles = (lead + rows) // TILE
    scale = 1.0 / math.sqrt(head)
    to_exp2 = scale * math.log2(math.e)
    device = place_ref[0]
    odd = lax.rem(device, 2)
    mixed_row = pl.multiple_of(jnp.where(odd == 1, lead - rows, 0), rows)
    swapped_row = pl.multiple_of(jnp.where(odd == 1, 0, lead - rows), rows)

    slots = (
        (own_ref, own_part_ref, lead),
        (two_ref, two_part_ref, lead - 2 * rows),
        (mixed_ref, mixed_part_ref, mixed_row),
        (swapped_ref, swapped_part_ref, swapped_row),
    )
    for block, _, at in slots:
        key_window[pl.ds(at, rows), :] = block[pl.ds(0, rows), :]
        value_window[pl.ds(at, rows), :] = block[pl.ds(rows, rows), :]

    lengths = lengths_ref[...]
    docs = lengths.shape[1]
    along = jnp.broadcast_to(lengths.astype(F32), (docs, docs))
    earlier = lax.broadcasted_iota(jnp.int32, (docs, docs), 0)
    later = lax.broadcasted_iota(jnp.int32, (docs, docs), 1)
    ends = jnp.sum(jnp.where(earlier <= later, along.T, 0.0), axis=0, keepdims=True)
    first = (device * rows).astype(F32)
    positions = first + lax.broadcasted_iota(jnp.int32, (rows, docs), 0).astype(F32)
    doc_start = jnp.sum(
        jnp.where(ends <= positions, lengths.astype(F32), 0.0), axis=1, keepdims=True
    )
    start_row = (doc_start - (first - lead)).astype(jnp.int32)
    starts[...] = jnp.broadcast_to(start_row, (rows, TILE))
    low = jnp.minimum(jnp.maximum(jnp.min(start_row), 0) // TILE, n_tiles - 1)

    top[...] = jnp.full(top.shape, -jnp.inf, F32)
    total[...] = jnp.zeros(total.shape, F32)
    out_sum[...] = jnp.zeros(out_sum.shape, F32)
    dq_sum[...] = jnp.zeros(dq_sum.shape, F32)
    for h in range(heads):
        cols = pl.ds(h * head, head)
        qt[h] = q_ref[:, cols].T
        dot_[h] = do_ref[:, cols].T

    column = lax.broadcasted_iota(jnp.int32, (rows, TILE), 1)
    row = lax.broadcasted_iota(jnp.int32, (rows, TILE), 0) + lead

    def score_tile(t, carry):
        at = pl.multiple_of(t * TILE, TILE)
        keys = key_window[pl.ds(at, TILE), :]
        key = column + t * TILE
        allowed = (key >= starts[...]) & (key <= row)
        for h in range(heads):
            s = dot_nt(q_ref[:, pl.ds(h * head, head)], keys)
            s = jnp.where(allowed, s, -jnp.inf)
            tiles[h, t] = s
            m = top[h]
            for c in range(0, TILE, head):
                m = jnp.maximum(m, s[:, c : c + head])
            top[h] = m
        return carry

    lax.fori_loop(low, n_tiles, score_tile, 0)

    for h in range(heads):
        top[h] = jnp.broadcast_to(jnp.max(top[h], axis=1, keepdims=True), (rows, head))

    def wide(x):
        return jnp.concatenate([x] * (TILE // head), axis=1)

    def out_tile(t, carry):
        at = pl.multiple_of(t * TILE, TILE)
        values = value_window[pl.ds(at, TILE), :]
        for h in range(heads):
            e = jnp.exp2((tiles[h, t] - wide(top[h])) * to_exp2)
            tiles[h, t] = e
            m = total[h]
            for c in range(0, TILE, head):
                m = m + e[:, c : c + head]
            total[h] = m
            out_sum[h] += dot_nn(e.astype(BF), values)
        return carry

    lax.fori_loop(low, n_tiles, out_tile, 0)

    for h in range(heads):
        cols = pl.ds(h * head, head)
        inverse = 1.0 / jnp.sum(total[h], axis=1, keepdims=True)
        attended = (out_sum[h] * inverse).astype(BF)
        att_ref[:, cols] = attended
        row_dot = jnp.sum(
            do_ref[:, cols].astype(F32) * attended.astype(F32), axis=1, keepdims=True
        )
        total[h] = jnp.broadcast_to(inverse, (rows, head))
        top[h] = jnp.broadcast_to(row_dot, (rows, head))

    def zero_tile(t, carry):
        at = pl.multiple_of(t * TILE, TILE)
        key_parts[pl.ds(at, TILE), :] = jnp.zeros((TILE, head), BF)
        value_parts[pl.ds(at, TILE), :] = jnp.zeros((TILE, head), BF)
        return carry

    lax.fori_loop(0, low, zero_tile, 0)

    def grad_tile(t, carry):
        at = pl.multiple_of(t * TILE, TILE)
        keys = key_window[pl.ds(at, TILE), :]
        values = value_window[pl.ds(at, TILE), :]
        dv = jnp.zeros((head, TILE), F32)
        dk = jnp.zeros((head, TILE), F32)
        for h in range(heads):
            dw = dot_nt(do_ref[:, pl.ds(h * head, head)], values)
            w = tiles[h, t] * wide(total[h])
            ds = (w * (dw - wide(top[h]))).astype(BF)
            dv = dv + dot_nn(dot_[h], w.astype(BF))
            dk = dk + dot_nn(qt[h], ds)
            dq_sum[h] += dot_nn(ds, keys)
        key_parts[pl.ds(at, TILE), :] = (dk * scale).T.astype(BF)
        value_parts[pl.ds(at, TILE), :] = dv.T.astype(BF)
        return carry

    lax.fori_loop(low, n_tiles, grad_tile, 0)

    for h in range(heads):
        dq_ref[:, pl.ds(h * head, head)] = (dq_sum[h] * scale).astype(BF)
    for _, part, at in slots:
        part[pl.ds(0, rows), :] = key_parts[pl.ds(at, rows), :]
        part[pl.ds(rows, rows), :] = value_parts[pl.ds(at, rows), :]


def attention(place, lengths, q, do, own, two, mixed, swapped):
    rows, width = q.shape
    head = own.shape[1]
    heads = width // head
    span = (SPAN + 1) * rows
    vmem = pl.BlockSpec(memory_space=pltpu.VMEM)
    like_q = jax.ShapeDtypeStruct(q.shape, BF)
    like_kv = jax.ShapeDtypeStruct(own.shape, BF)
    return pl.pallas_call(
        attention_kernel,
        out_shape=(like_q, like_q) + (like_kv,) * 4,
        in_specs=[pl.BlockSpec(memory_space=pltpu.SMEM)] + [vmem] * 7,
        out_specs=(vmem,) * 6,
        scratch_shapes=[
            pltpu.VMEM((span, head), BF),
            pltpu.VMEM((span, head), BF),
            pltpu.VMEM((span, head), BF),
            pltpu.VMEM((span, head), BF),
            pltpu.VMEM((heads, span // TILE, rows, TILE), F32),
            pltpu.VMEM((rows, TILE), jnp.int32),
            pltpu.VMEM((heads, rows, head), F32),
            pltpu.VMEM((heads, rows, head), F32),
            pltpu.VMEM((heads, rows, head), F32),
            pltpu.VMEM((heads, rows, head), F32),
            pltpu.VMEM((heads, head, rows), BF),
            pltpu.VMEM((heads, head, rows), BF),
        ],
        compiler_params=pltpu.CompilerParams(vmem_limit_bytes=40 << 20),
        cost_estimate=pl.CostEstimate(
            flops=6_000_000_000, bytes_accessed=4 << 20, transcendentals=2 << 20
        ),
        name="attention",
    )(place, lengths, q, do, own, two, mixed, swapped)


def pack_kernel(key_ref, value_ref, both_ref, sems):
    rows = key_ref.shape[0]
    copies = [
        pltpu.make_async_copy(key_ref, both_ref.at[pl.ds(0, rows)], sems.at[0]),
        pltpu.make_async_copy(value_ref, both_ref.at[pl.ds(rows, rows)], sems.at[1]),
    ]
    for copy in copies:
        copy.start()
    for copy in copies:
        copy.wait()


def packed(keys, values):
    rows, head = keys.shape
    return pl.pallas_call(
        pack_kernel,
        out_shape=jax.ShapeDtypeStruct((2 * rows, head), BF),
        in_specs=[pl.BlockSpec(memory_space=pl.ANY)] * 2,
        out_specs=pl.BlockSpec(memory_space=pltpu.VMEM),
        scratch_shapes=[pltpu.SemaphoreType.DMA((2,))],
        name="pack",
    )(keys, values)


def head_sum(part):
    heads = lax.axis_size("head")
    pieces = part.reshape(heads, part.shape[0] // heads, part.shape[1])
    theirs = lax.all_to_all(pieces, "head", split_axis=0, concat_axis=0)
    mine = jnp.sum(theirs.astype(F32), axis=0).astype(BF)
    mine = jnp.broadcast_to(mine[None], pieces.shape)
    return lax.all_to_all(mine, "head", split_axis=0, concat_axis=0).reshape(part.shape)


def moved(value, pairs):
    return lax.ppermute(value, "ctx", pairs)


def on_device(queries, keys, values, d_out, doc_lengths):
    count = lax.axis_size("ctx")
    rows = keys.shape[0]
    place = lax.axis_index("ctx").reshape(1).astype(jnp.int32)
    two_on = [(i, i + 2) for i in range(count - 2)]
    mixed_on = [(i, i + (3 if i % 2 else 1)) for i in range(count) if i + (3 if i % 2 else 1) < count]
    across = [(i, i ^ 1) for i in range(count)]

    def back(pairs):
        return [(there, here) for here, there in pairs]

    own = packed(keys, values)
    two = moved(own, two_on)
    mixed = moved(own, mixed_on)
    swapped = moved(two, across)
    attended, d_queries, own_part, two_part, mixed_part, swapped_part = attention(
        place, doc_lengths.reshape(1, -1), queries, d_out, own, two, mixed, swapped
    )
    from_core = moved(swapped_part, across)
    from_mixed = moved(mixed_part, back(mixed_on))
    passed = (two_part.astype(F32) + from_core.astype(F32)).astype(BF)
    from_two = moved(passed, back(two_on))
    mine = (own_part.astype(F32) + from_mixed.astype(F32) + from_two.astype(F32)).astype(BF)
    summed = head_sum(mine)
    return (attended, d_queries, summed[:rows], summed[rows:])


def solution(mesh):
    in_specs = (P("ctx", "head"), P("ctx", None), P("ctx", None), P("ctx", "head"), P())
    out_specs = (P("ctx", "head"), P("ctx", "head"), P("ctx", None), P("ctx", None))
    return jax.shard_map(
        on_device, mesh=mesh, in_specs=in_specs, out_specs=out_specs, check_vma=False
    )
```

```python
import functools
import math

import jax
import jax.numpy as jnp
from jax import lax
from jax.experimental import pallas as pl
from jax.experimental.pallas import tpu as pltpu
from jax.sharding import PartitionSpec as P

SPAN = 3
BF = jnp.bfloat16
F32 = jnp.float32


def dot_nt(a, b):
    return lax.dot_general(a, b, (((1,), (1,)), ((), ())), preferred_element_type=F32)


def dot_nn(a, b):
    return jnp.dot(a, b, preferred_element_type=F32)


def diagonal_kernel(
    place_ref, lengths_ref, q_ref, do_ref, own_ref,
    first_ref, starts_ref, top_ref, total_ref, out_ref, qt_ref, dot_ref,
):
    rows, width = q_ref.shape
    head = own_ref.shape[1]
    heads = width // head
    lead = SPAN * rows
    lengths = lengths_ref[...].astype(F32)
    docs = lengths.shape[1]
    along = jnp.broadcast_to(lengths, (docs, docs))
    earlier = lax.broadcasted_iota(jnp.int32, (docs, docs), 0)
    later = lax.broadcasted_iota(jnp.int32, (docs, docs), 1)
    ends = jnp.sum(jnp.where(earlier <= later, along.T, 0.0), axis=0, keepdims=True)
    begin = (place_ref[0] * rows).astype(F32)
    positions = begin + lax.broadcasted_iota(jnp.int32, (rows, docs), 0).astype(F32)
    doc_start = jnp.sum(jnp.where(ends <= positions, lengths, 0.0), axis=1, keepdims=True)
    start = (doc_start - begin).astype(jnp.int32)
    starts_ref[...] = jnp.broadcast_to(start, starts_ref.shape)
    first_ref[0] = jnp.min(start) + lead

    column = lax.broadcasted_iota(jnp.int32, (rows, rows), 1)
    row = lax.broadcasted_iota(jnp.int32, (rows, rows), 0)
    allowed = (column >= start) & (column <= row)
    keys = own_ref[pl.ds(0, rows), :]
    values = own_ref[pl.ds(rows, rows), :]
    for h in range(heads):
        cols = pl.ds(h * head, head)
        s = jnp.where(allowed, dot_nt(q_ref[:, cols], keys), -jnp.inf)
        m = jnp.max(s, axis=1, keepdims=True)
        e = jnp.exp2((s - m) * exp2_scale(head))
        top_ref[h] = jnp.broadcast_to(m, (rows, head))
        total_ref[h] = jnp.broadcast_to(jnp.sum(e, axis=1, keepdims=True), (rows, head))
        out_ref[h] = dot_nn(e.astype(BF), values)
        qt_ref[h] = q_ref[:, cols].T
        dot_ref[h] = do_ref[:, cols].T


def earlier_kernel(
    place_ref, first_ref, q_ref, do_ref, qt_ref, dot_ref, starts_ref, top0_ref, total0_ref, out0_ref,
    two_ref, mixed_ref, swapped_ref,
    att_ref, top_ref, inverse_ref, row_dot_ref, dq_ref, two_part_ref, mixed_part_ref, swapped_part_ref,
    key_window, value_window, key_parts, value_parts, tiles, lanes,
):
    rows, width = q_ref.shape
    head = two_ref.shape[1]
    heads = width // head
    to_exp2 = exp2_scale(head)
    scale = score_scale(head)
    odd = lax.rem(place_ref[0], 2)
    last = (SPAN - 1) * rows
    mixed_row = pl.multiple_of(jnp.where(odd == 1, last, 0), rows)
    swapped_row = pl.multiple_of(jnp.where(odd == 1, 0, last), rows)
    slots = (
        (two_ref, two_part_ref, last - rows),
        (mixed_ref, mixed_part_ref, mixed_row),
        (swapped_ref, swapped_part_ref, swapped_row),
    )
    low = jnp.minimum(jnp.maximum(first_ref[0], 0) // rows, SPAN)
    column = lax.broadcasted_iota(jnp.int32, (rows, rows), 1)

    def wide(x):
        return jnp.concatenate([x] * (rows // head), axis=1)

    def folded(x, op):
        parts = [x[:, c : c + head] for c in range(0, rows, head)]
        return functools.reduce(op, parts)

    def score_tile(t, carry):
        at = pl.multiple_of(t * rows, rows)
        keys = key_window[pl.ds(at, rows), :]
        allowed = column >= wide(starts_ref[...] + (SPAN * rows - at))
        for h in range(heads):
            s = dot_nt(q_ref[:, pl.ds(h * head, head)], keys)
            s = jnp.where(allowed, s, -jnp.inf)
            tiles[h, t] = s
            lanes[h] = jnp.maximum(lanes[h], folded(s, jnp.maximum))
        return carry

    def out_tile(t, carry):
        at = pl.multiple_of(t * rows, rows)
        values = value_window[pl.ds(at, rows), :]
        for h in range(heads):
            e = jnp.exp2((tiles[h, t] - wide(top_ref[h])) * to_exp2)
            tiles[h, t] = e
            lanes[h] += folded(e, jnp.add)
            dq_ref[h] += dot_nn(e.astype(BF), values)
        return carry

    def grad_tile(t, carry):
        at = pl.multiple_of(t * rows, rows)
        keys = key_window[pl.ds(at, rows), :]
        values = value_window[pl.ds(at, rows), :]
        dv = jnp.zeros((head, rows), F32)
        dk = jnp.zeros((head, rows), F32)
        for h in range(heads):
            dw = dot_nt(do_ref[:, pl.ds(h * head, head)], values)
            w = tiles[h, t] * wide(inverse_ref[h])
            ds = (w * (dw - wide(row_dot_ref[h]))).astype(BF)
            dv = dv + dot_nn(dot_ref[h], w.astype(BF))
            dk = dk + dot_nn(qt_ref[h], ds)
            dq_ref[h] += dot_nn(ds, keys)
        key_parts[pl.ds(at, rows), :] = (dk * scale).T.astype(BF)
        value_parts[pl.ds(at, rows), :] = dv.T.astype(BF)
        return carry

    def zero_tile(t, carry):
        at = pl.multiple_of(t * rows, rows)
        key_parts[pl.ds(at, rows), :] = jnp.zeros((rows, head), BF)
        value_parts[pl.ds(at, rows), :] = jnp.zeros((rows, head), BF)
        return carry

    reaches = low < SPAN

    @pl.when(reaches)
    def _():
        for block, _, at in slots:
            key_window[pl.ds(at, rows), :] = block[pl.ds(0, rows), :]
            value_window[pl.ds(at, rows), :] = block[pl.ds(rows, rows), :]
        lanes[...] = top0_ref[...]
        lax.fori_loop(low, SPAN, score_tile, 0)
        for h in range(heads):
            top = jnp.broadcast_to(jnp.max(lanes[h], axis=1, keepdims=True), (rows, head))
            top_ref[h] = top
            kept = jnp.exp2((top0_ref[h] - top) * to_exp2)
            inverse_ref[h] = total0_ref[h] * kept
            dq_ref[h] = out0_ref[h] * kept
        lanes[...] = jnp.zeros(lanes.shape, F32)
        lax.fori_loop(low, SPAN, out_tile, 0)
        for h in range(heads):
            inverse_ref[h] += jnp.sum(lanes[h], axis=1, keepdims=True)

    @pl.when(jnp.logical_not(reaches))
    def _():
        top_ref[...] = top0_ref[...]
        inverse_ref[...] = total0_ref[...]
        dq_ref[...] = out0_ref[...]

    for h in range(heads):
        cols = pl.ds(h * head, head)
        inverse = 1.0 / inverse_ref[h]
        inverse_ref[h] = inverse
        attended = (dq_ref[h] * inverse).astype(BF)
        att_ref[:, cols] = attended
        row_dot = jnp.sum(do_ref[:, cols].astype(F32) * attended.astype(F32), axis=1, keepdims=True)
        row_dot_ref[h] = jnp.broadcast_to(row_dot, (rows, head))
    dq_ref[...] = jnp.zeros(dq_ref.shape, F32)
    lax.fori_loop(0, low, zero_tile, 0)
    lax.fori_loop(low, SPAN, grad_tile, 0)
    for _, part, at in slots:
        part[pl.ds(0, rows), :] = key_parts[pl.ds(at, rows), :]
        part[pl.ds(rows, rows), :] = value_parts[pl.ds(at, rows), :]


def own_kernel(
    q_ref, do_ref, qt_ref, dot_ref, own_ref, starts_ref, top_ref, inverse_ref, row_dot_ref, earlier_ref,
    dq_ref, part_ref,
):
    rows, width = q_ref.shape
    head = own_ref.shape[1]
    heads = width // head
    to_exp2 = exp2_scale(head)
    scale = score_scale(head)
    column = lax.broadcasted_iota(jnp.int32, (rows, rows), 1)
    row = lax.broadcasted_iota(jnp.int32, (rows, rows), 0)

    def wide(x):
        return jnp.concatenate([x] * (rows // head), axis=1)

    allowed = (column >= wide(starts_ref[...])) & (column <= row)
    keys = own_ref[pl.ds(0, rows), :]
    values = own_ref[pl.ds(rows, rows), :]
    dv = jnp.zeros((head, rows), F32)
    dk = jnp.zeros((head, rows), F32)
    for h in range(heads):
        cols = pl.ds(h * head, head)
        s = jnp.where(allowed, dot_nt(q_ref[:, cols], keys), -jnp.inf)
        w = jnp.exp2((s - wide(top_ref[h])) * to_exp2) * wide(inverse_ref[h])
        dw = dot_nt(do_ref[:, cols], values)
        ds = (w * (dw - wide(row_dot_ref[h]))).astype(BF)
        dv = dv + dot_nn(dot_ref[h], w.astype(BF))
        dk = dk + dot_nn(qt_ref[h], ds)
        dq_ref[:, cols] = ((earlier_ref[h] + dot_nn(ds, keys)) * scale).astype(BF)
    part_ref[pl.ds(0, rows), :] = (dk * scale).T.astype(BF)
    part_ref[pl.ds(rows, rows), :] = dv.T.astype(BF)


def score_scale(head):
    return 1.0 / math.sqrt(head)


def exp2_scale(head):
    return score_scale(head) * math.log2(math.e)


VMEM = pl.BlockSpec(memory_space=pltpu.VMEM)
SMEM = pl.BlockSpec(memory_space=pltpu.SMEM)


def shape(dims, dtype):
    return jax.ShapeDtypeStruct(dims, dtype)


def on_core(kernel, name, mflop, outs, ins, scratch=()):
    return pl.pallas_call(
        kernel,
        out_shape=tuple(outs),
        in_specs=[SMEM if x.ndim == 1 else VMEM for x in ins],
        out_specs=tuple(SMEM if len(x.shape) == 1 else VMEM for x in outs),
        scratch_shapes=list(scratch),
        compiler_params=pltpu.CompilerParams(vmem_limit_bytes=40 << 20),
        cost_estimate=pl.CostEstimate(
            flops=mflop * 1_000_000, bytes_accessed=2 << 20, transcendentals=1 << 19
        ),
        name=name,
    )(*ins)


def attention_before(place, lengths, q, do, own):
    rows, width = q.shape
    head = own.shape[1]
    heads = width // head
    state = shape((heads, rows, head), F32)
    turned = shape((heads, head, rows), BF)
    outs = [shape((1,), jnp.int32), shape((rows, head), jnp.int32), state, state, state, turned, turned]
    return on_core(diagonal_kernel, "diagonal", 1200, outs, (place, lengths, q, do, own))


def attention_earlier(place, first, q, do, qt, dot_, starts, top, total, out, two, mixed, swapped):
    rows, width = q.shape
    head = two.shape[1]
    heads = width // head
    state = shape((heads, rows, head), F32)
    part = shape(two.shape, BF)
    span = SPAN * rows
    return on_core(
        earlier_kernel,
        "earlier",
        5000,
        [shape(q.shape, BF), state, state, state, state, part, part, part],
        (place, first, q, do, qt, dot_, starts, top, total, out, two, mixed, swapped),
        [pltpu.VMEM((span, head), BF)] * 4
        + [pltpu.VMEM((heads, SPAN, rows, rows), F32), pltpu.VMEM((heads, rows, head), F32)],
    )


def attention_own(q, do, qt, dot_, own, starts, top, inverse, row_dot, dq):
    outs = [shape(q.shape, BF), shape(own.shape, BF)]
    ins = (q, do, qt, dot_, own, starts, top, inverse, row_dot, dq)
    return on_core(own_kernel, "own", 2500, outs, ins)


def pack_kernel(key_ref, value_ref, both_ref, sems):
    rows = key_ref.shape[0]
    copies = [
        pltpu.make_async_copy(key_ref, both_ref.at[pl.ds(0, rows)], sems.at[0]),
        pltpu.make_async_copy(value_ref, both_ref.at[pl.ds(rows, rows)], sems.at[1]),
    ]
    for copy in copies:
        copy.start()
    for copy in copies:
        copy.wait()


def packed(keys, values):
    rows, head = keys.shape
    return pl.pallas_call(
        pack_kernel,
        out_shape=jax.ShapeDtypeStruct((2 * rows, head), BF),
        in_specs=[pl.BlockSpec(memory_space=pl.ANY)] * 2,
        out_specs=pl.BlockSpec(memory_space=pltpu.VMEM),
        scratch_shapes=[pltpu.SemaphoreType.DMA((2,))],
        name="pack",
    )(keys, values)


def head_sum(part):
    heads = lax.axis_size("head")
    pieces = part.reshape(heads, part.shape[0] // heads, part.shape[1])
    theirs = lax.all_to_all(pieces, "head", split_axis=0, concat_axis=0)
    mine = jnp.sum(theirs.astype(F32), axis=0).astype(BF)
    mine = jnp.broadcast_to(mine[None], pieces.shape)
    return lax.all_to_all(mine, "head", split_axis=0, concat_axis=0).reshape(part.shape)


def moved(value, pairs):
    return lax.ppermute(value, "ctx", pairs)


def on_device(queries, keys, values, d_out, doc_lengths):
    count = lax.axis_size("ctx")
    rows = keys.shape[0]
    place = lax.axis_index("ctx").reshape(1).astype(jnp.int32)
    two_on = [(i, i + 2) for i in range(count - 2)]
    mixed_on = [(i, i + (3 if i % 2 else 1)) for i in range(count) if i + (3 if i % 2 else 1) < count]
    across = [(i, i ^ 1) for i in range(count)]

    def back(pairs):
        return [(there, here) for here, there in pairs]

    lengths = doc_lengths.reshape(1, -1)
    own = packed(keys, values)
    two = moved(own, two_on)
    mixed = moved(own, mixed_on)
    first, starts, top, total, out, qt, dot_ = attention_before(place, lengths, queries, d_out, own)
    swapped = moved(two, across)
    attended, top, inverse, row_dot, dq, two_part, mixed_part, swapped_part = attention_earlier(
        place, first, queries, d_out, qt, dot_, starts, top, total, out, two, mixed, swapped
    )
    d_queries, own_part = attention_own(
        queries, d_out, qt, dot_, own, starts, top, inverse, row_dot, dq
    )
    from_core = moved(swapped_part, across)
    from_mixed = moved(mixed_part, back(mixed_on))
    passed = (two_part.astype(F32) + from_core.astype(F32)).astype(BF)
    from_two = moved(passed, back(two_on))
    mine = (own_part.astype(F32) + from_mixed.astype(F32) + from_two.astype(F32)).astype(BF)
    summed = head_sum(mine)
    return (attended, d_queries, summed[:rows], summed[rows:])


def solution(mesh):
    in_specs = (P("ctx", "head"), P("ctx", None), P("ctx", None), P("ctx", "head"), P())
    out_specs = (P("ctx", "head"), P("ctx", "head"), P("ctx", None), P("ctx", None))
    return jax.shard_map(
        on_device, mesh=mesh, in_specs=in_specs, out_specs=out_specs, check_vma=False
    )
```

```python
import functools
import math

import jax
import jax.numpy as jnp
from jax import lax
from jax.experimental import pallas as pl
from jax.experimental.pallas import tpu as pltpu
from jax.sharding import PartitionSpec as P

SPAN = 3
BF = jnp.bfloat16
F32 = jnp.float32


def dot_nt(a, b):
    return lax.dot_general(a, b, (((1,), (1,)), ((), ())), preferred_element_type=F32)


def dot_nn(a, b):
    return jnp.dot(a, b, preferred_element_type=F32)


def diagonal_kernel(
    place_ref, lengths_ref, q_ref, do_ref, own_ref,
    first_ref, starts_ref, top_ref, total_ref, out_ref, qt_ref, dot_ref,
):
    rows, width = q_ref.shape
    head = own_ref.shape[1]
    heads = width // head
    lead = SPAN * rows
    lengths = lengths_ref[...].astype(F32)
    docs = lengths.shape[1]
    along = jnp.broadcast_to(lengths, (docs, docs))
    earlier = lax.broadcasted_iota(jnp.int32, (docs, docs), 0)
    later = lax.broadcasted_iota(jnp.int32, (docs, docs), 1)
    ends = jnp.sum(jnp.where(earlier <= later, along.T, 0.0), axis=0, keepdims=True)
    begin = (place_ref[0] * rows).astype(F32)
    positions = begin + lax.broadcasted_iota(jnp.int32, (rows, docs), 0).astype(F32)
    doc_start = jnp.sum(jnp.where(ends <= positions, lengths, 0.0), axis=1, keepdims=True)
    start = (doc_start - begin).astype(jnp.int32)
    starts_ref[...] = jnp.broadcast_to(start, starts_ref.shape)
    first_ref[0] = jnp.min(start) + lead

    column = lax.broadcasted_iota(jnp.int32, (rows, rows), 1)
    row = lax.broadcasted_iota(jnp.int32, (rows, rows), 0)
    allowed = (column >= start) & (column <= row)
    keys = own_ref[pl.ds(0, rows), :]
    values = own_ref[pl.ds(rows, rows), :]
    for h in range(heads):
        cols = pl.ds(h * head, head)
        s = jnp.where(allowed, dot_nt(q_ref[:, cols], keys), -jnp.inf)
        m = jnp.max(s, axis=1, keepdims=True)
        e = jnp.exp2((s - m) * exp2_scale(head))
        top_ref[h] = jnp.broadcast_to(m, (rows, head))
        total_ref[h] = jnp.broadcast_to(jnp.sum(e, axis=1, keepdims=True), (rows, head))
        out_ref[h] = dot_nn(e.astype(BF), values)
        qt_ref[h] = q_ref[:, cols].T
        dot_ref[h] = do_ref[:, cols].T


def earlier_kernel(
    place_ref, first_ref, q_ref, do_ref, qt_ref, dot_ref, starts_ref, top0_ref, total0_ref, out0_ref,
    two_ref, mixed_ref, swapped_ref,
    att_ref, top_ref, inverse_ref, row_dot_ref, dq_ref, two_part_ref, mixed_part_ref, swapped_part_ref,
    key_window, value_window, key_parts, value_parts, tiles, lanes,
):
    rows, width = q_ref.shape
    head = two_ref.shape[1]
    heads = width // head
    to_exp2 = exp2_scale(head)
    scale = score_scale(head)
    odd = lax.rem(place_ref[0], 2)
    last = (SPAN - 1) * rows
    mixed_row = pl.multiple_of(jnp.where(odd == 1, last, 0), rows)
    swapped_row = pl.multiple_of(jnp.where(odd == 1, 0, last), rows)
    slots = (
        (two_ref, two_part_ref, last - rows),
        (mixed_ref, mixed_part_ref, mixed_row),
        (swapped_ref, swapped_part_ref, swapped_row),
    )
    low = jnp.minimum(jnp.maximum(first_ref[0], 0) // rows, SPAN)
    column = lax.broadcasted_iota(jnp.int32, (rows, rows), 1)

    def wide(x):
        return jnp.concatenate([x] * (rows // head), axis=1)

    def folded(x, op):
        parts = [x[:, c : c + head] for c in range(0, rows, head)]
        return functools.reduce(op, parts)

    def score_tile(t, carry):
        at = pl.multiple_of(t * rows, rows)
        keys = key_window[pl.ds(at, rows), :]
        allowed = column >= wide(starts_ref[...] + (SPAN * rows - at))
        for h in range(heads):
            s = dot_nt(q_ref[:, pl.ds(h * head, head)], keys)
            s = jnp.where(allowed, s, -jnp.inf)
            tiles[h, t] = s
            lanes[h] = jnp.maximum(lanes[h], folded(s, jnp.maximum))
        return carry

    def out_tile(t, carry):
        at = pl.multiple_of(t * rows, rows)
        values = value_window[pl.ds(at, rows), :]
        for h in range(heads):
            e = jnp.exp2((tiles[h, t] - wide(top_ref[h])) * to_exp2)
            tiles[h, t] = e
            lanes[h] += folded(e, jnp.add)
            dq_ref[h] += dot_nn(e.astype(BF), values)
        return carry

    def grad_tile(t, carry):
        at = pl.multiple_of(t * rows, rows)
        keys = key_window[pl.ds(at, rows), :]
        values = value_window[pl.ds(at, rows), :]
        dv = jnp.zeros((head, rows), F32)
        dk = jnp.zeros((head, rows), F32)
        for h in range(heads):
            dw = dot_nt(do_ref[:, pl.ds(h * head, head)], values)
            w = tiles[h, t] * wide(inverse_ref[h])
            ds = (w * (dw - wide(row_dot_ref[h]))).astype(BF)
            dv = dv + dot_nn(dot_ref[h], w.astype(BF))
            dk = dk + dot_nn(qt_ref[h], ds)
            dq_ref[h] += dot_nn(ds, keys)
        key_parts[pl.ds(at, rows), :] = (dk * scale).T.astype(BF)
        value_parts[pl.ds(at, rows), :] = dv.T.astype(BF)
        return carry

    def zero_tile(t, carry):
        at = pl.multiple_of(t * rows, rows)
        key_parts[pl.ds(at, rows), :] = jnp.zeros((rows, head), BF)
        value_parts[pl.ds(at, rows), :] = jnp.zeros((rows, head), BF)
        return carry

    reaches = low < SPAN

    @pl.when(reaches)
    def _():
        for block, _, at in slots:
            key_window[pl.ds(at, rows), :] = block[pl.ds(0, rows), :]
            value_window[pl.ds(at, rows), :] = block[pl.ds(rows, rows), :]
        lanes[...] = top0_ref[...]
        lax.fori_loop(low, SPAN, score_tile, 0)
        for h in range(heads):
            top = jnp.broadcast_to(jnp.max(lanes[h], axis=1, keepdims=True), (rows, head))
            top_ref[h] = top
            kept = jnp.exp2((top0_ref[h] - top) * to_exp2)
            inverse_ref[h] = total0_ref[h] * kept
            dq_ref[h] = out0_ref[h] * kept
        lanes[...] = jnp.zeros(lanes.shape, F32)
        lax.fori_loop(low, SPAN, out_tile, 0)
        for h in range(heads):
            inverse_ref[h] += jnp.sum(lanes[h], axis=1, keepdims=True)

    @pl.when(jnp.logical_not(reaches))
    def _():
        top_ref[...] = top0_ref[...]
        inverse_ref[...] = total0_ref[...]
        dq_ref[...] = out0_ref[...]

    for h in range(heads):
        cols = pl.ds(h * head, head)
        inverse = 1.0 / inverse_ref[h]
        inverse_ref[h] = inverse
        attended = (dq_ref[h] * inverse).astype(BF)
        att_ref[:, cols] = attended
        row_dot = jnp.sum(do_ref[:, cols].astype(F32) * attended.astype(F32), axis=1, keepdims=True)
        row_dot_ref[h] = jnp.broadcast_to(row_dot, (rows, head))
    dq_ref[...] = jnp.zeros(dq_ref.shape, F32)
    lax.fori_loop(0, low, zero_tile, 0)
    lax.fori_loop(low, SPAN, grad_tile, 0)
    for _, part, at in slots:
        part[pl.ds(0, rows), :] = key_parts[pl.ds(at, rows), :]
        part[pl.ds(rows, rows), :] = value_parts[pl.ds(at, rows), :]


def own_kernel(
    q_ref, do_ref, qt_ref, dot_ref, own_ref, starts_ref, top_ref, inverse_ref, row_dot_ref, earlier_ref,
    attended_ref, dq_ref, part_ref, att_ref,
):
    rows, width = q_ref.shape
    head = own_ref.shape[1]
    heads = width // head
    to_exp2 = exp2_scale(head)
    scale = score_scale(head)
    column = lax.broadcasted_iota(jnp.int32, (rows, rows), 1)
    row = lax.broadcasted_iota(jnp.int32, (rows, rows), 0)

    def wide(x):
        return jnp.concatenate([x] * (rows // head), axis=1)

    allowed = (column >= wide(starts_ref[...])) & (column <= row)
    keys = own_ref[pl.ds(0, rows), :]
    values = own_ref[pl.ds(rows, rows), :]
    dv = jnp.zeros((head, rows), F32)
    dk = jnp.zeros((head, rows), F32)
    att_ref[...] = attended_ref[...]
    for h in range(heads):
        cols = pl.ds(h * head, head)
        s = jnp.where(allowed, dot_nt(q_ref[:, cols], keys), -jnp.inf)
        w = jnp.exp2((s - wide(top_ref[h])) * to_exp2) * wide(inverse_ref[h])
        dw = dot_nt(do_ref[:, cols], values)
        ds = (w * (dw - wide(row_dot_ref[h]))).astype(BF)
        dv = dv + dot_nn(dot_ref[h], w.astype(BF))
        dk = dk + dot_nn(qt_ref[h], ds)
        dq_ref[:, cols] = ((earlier_ref[h] + dot_nn(ds, keys)) * scale).astype(BF)
    part_ref[pl.ds(0, rows), :] = (dk * scale).T.astype(BF)
    part_ref[pl.ds(rows, rows), :] = dv.T.astype(BF)


def score_scale(head):
    return 1.0 / math.sqrt(head)


def exp2_scale(head):
    return score_scale(head) * math.log2(math.e)


VMEM = pl.BlockSpec(memory_space=pltpu.VMEM)
SMEM = pl.BlockSpec(memory_space=pltpu.SMEM)


def shape(dims, dtype):
    return jax.ShapeDtypeStruct(dims, dtype)


def on_core(kernel, name, mflop, outs, ins, scratch=()):
    return pl.pallas_call(
        kernel,
        out_shape=tuple(outs),
        in_specs=[SMEM if x.ndim == 1 else VMEM for x in ins],
        out_specs=tuple(SMEM if len(x.shape) == 1 else VMEM for x in outs),
        scratch_shapes=list(scratch),
        compiler_params=pltpu.CompilerParams(vmem_limit_bytes=40 << 20),
        cost_estimate=pl.CostEstimate(
            flops=mflop * 1_000_000, bytes_accessed=2 << 20, transcendentals=1 << 19
        ),
        name=name,
    )(*ins)


def attention_before(place, lengths, q, do, own):
    rows, width = q.shape
    head = own.shape[1]
    heads = width // head
    state = shape((heads, rows, head), F32)
    turned = shape((heads, head, rows), BF)
    outs = [shape((1,), jnp.int32), shape((rows, head), jnp.int32), state, state, state, turned, turned]
    return on_core(diagonal_kernel, "diagonal", 1200, outs, (place, lengths, q, do, own))


def attention_earlier(place, first, q, do, qt, dot_, starts, top, total, out, two, mixed, swapped):
    rows, width = q.shape
    head = two.shape[1]
    heads = width // head
    state = shape((heads, rows, head), F32)
    part = shape(two.shape, BF)
    span = SPAN * rows
    return on_core(
        earlier_kernel,
        "earlier",
        5000,
        [shape(q.shape, BF), state, state, state, state, part, part, part],
        (place, first, q, do, qt, dot_, starts, top, total, out, two, mixed, swapped),
        [pltpu.VMEM((span, head), BF)] * 4
        + [pltpu.VMEM((heads, SPAN, rows, rows), F32), pltpu.VMEM((heads, rows, head), F32)],
    )


def attention_own(q, do, qt, dot_, own, starts, top, inverse, row_dot, dq, attended):
    outs = [shape(q.shape, BF), shape(own.shape, BF), shape(q.shape, BF)]
    ins = (q, do, qt, dot_, own, starts, top, inverse, row_dot, dq, attended)
    return on_core(own_kernel, "own", 2500, outs, ins)


def pack_kernel(key_ref, value_ref, both_ref, sems):
    rows = key_ref.shape[0]
    copies = [
        pltpu.make_async_copy(key_ref, both_ref.at[pl.ds(0, rows)], sems.at[0]),
        pltpu.make_async_copy(value_ref, both_ref.at[pl.ds(rows, rows)], sems.at[1]),
    ]
    for copy in copies:
        copy.start()
    for copy in copies:
        copy.wait()


def packed(keys, values):
    rows, head = keys.shape
    return pl.pallas_call(
        pack_kernel,
        out_shape=jax.ShapeDtypeStruct((2 * rows, head), BF),
        in_specs=[pl.BlockSpec(memory_space=pl.ANY)] * 2,
        out_specs=pl.BlockSpec(memory_space=pltpu.VMEM),
        scratch_shapes=[pltpu.SemaphoreType.DMA((2,))],
        name="pack",
    )(keys, values)


def head_sum(part):
    heads = lax.axis_size("head")
    pieces = part.reshape(heads, part.shape[0] // heads, part.shape[1])
    theirs = lax.all_to_all(pieces, "head", split_axis=0, concat_axis=0)
    mine = jnp.sum(theirs.astype(F32), axis=0).astype(BF)
    mine = jnp.broadcast_to(mine[None], pieces.shape)
    return lax.all_to_all(mine, "head", split_axis=0, concat_axis=0).reshape(part.shape)


def moved(value, pairs):
    return lax.ppermute(value, "ctx", pairs)


def on_device(queries, keys, values, d_out, doc_lengths):
    count = lax.axis_size("ctx")
    rows = keys.shape[0]
    place = lax.axis_index("ctx").reshape(1).astype(jnp.int32)
    two_on = [(i, i + 2) for i in range(count - 2)]
    mixed_on = [(i, i + (3 if i % 2 else 1)) for i in range(count) if i + (3 if i % 2 else 1) < count]
    across = [(i, i ^ 1) for i in range(count)]

    lengths = doc_lengths.reshape(1, -1)
    own = packed(keys, values)
    two = moved(own, two_on)
    first, starts, top, total, out, qt, dot_ = attention_before(place, lengths, queries, d_out, own)
    own_later, first = lax.optimization_barrier((own, first))
    mixed = moved(own_later, mixed_on)
    swapped = moved(two, across)
    attended, top, inverse, row_dot, dq, two_part, mixed_part, swapped_part = attention_earlier(
        place, first, queries, d_out, qt, dot_, starts, top, total, out, two, mixed, swapped
    )
    from_next = moved(mixed_part, [(i + 1, i) for i in range(count - 1)]).astype(F32)
    from_core = moved(swapped_part, across).astype(F32)
    odd = (place[0] & 1) == 1
    passed = two_part.astype(F32) + from_core + jnp.where(odd, from_next, 0.0)
    from_two = moved(passed.astype(BF), [(there, here) for here, there in two_on]).astype(F32)
    d_queries, own_part, attended = attention_own(
        queries, d_out, qt, dot_, own, starts, top, inverse, row_dot, dq, attended
    )
    mine = own_part.astype(F32) + from_two + jnp.where(odd, 0.0, from_next)
    mine = mine.astype(BF)
    summed = head_sum(mine)
    return (attended, d_queries, summed[:rows], summed[rows:])


def solution(mesh):
    in_specs = (P("ctx", "head"), P("ctx", None), P("ctx", None), P("ctx", "head"), P())
    out_specs = (P("ctx", "head"), P("ctx", "head"), P("ctx", None), P("ctx", None))
    return jax.shard_map(
        on_device, mesh=mesh, in_specs=in_specs, out_specs=out_specs, check_vma=False
    )
```

```python
import functools
import math

import jax
import jax.numpy as jnp
from jax import lax
from jax.experimental import pallas as pl
from jax.experimental.pallas import tpu as pltpu
from jax.sharding import PartitionSpec as P

SPAN = 3
BF = jnp.bfloat16
F32 = jnp.float32


def dot_nt(a, b):
    return lax.dot_general(a, b, (((1,), (1,)), ((), ())), preferred_element_type=F32)


def dot_nn(a, b):
    return jnp.dot(a, b, preferred_element_type=F32)


def wide(x, width):
    return jnp.concatenate([x] * (width // x.shape[1]), axis=1)


def folded(x, width, op):
    return functools.reduce(op, [x[:, c : c + width] for c in range(0, x.shape[1], width)])


def across_lanes(x, op, like):
    return jnp.broadcast_to(op(x, axis=1, keepdims=True), like.shape)


def lowest_block(first_ref, rows):
    return jnp.minimum(jnp.maximum(first_ref[0], 0) // rows, SPAN)


def diagonal_kernel(
    place_ref, lengths_ref, q_ref, do_ref, own_ref,
    first_ref, starts_ref, top_ref, total_ref, out_ref, qt_ref, dot_ref,
):
    rows, width = q_ref.shape
    head = own_ref.shape[1]
    heads = width // head
    lead = SPAN * rows
    lengths = lengths_ref[...].astype(F32)
    docs = lengths.shape[1]
    along = jnp.broadcast_to(lengths, (docs, docs))
    earlier = lax.broadcasted_iota(jnp.int32, (docs, docs), 0)
    later = lax.broadcasted_iota(jnp.int32, (docs, docs), 1)
    ends = jnp.sum(jnp.where(earlier <= later, along.T, 0.0), axis=0, keepdims=True)
    begin = (place_ref[0] * rows).astype(F32)
    positions = begin + lax.broadcasted_iota(jnp.int32, (rows, docs), 0).astype(F32)
    doc_start = jnp.sum(jnp.where(ends <= positions, lengths, 0.0), axis=1, keepdims=True)
    start = (doc_start - begin).astype(jnp.int32)
    starts_ref[...] = jnp.broadcast_to(start, starts_ref.shape)
    first_ref[0] = jnp.min(start) + lead

    column = lax.broadcasted_iota(jnp.int32, (rows, rows), 1)
    row = lax.broadcasted_iota(jnp.int32, (rows, rows), 0)
    allowed = (column >= start) & (column <= row)
    keys = own_ref[pl.ds(0, rows), :]
    values = own_ref[pl.ds(rows, rows), :]
    for h in range(heads):
        cols = pl.ds(h * head, head)
        s = jnp.where(allowed, dot_nt(q_ref[:, cols], keys), -jnp.inf)
        m = jnp.max(s, axis=1, keepdims=True)
        e = jnp.exp2((s - m) * exp2_scale(head))
        top_ref[h] = jnp.broadcast_to(m, (rows, head))
        total_ref[h] = jnp.broadcast_to(jnp.sum(e, axis=1, keepdims=True), (rows, head))
        out_ref[h] = dot_nn(e.astype(BF), values)
        qt_ref[h] = q_ref[:, cols].T
        dot_ref[h] = do_ref[:, cols].T


def second_kernel(
    first_ref, q_ref, starts_ref, top0_ref, total0_ref, out0_ref, block_ref,
    top_ref, total_ref, out_ref, tile_ref,
):
    rows, width = q_ref.shape
    head = block_ref.shape[1]
    heads = width // head
    to_exp2 = exp2_scale(head)
    place = SPAN - 2
    live = lowest_block(first_ref, rows) <= place

    @pl.when(live)
    def _():
        keys = block_ref[pl.ds(0, rows), :]
        values = block_ref[pl.ds(rows, rows), :]
        column = lax.broadcasted_iota(jnp.int32, (rows, rows), 1)
        allowed = column >= wide(starts_ref[...] + (SPAN - place) * rows, rows)
        for h in range(heads):
            s = jnp.where(allowed, dot_nt(q_ref[:, pl.ds(h * head, head)], keys), -jnp.inf)
            top0 = top0_ref[h]
            top = across_lanes(jnp.maximum(folded(s, head, jnp.maximum), top0), jnp.max, top0)
            e = jnp.exp2((s - wide(top, rows)) * to_exp2)
            kept = jnp.exp2((top0 - top) * to_exp2)
            tile_ref[h] = e
            top_ref[h] = top
            total_ref[h] = total0_ref[h] * kept + across_lanes(folded(e, head, jnp.add), jnp.sum, top)
            out_ref[h] = out0_ref[h] * kept + dot_nn(e.astype(BF), values)

    @pl.when(jnp.logical_not(live))
    def _():
        top_ref[...] = top0_ref[...]
        total_ref[...] = total0_ref[...]
        out_ref[...] = out0_ref[...]


def far_kernel(
    place_ref, first_ref, q_ref, do_ref, qt_ref, dot_ref, starts_ref, top0_ref, total0_ref, out0_ref,
    mixed_ref, swapped_ref,
    att_ref, top_ref, inverse_ref, row_dot_ref, second_ref, dq_ref, mixed_part_ref, swapped_part_ref,
    key_window, value_window, key_parts, value_parts, tiles, lanes,
):
    rows, width = q_ref.shape
    head = mixed_ref.shape[1]
    heads = width // head
    to_exp2 = exp2_scale(head)
    scale = score_scale(head)
    odd = lax.rem(place_ref[0], 2)
    mixed_row = pl.multiple_of((1 - odd) * rows, rows)
    swapped_row = pl.multiple_of(odd * rows, rows)
    slots = (
        (mixed_ref, mixed_part_ref, mixed_row),
        (swapped_ref, swapped_part_ref, swapped_row),
    )
    low = lowest_block(first_ref, rows)
    live = (low < SPAN).astype(jnp.int32) + (low < 1).astype(jnp.int32)
    column = lax.broadcasted_iota(jnp.int32, (rows, rows), 1)

    def score_tile(t, carry):
        at = pl.multiple_of(t * rows, rows)
        keys = key_window[pl.ds(at, rows), :]
        allowed = column >= wide(starts_ref[...] + (rows + 2 * at), rows)
        for h in range(heads):
            s = dot_nt(q_ref[:, pl.ds(h * head, head)], keys)
            s = jnp.where(allowed, s, -jnp.inf)
            tiles[h, t] = s
            lanes[h] = jnp.maximum(lanes[h], folded(s, head, jnp.maximum))
        return carry

    def out_tile(t, carry):
        at = pl.multiple_of(t * rows, rows)
        values = value_window[pl.ds(at, rows), :]
        for h in range(heads):
            e = jnp.exp2((tiles[h, t] - wide(top_ref[h], rows)) * to_exp2)
            tiles[h, t] = e
            lanes[h] += folded(e, head, jnp.add)
            dq_ref[h] += dot_nn(e.astype(BF), values)
        return carry

    def grad_tile(t, carry):
        at = pl.multiple_of(t * rows, rows)
        keys = key_window[pl.ds(at, rows), :]
        values = value_window[pl.ds(at, rows), :]
        dv = jnp.zeros((head, rows), F32)
        dk = jnp.zeros((head, rows), F32)
        for h in range(heads):
            dw = dot_nt(do_ref[:, pl.ds(h * head, head)], values)
            w = tiles[h, t] * wide(inverse_ref[h], rows)
            ds = (w * (dw - wide(row_dot_ref[h], rows))).astype(BF)
            dv = dv + dot_nn(dot_ref[h], w.astype(BF))
            dk = dk + dot_nn(qt_ref[h], ds)
            dq_ref[h] += dot_nn(ds, keys)
        key_parts[pl.ds(at, rows), :] = (dk * scale).T.astype(BF)
        value_parts[pl.ds(at, rows), :] = dv.T.astype(BF)
        return carry

    def zero_tile(t, carry):
        at = pl.multiple_of(t * rows, rows)
        key_parts[pl.ds(at, rows), :] = jnp.zeros((rows, head), BF)
        value_parts[pl.ds(at, rows), :] = jnp.zeros((rows, head), BF)
        return carry

    @pl.when(live > 0)
    def _():
        for block, _, at in slots:
            key_window[pl.ds(at, rows), :] = block[pl.ds(0, rows), :]
            value_window[pl.ds(at, rows), :] = block[pl.ds(rows, rows), :]
        lanes[...] = top0_ref[...]
        lax.fori_loop(0, live, score_tile, 0)
        for h in range(heads):
            top = across_lanes(lanes[h], jnp.max, lanes[h])
            top_ref[h] = top
            kept = jnp.exp2((top0_ref[h] - top) * to_exp2)
            second_ref[h] = kept
            inverse_ref[h] = total0_ref[h] * kept
            dq_ref[h] = out0_ref[h] * kept
        lanes[...] = jnp.zeros(lanes.shape, F32)
        lax.fori_loop(0, live, out_tile, 0)
        for h in range(heads):
            inverse_ref[h] += jnp.sum(lanes[h], axis=1, keepdims=True)

    @pl.when(live == 0)
    def _():
        top_ref[...] = top0_ref[...]
        second_ref[...] = jnp.ones(second_ref.shape, F32)
        inverse_ref[...] = total0_ref[...]
        dq_ref[...] = out0_ref[...]

    for h in range(heads):
        cols = pl.ds(h * head, head)
        inverse = 1.0 / inverse_ref[h]
        inverse_ref[h] = inverse
        second_ref[h] = second_ref[h] * inverse
        attended = (dq_ref[h] * inverse).astype(BF)
        att_ref[:, cols] = attended
        row_dot = jnp.sum(do_ref[:, cols].astype(F32) * attended.astype(F32), axis=1, keepdims=True)
        row_dot_ref[h] = jnp.broadcast_to(row_dot, (rows, head))
    dq_ref[...] = jnp.zeros(dq_ref.shape, F32)
    lax.fori_loop(0, live, grad_tile, 0)
    lax.fori_loop(live, 2, zero_tile, 0)
    for _, part, at in slots:
        part[pl.ds(0, rows), :] = key_parts[pl.ds(at, rows), :]
        part[pl.ds(rows, rows), :] = value_parts[pl.ds(at, rows), :]


def second_back_kernel(
    first_ref, do_ref, qt_ref, dot_ref, block_ref, tile_ref, factor_ref, row_dot_ref, far_ref,
    dq_ref, part_ref,
):
    heads, rows, head = far_ref.shape
    scale = score_scale(head)
    live = lowest_block(first_ref, rows) <= SPAN - 2

    @pl.when(live)
    def _():
        keys = block_ref[pl.ds(0, rows), :]
        values = block_ref[pl.ds(rows, rows), :]
        dv = jnp.zeros((head, rows), F32)
        dk = jnp.zeros((head, rows), F32)
        for h in range(heads):
            dw = dot_nt(do_ref[:, pl.ds(h * head, head)], values)
            w = tile_ref[h] * wide(factor_ref[h], rows)
            ds = (w * (dw - wide(row_dot_ref[h], rows))).astype(BF)
            dv = dv + dot_nn(dot_ref[h], w.astype(BF))
            dk = dk + dot_nn(qt_ref[h], ds)
            dq_ref[h] = far_ref[h] + dot_nn(ds, keys)
        part_ref[pl.ds(0, rows), :] = (dk * scale).T.astype(BF)
        part_ref[pl.ds(rows, rows), :] = dv.T.astype(BF)

    @pl.when(jnp.logical_not(live))
    def _():
        dq_ref[...] = far_ref[...]
        part_ref[...] = jnp.zeros(part_ref.shape, BF)


def own_kernel(
    q_ref, do_ref, qt_ref, dot_ref, own_ref, starts_ref, top_ref, inverse_ref, row_dot_ref, earlier_ref,
    attended_ref, dq_ref, part_ref, att_ref,
):
    rows, width = q_ref.shape
    head = own_ref.shape[1]
    heads = width // head
    to_exp2 = exp2_scale(head)
    scale = score_scale(head)
    column = lax.broadcasted_iota(jnp.int32, (rows, rows), 1)
    row = lax.broadcasted_iota(jnp.int32, (rows, rows), 0)
    allowed = (column >= wide(starts_ref[...], rows)) & (column <= row)
    keys = own_ref[pl.ds(0, rows), :]
    values = own_ref[pl.ds(rows, rows), :]
    dv = jnp.zeros((head, rows), F32)
    dk = jnp.zeros((head, rows), F32)
    att_ref[...] = attended_ref[...]
    for h in range(heads):
        cols = pl.ds(h * head, head)
        s = jnp.where(allowed, dot_nt(q_ref[:, cols], keys), -jnp.inf)
        w = jnp.exp2((s - wide(top_ref[h], rows)) * to_exp2) * wide(inverse_ref[h], rows)
        dw = dot_nt(do_ref[:, cols], values)
        ds = (w * (dw - wide(row_dot_ref[h], rows))).astype(BF)
        dv = dv + dot_nn(dot_ref[h], w.astype(BF))
        dk = dk + dot_nn(qt_ref[h], ds)
        dq_ref[:, cols] = ((earlier_ref[h] + dot_nn(ds, keys)) * scale).astype(BF)
    part_ref[pl.ds(0, rows), :] = (dk * scale).T.astype(BF)
    part_ref[pl.ds(rows, rows), :] = dv.T.astype(BF)


def merge_kernel(weight_ref, a_ref, b_ref, c_ref, out_ref):
    weight = weight_ref[0].astype(F32)
    out = a_ref[...].astype(F32) + b_ref[...].astype(F32) + weight * c_ref[...].astype(F32)
    out_ref[...] = out.astype(BF)


def score_scale(head):
    return 1.0 / math.sqrt(head)


def exp2_scale(head):
    return score_scale(head) * math.log2(math.e)


VMEM = pl.BlockSpec(memory_space=pltpu.VMEM)
SMEM = pl.BlockSpec(memory_space=pltpu.SMEM)


def shape(dims, dtype):
    return jax.ShapeDtypeStruct(dims, dtype)


def on_core(kernel, name, mflop, mib, outs, ins, scratch=(), aliases={}):
    return pl.pallas_call(
        kernel,
        out_shape=tuple(outs),
        in_specs=[SMEM if x.ndim == 1 else VMEM for x in ins],
        out_specs=tuple(SMEM if len(x.shape) == 1 else VMEM for x in outs),
        scratch_shapes=list(scratch),
        input_output_aliases=aliases,
        compiler_params=pltpu.CompilerParams(vmem_limit_bytes=mib << 20),
        cost_estimate=pl.CostEstimate(
            flops=mflop * 1_000_000, bytes_accessed=2 << 20, transcendentals=1 << 19
        ),
        name=name,
    )(*ins)


def sizes(q, own):
    rows, width = q.shape
    head = own.shape[1]
    heads = width // head
    state = shape((heads, rows, head), F32)
    turned = shape((heads, head, rows), BF)
    tile = shape((heads, rows, rows), F32)
    return state, turned, tile, shape(q.shape, BF), shape(own.shape, BF)


def attention_before(place, lengths, q, do, own):
    state, turned, _, _, _ = sizes(q, own)
    starts = shape(state.shape[1:], jnp.int32)
    outs = [shape((1,), jnp.int32), starts, state, state, state, turned, turned]
    return on_core(diagonal_kernel, "diagonal", 1200, 20, outs, (place, lengths, q, do, own))


def attention_second(first, q, starts, top, total, out, two):
    state, _, tile, _, _ = sizes(q, two)
    ins = (first, q, starts, top, total, out, two)
    return on_core(second_kernel, "second", 1200, 20, [state, state, state, tile], ins)


def attention_far(place, first, q, do, qt, dot_, starts, top, total, out, mixed, swapped):
    state, _, tile, like_q, part = sizes(q, mixed)
    rows, head = state.shape[1:]
    return on_core(
        far_kernel,
        "far",
        3000,
        24,
        [like_q] + [state] * 5 + [part] * 2,
        (place, first, q, do, qt, dot_, starts, top, total, out, mixed, swapped),
        [pltpu.VMEM((2 * rows, head), BF)] * 4
        + [pltpu.VMEM((state.shape[0], 2, rows, rows), F32), pltpu.VMEM(state.shape, F32)],
    )


def attention_second_back(first, q, do, qt, dot_, two, tile, factor, row_dot, dq):
    state, _, _, _, part = sizes(q, two)
    ins = (first, do, qt, dot_, two, tile, factor, row_dot, dq)
    return on_core(second_back_kernel, "second_back", 1500, 20, [state, part], ins)


def attention_own(q, do, qt, dot_, own, starts, top, inverse, row_dot, dq, attended):
    _, _, _, like_q, part = sizes(q, own)
    ins = (q, do, qt, dot_, own, starts, top, inverse, row_dot, dq, attended)
    return on_core(own_kernel, "own", 2500, 20, [like_q, part, like_q], ins)


def merged(weight, a, b, c):
    return on_core(merge_kernel, "merge", 1, 6, [shape(a.shape, BF)], (weight, a, b, c))[0]


def pack_kernel(key_ref, value_ref, both_ref, sems):
    rows = key_ref.shape[0]
    copies = [
        pltpu.make_async_copy(key_ref, both_ref.at[pl.ds(0, rows)], sems.at[0]),
        pltpu.make_async_copy(value_ref, both_ref.at[pl.ds(rows, rows)], sems.at[1]),
    ]
    for copy in copies:
        copy.start()
    for copy in copies:
        copy.wait()


def packed(keys, values):
    rows, head = keys.shape
    return pl.pallas_call(
        pack_kernel,
        out_shape=jax.ShapeDtypeStruct((2 * rows, head), BF),
        in_specs=[pl.BlockSpec(memory_space=pl.ANY)] * 2,
        out_specs=pl.BlockSpec(memory_space=pl.ANY),
        scratch_shapes=[pltpu.SemaphoreType.DMA((2,))],
        name="pack",
    )(keys, values)


def head_sum(part):
    heads = lax.axis_size("head")
    pieces = part.reshape(heads, part.shape[0] // heads, part.shape[1])
    theirs = lax.all_to_all(pieces, "head", split_axis=0, concat_axis=0)
    mine = jnp.sum(theirs.astype(F32), axis=0).astype(BF)
    mine = jnp.broadcast_to(mine[None], pieces.shape)
    return lax.all_to_all(mine, "head", split_axis=0, concat_axis=0).reshape(part.shape)


def moved(value, pairs):
    return lax.ppermute(value, "ctx", pairs)


def on_device(queries, keys, values, d_out, doc_lengths):
    count = lax.axis_size("ctx")
    rows = keys.shape[0]
    place = lax.axis_index("ctx").reshape(1).astype(jnp.int32)
    two_on = [(i, i + 2) for i in range(count - 2)]
    mixed_on = [(i, i + (3 if i % 2 else 1)) for i in range(count) if i + (3 if i % 2 else 1) < count]
    across = [(i, i ^ 1) for i in range(count)]

    lengths = doc_lengths.reshape(1, -1)
    own = packed(keys, values)
    two = moved(own, two_on)
    first, starts, top, total, out, qt, dot_ = attention_before(place, lengths, queries, d_out, own)
    own_later, first = lax.optimization_barrier((own, first))
    mixed = moved(own_later, mixed_on)
    swapped = moved(two, across)
    top, total, out, tile = attention_second(first, queries, starts, top, total, out, two)
    attended, top, inverse, row_dot, factor, dq, mixed_part, swapped_part = attention_far(
        place, first, queries, d_out, qt, dot_, starts, top, total, out, mixed, swapped
    )
    from_next = moved(mixed_part, [(i + 1, i) for i in range(count - 1)])
    from_core = moved(swapped_part, across)
    dq, two_part = attention_second_back(
        first, queries, d_out, qt, dot_, two, tile, factor, row_dot, dq
    )
    odd = place & 1
    passed = merged(odd, two_part, from_core, from_next)
    from_two = moved(passed, [(there, here) for here, there in two_on])
    d_queries, own_part, attended = attention_own(
        queries, d_out, qt, dot_, own, starts, top, inverse, row_dot, dq, attended
    )
    mine = merged(1 - odd, own_part, from_two, from_next)
    summed = head_sum(mine)
    return (attended, d_queries, summed[:rows], summed[rows:])


def solution(mesh):
    in_specs = (P("ctx", "head"), P("ctx", None), P("ctx", None), P("ctx", "head"), P())
    out_specs = (P("ctx", "head"), P("ctx", "head"), P("ctx", None), P("ctx", None))
    return jax.shard_map(
        on_device, mesh=mesh, in_specs=in_specs, out_specs=out_specs, check_vma=False
    )
```

```python
import functools
import math

import jax
import jax.numpy as jnp
from jax import lax
from jax.experimental import pallas as pl
from jax.experimental.pallas import tpu as pltpu
from jax.sharding import PartitionSpec as P

SPAN = 3
BF = jnp.bfloat16
F32 = jnp.float32


def dot_nt(a, b):
    return lax.dot_general(a, b, (((1,), (1,)), ((), ())), preferred_element_type=F32)


def dot_nn(a, b):
    return jnp.dot(a, b, preferred_element_type=F32)


def wide(x, width):
    return jnp.concatenate([x] * (width // x.shape[1]), axis=1)


def folded(x, width, op):
    return functools.reduce(op, [x[:, c : c + width] for c in range(0, x.shape[1], width)])


def across_lanes(x, op, like):
    return jnp.broadcast_to(op(x, axis=1, keepdims=True), like.shape)


def lowest_block(first_ref, rows):
    return jnp.minimum(jnp.maximum(first_ref[0], 0) // rows, SPAN)


def diagonal_kernel(
    place_ref, lengths_ref, q_ref, do_ref, own_ref,
    first_ref, starts_ref, top_ref, total_ref, out_ref, qt_ref, dot_ref,
):
    rows, width = q_ref.shape
    head = own_ref.shape[1]
    heads = width // head
    lead = SPAN * rows
    lengths = lengths_ref[...].astype(F32)
    docs = lengths.shape[1]
    along = jnp.broadcast_to(lengths, (docs, docs))
    earlier = lax.broadcasted_iota(jnp.int32, (docs, docs), 0)
    later = lax.broadcasted_iota(jnp.int32, (docs, docs), 1)
    ends = jnp.sum(jnp.where(earlier <= later, along.T, 0.0), axis=0, keepdims=True)
    begin = (place_ref[0] * rows).astype(F32)
    positions = begin + lax.broadcasted_iota(jnp.int32, (rows, docs), 0).astype(F32)
    doc_start = jnp.sum(jnp.where(ends <= positions, lengths, 0.0), axis=1, keepdims=True)
    start = (doc_start - begin).astype(jnp.int32)
    starts_ref[...] = jnp.broadcast_to(start, starts_ref.shape)
    first_ref[0] = jnp.min(start) + lead

    column = lax.broadcasted_iota(jnp.int32, (rows, rows), 1)
    row = lax.broadcasted_iota(jnp.int32, (rows, rows), 0)
    allowed = (column >= start) & (column <= row)
    keys = own_ref[pl.ds(0, rows), :]
    values = own_ref[pl.ds(rows, rows), :]
    for h in range(heads):
        cols = pl.ds(h * head, head)
        s = jnp.where(allowed, dot_nt(q_ref[:, cols], keys), -jnp.inf)
        m = jnp.max(s, axis=1, keepdims=True)
        e = jnp.exp2((s - m) * exp2_scale(head))
        top_ref[h] = jnp.broadcast_to(m, (rows, head))
        total_ref[h] = jnp.broadcast_to(jnp.sum(e, axis=1, keepdims=True), (rows, head))
        out_ref[h] = dot_nn(e.astype(BF), values)
        qt_ref[h] = q_ref[:, cols].T
        dot_ref[h] = do_ref[:, cols].T


def second_kernel(
    first_ref, q_ref, starts_ref, top0_ref, total0_ref, out0_ref, block_ref,
    top_ref, total_ref, out_ref, tile_ref,
):
    rows, width = q_ref.shape
    head = block_ref.shape[1]
    heads = width // head
    to_exp2 = exp2_scale(head)
    place = SPAN - 2
    live = lowest_block(first_ref, rows) <= place

    @pl.when(live)
    def _():
        keys = block_ref[pl.ds(0, rows), :]
        values = block_ref[pl.ds(rows, rows), :]
        column = lax.broadcasted_iota(jnp.int32, (rows, rows), 1)
        allowed = column >= wide(starts_ref[...] + (SPAN - place) * rows, rows)
        for h in range(heads):
            s = jnp.where(allowed, dot_nt(q_ref[:, pl.ds(h * head, head)], keys), -jnp.inf)
            top0 = top0_ref[h]
            top = across_lanes(jnp.maximum(folded(s, head, jnp.maximum), top0), jnp.max, top0)
            e = jnp.exp2((s - wide(top, rows)) * to_exp2)
            kept = jnp.exp2((top0 - top) * to_exp2)
            tile_ref[h] = e
            top_ref[h] = top
            total_ref[h] = total0_ref[h] * kept + across_lanes(folded(e, head, jnp.add), jnp.sum, top)
            out_ref[h] = out0_ref[h] * kept + dot_nn(e.astype(BF), values)

    @pl.when(jnp.logical_not(live))
    def _():
        top_ref[...] = top0_ref[...]
        total_ref[...] = total0_ref[...]
        out_ref[...] = out0_ref[...]


def far_kernel(
    place_ref, first_ref, q_ref, do_ref, qt_ref, dot_ref, starts_ref, top0_ref, total0_ref, out0_ref,
    mixed_ref, swapped_ref,
    att_ref, top_ref, inverse_ref, row_dot_ref, second_ref, dq_ref, mixed_part_ref, swapped_part_ref,
    key_window, value_window, key_parts, value_parts, tiles, lanes,
):
    rows, width = q_ref.shape
    head = mixed_ref.shape[1]
    heads = width // head
    to_exp2 = exp2_scale(head)
    scale = score_scale(head)
    odd = lax.rem(place_ref[0], 2)
    mixed_row = pl.multiple_of((1 - odd) * rows, rows)
    swapped_row = pl.multiple_of(odd * rows, rows)
    slots = (
        (mixed_ref, mixed_part_ref, mixed_row),
        (swapped_ref, swapped_part_ref, swapped_row),
    )
    low = lowest_block(first_ref, rows)
    live = (low < SPAN).astype(jnp.int32) + (low < 1).astype(jnp.int32)
    column = lax.broadcasted_iota(jnp.int32, (rows, rows), 1)

    def score_tile(t, carry):
        at = pl.multiple_of(t * rows, rows)
        keys = key_window[pl.ds(at, rows), :]
        allowed = column >= wide(starts_ref[...] + (rows + 2 * at), rows)
        for h in range(heads):
            s = dot_nt(q_ref[:, pl.ds(h * head, head)], keys)
            s = jnp.where(allowed, s, -jnp.inf)
            tiles[h, t] = s
            lanes[h] = jnp.maximum(lanes[h], folded(s, head, jnp.maximum))
        return carry

    def out_tile(t, carry):
        at = pl.multiple_of(t * rows, rows)
        values = value_window[pl.ds(at, rows), :]
        for h in range(heads):
            e = jnp.exp2((tiles[h, t] - wide(top_ref[h], rows)) * to_exp2)
            tiles[h, t] = e
            lanes[h] += folded(e, head, jnp.add)
            dq_ref[h] += dot_nn(e.astype(BF), values)
        return carry

    def grad_tile(t, carry):
        at = pl.multiple_of(t * rows, rows)
        keys = key_window[pl.ds(at, rows), :]
        values = value_window[pl.ds(at, rows), :]
        dv = jnp.zeros((head, rows), F32)
        dk = jnp.zeros((head, rows), F32)
        for h in range(heads):
            dw = dot_nt(do_ref[:, pl.ds(h * head, head)], values)
            w = tiles[h, t] * wide(inverse_ref[h], rows)
            ds = (w * (dw - wide(row_dot_ref[h], rows))).astype(BF)
            dv = dv + dot_nn(dot_ref[h], w.astype(BF))
            dk = dk + dot_nn(qt_ref[h], ds)
            dq_ref[h] += dot_nn(ds, keys)
        key_parts[pl.ds(at, rows), :] = (dk * scale).T.astype(BF)
        value_parts[pl.ds(at, rows), :] = dv.T.astype(BF)
        return carry

    def zero_tile(t, carry):
        at = pl.multiple_of(t * rows, rows)
        key_parts[pl.ds(at, rows), :] = jnp.zeros((rows, head), BF)
        value_parts[pl.ds(at, rows), :] = jnp.zeros((rows, head), BF)
        return carry

    @pl.when(live > 0)
    def _():
        for block, _, at in slots:
            key_window[pl.ds(at, rows), :] = block[pl.ds(0, rows), :]
            value_window[pl.ds(at, rows), :] = block[pl.ds(rows, rows), :]
        lanes[...] = top0_ref[...]
        lax.fori_loop(0, live, score_tile, 0)
        for h in range(heads):
            top = across_lanes(lanes[h], jnp.max, lanes[h])
            top_ref[h] = top
            kept = jnp.exp2((top0_ref[h] - top) * to_exp2)
            second_ref[h] = kept
            inverse_ref[h] = total0_ref[h] * kept
            dq_ref[h] = out0_ref[h] * kept
        lanes[...] = jnp.zeros(lanes.shape, F32)
        lax.fori_loop(0, live, out_tile, 0)
        for h in range(heads):
            inverse_ref[h] += jnp.sum(lanes[h], axis=1, keepdims=True)

    @pl.when(live == 0)
    def _():
        top_ref[...] = top0_ref[...]
        second_ref[...] = jnp.ones(second_ref.shape, F32)
        inverse_ref[...] = total0_ref[...]
        dq_ref[...] = out0_ref[...]

    for h in range(heads):
        cols = pl.ds(h * head, head)
        inverse = 1.0 / inverse_ref[h]
        inverse_ref[h] = inverse
        second_ref[h] = second_ref[h] * inverse
        attended = (dq_ref[h] * inverse).astype(BF)
        att_ref[:, cols] = attended
        row_dot = jnp.sum(do_ref[:, cols].astype(F32) * attended.astype(F32), axis=1, keepdims=True)
        row_dot_ref[h] = jnp.broadcast_to(row_dot, (rows, head))
    dq_ref[...] = jnp.zeros(dq_ref.shape, F32)
    lax.fori_loop(0, live, grad_tile, 0)
    lax.fori_loop(live, 2, zero_tile, 0)
    for _, part, at in slots:
        part[pl.ds(0, rows), :] = key_parts[pl.ds(at, rows), :]
        part[pl.ds(rows, rows), :] = value_parts[pl.ds(at, rows), :]


def second_back_kernel(
    first_ref, do_ref, qt_ref, dot_ref, block_ref, tile_ref, factor_ref, row_dot_ref, far_ref,
    dq_ref, part_ref,
):
    heads, rows, head = far_ref.shape
    scale = score_scale(head)
    live = lowest_block(first_ref, rows) <= SPAN - 2

    @pl.when(live)
    def _():
        keys = block_ref[pl.ds(0, rows), :]
        values = block_ref[pl.ds(rows, rows), :]
        dv = jnp.zeros((head, rows), F32)
        dk = jnp.zeros((head, rows), F32)
        for h in range(heads):
            dw = dot_nt(do_ref[:, pl.ds(h * head, head)], values)
            w = tile_ref[h] * wide(factor_ref[h], rows)
            ds = (w * (dw - wide(row_dot_ref[h], rows))).astype(BF)
            dv = dv + dot_nn(dot_ref[h], w.astype(BF))
            dk = dk + dot_nn(qt_ref[h], ds)
            dq_ref[h] = far_ref[h] + dot_nn(ds, keys)
        part_ref[pl.ds(0, rows), :] = (dk * scale).T.astype(BF)
        part_ref[pl.ds(rows, rows), :] = dv.T.astype(BF)

    @pl.when(jnp.logical_not(live))
    def _():
        dq_ref[...] = far_ref[...]
        part_ref[...] = jnp.zeros(part_ref.shape, BF)


def own_kernel(
    q_ref, do_ref, qt_ref, dot_ref, own_ref, starts_ref, top_ref, inverse_ref, row_dot_ref, earlier_ref,
    attended_ref, dq_ref, part_ref, att_ref,
):
    rows, width = q_ref.shape
    head = own_ref.shape[1]
    heads = width // head
    to_exp2 = exp2_scale(head)
    scale = score_scale(head)
    column = lax.broadcasted_iota(jnp.int32, (rows, rows), 1)
    row = lax.broadcasted_iota(jnp.int32, (rows, rows), 0)
    allowed = (column >= wide(starts_ref[...], rows)) & (column <= row)
    keys = own_ref[pl.ds(0, rows), :]
    values = own_ref[pl.ds(rows, rows), :]
    dv = jnp.zeros((head, rows), F32)
    dk = jnp.zeros((head, rows), F32)
    att_ref[...] = attended_ref[...]
    for h in range(heads):
        cols = pl.ds(h * head, head)
        s = jnp.where(allowed, dot_nt(q_ref[:, cols], keys), -jnp.inf)
        w = jnp.exp2((s - wide(top_ref[h], rows)) * to_exp2) * wide(inverse_ref[h], rows)
        dw = dot_nt(do_ref[:, cols], values)
        ds = (w * (dw - wide(row_dot_ref[h], rows))).astype(BF)
        dv = dv + dot_nn(dot_ref[h], w.astype(BF))
        dk = dk + dot_nn(qt_ref[h], ds)
        dq_ref[:, cols] = ((earlier_ref[h] + dot_nn(ds, keys)) * scale).astype(BF)
    part_ref[pl.ds(0, rows), :] = (dk * scale).T.astype(BF)
    part_ref[pl.ds(rows, rows), :] = dv.T.astype(BF)


def merge_kernel(weight_ref, a_ref, b_ref, c_ref, out_ref):
    weight = weight_ref[0].astype(F32)
    out = a_ref[...].astype(F32) + b_ref[...].astype(F32) + weight * c_ref[...].astype(F32)
    out_ref[...] = out.astype(BF)


def score_scale(head):
    return 1.0 / math.sqrt(head)


def exp2_scale(head):
    return score_scale(head) * math.log2(math.e)


VMEM = pl.BlockSpec(memory_space=pltpu.VMEM)
SMEM = pl.BlockSpec(memory_space=pltpu.SMEM)


def shape(dims, dtype):
    return jax.ShapeDtypeStruct(dims, dtype)


def on_core(kernel, name, mflop, mib, outs, ins, scratch=(), aliases={}):
    return pl.pallas_call(
        kernel,
        out_shape=tuple(outs),
        in_specs=[SMEM if x.ndim == 1 else VMEM for x in ins],
        out_specs=tuple(SMEM if len(x.shape) == 1 else VMEM for x in outs),
        scratch_shapes=list(scratch),
        input_output_aliases=aliases,
        compiler_params=pltpu.CompilerParams(vmem_limit_bytes=mib << 20),
        cost_estimate=pl.CostEstimate(
            flops=mflop * 1_000_000, bytes_accessed=2 << 20, transcendentals=1 << 19
        ),
        name=name,
    )(*ins)


def sizes(q, own):
    rows, width = q.shape
    head = own.shape[1]
    heads = width // head
    state = shape((heads, rows, head), F32)
    turned = shape((heads, head, rows), BF)
    tile = shape((heads, rows, rows), F32)
    return state, turned, tile, shape(q.shape, BF), shape(own.shape, BF)


def attention_before(place, lengths, q, do, own):
    state, turned, _, _, _ = sizes(q, own)
    starts = shape(state.shape[1:], jnp.int32)
    outs = [shape((1,), jnp.int32), starts, state, state, state, turned, turned]
    return on_core(diagonal_kernel, "diagonal", 1200, 20, outs, (place, lengths, q, do, own))


def attention_second(first, q, starts, top, total, out, two):
    state, _, tile, _, _ = sizes(q, two)
    ins = (first, q, starts, top, total, out, two)
    return on_core(second_kernel, "second", 1200, 20, [state, state, state, tile], ins)


def attention_far(place, first, q, do, qt, dot_, starts, top, total, out, mixed, swapped):
    state, _, tile, like_q, part = sizes(q, mixed)
    rows, head = state.shape[1:]
    return on_core(
        far_kernel,
        "far",
        3000,
        24,
        [like_q] + [state] * 5 + [part] * 2,
        (place, first, q, do, qt, dot_, starts, top, total, out, mixed, swapped),
        [pltpu.VMEM((2 * rows, head), BF)] * 4
        + [pltpu.VMEM((state.shape[0], 2, rows, rows), F32), pltpu.VMEM(state.shape, F32)],
    )


def attention_second_back(first, q, do, qt, dot_, two, tile, factor, row_dot, dq):
    state, _, _, _, part = sizes(q, two)
    ins = (first, do, qt, dot_, two, tile, factor, row_dot, dq)
    return on_core(second_back_kernel, "second_back", 1500, 20, [state, part], ins)


def attention_own(q, do, qt, dot_, own, starts, top, inverse, row_dot, dq, attended):
    _, _, _, like_q, part = sizes(q, own)
    ins = (q, do, qt, dot_, own, starts, top, inverse, row_dot, dq, attended)
    return on_core(own_kernel, "own", 2500, 20, [like_q, part, like_q], ins)


def merged(weight, a, b, c):
    return on_core(merge_kernel, "merge", 1, 6, [shape(a.shape, BF)], (weight, a, b, c))[0]


def pack_kernel(key_ref, value_ref, both_ref, sems):
    rows = key_ref.shape[0]
    copies = [
        pltpu.make_async_copy(key_ref, both_ref.at[pl.ds(0, rows)], sems.at[0]),
        pltpu.make_async_copy(value_ref, both_ref.at[pl.ds(rows, rows)], sems.at[1]),
    ]
    for copy in copies:
        copy.start()
    for copy in copies:
        copy.wait()


def packed(keys, values):
    rows, head = keys.shape
    return pl.pallas_call(
        pack_kernel,
        out_shape=jax.ShapeDtypeStruct((2 * rows, head), BF),
        in_specs=[pl.BlockSpec(memory_space=pl.ANY)] * 2,
        out_specs=VMEM,
        scratch_shapes=[pltpu.SemaphoreType.DMA((2,))],
        compiler_params=pltpu.CompilerParams(vmem_limit_bytes=2 << 20),
        name="pack",
    )(keys, values)


def head_sum(part):
    heads = lax.axis_size("head")
    pieces = part.reshape(heads, part.shape[0] // heads, part.shape[1])
    theirs = lax.all_to_all(pieces, "head", split_axis=0, concat_axis=0)
    mine = jnp.sum(theirs.astype(F32), axis=0).astype(BF)
    mine = jnp.broadcast_to(mine[None], pieces.shape)
    return lax.all_to_all(mine, "head", split_axis=0, concat_axis=0).reshape(part.shape)


def moved(value, pairs):
    return lax.ppermute(value, "ctx", pairs)


def on_device(queries, keys, values, d_out, doc_lengths):
    count = lax.axis_size("ctx")
    rows = keys.shape[0]
    place = lax.axis_index("ctx").reshape(1).astype(jnp.int32)
    two_on = [(i, i + 2) for i in range(count - 2)]
    mixed_on = [(i, i + (3 if i % 2 else 1)) for i in range(count) if i + (3 if i % 2 else 1) < count]
    across = [(i, i ^ 1) for i in range(count)]

    lengths = doc_lengths.reshape(1, -1)
    own = packed(keys, values)
    two = moved(own, two_on)
    first, starts, top, total, out, qt, dot_ = attention_before(place, lengths, queries, d_out, own)
    own_later, first = lax.optimization_barrier((own, first))
    mixed = moved(own_later, mixed_on)
    swapped = moved(two, across)
    top, total, out, tile = attention_second(first, queries, starts, top, total, out, two)
    attended, top, inverse, row_dot, factor, dq, mixed_part, swapped_part = attention_far(
        place, first, queries, d_out, qt, dot_, starts, top, total, out, mixed, swapped
    )
    from_next = moved(mixed_part, [(i + 1, i) for i in range(count - 1)])
    from_core = moved(swapped_part, across)
    dq, two_part = attention_second_back(
        first, queries, d_out, qt, dot_, two, tile, factor, row_dot, dq
    )
    odd = place & 1
    passed = merged(odd, two_part, from_core, from_next)
    from_two = moved(passed, [(there, here) for here, there in two_on])
    d_queries, own_part, attended = attention_own(
        queries, d_out, qt, dot_, own, starts, top, inverse, row_dot, dq, attended
    )
    mine = merged(1 - odd, own_part, from_two, from_next)
    summed = head_sum(mine)
    return (attended, d_queries, summed[:rows], summed[rows:])


def solution(mesh):
    in_specs = (P("ctx", "head"), P("ctx", None), P("ctx", None), P("ctx", "head"), P())
    out_specs = (P("ctx", "head"), P("ctx", "head"), P("ctx", None), P("ctx", None))
    return jax.shard_map(
        on_device, mesh=mesh, in_specs=in_specs, out_specs=out_specs, check_vma=False
    )
```

```python
import functools
import math

import jax
import jax.numpy as jnp
from jax import lax
from jax.experimental import pallas as pl
from jax.experimental.pallas import tpu as pltpu
from jax.sharding import PartitionSpec as P

SPAN = 3
BF = jnp.bfloat16
F32 = jnp.float32


def dot_nt(a, b):
    return lax.dot_general(a, b, (((1,), (1,)), ((), ())), preferred_element_type=F32)


def dot_nn(a, b):
    return jnp.dot(a, b, preferred_element_type=F32)


def wide(x, width):
    return jnp.concatenate([x] * (width // x.shape[1]), axis=1)


def folded(x, width, op):
    return functools.reduce(op, [x[:, c : c + width] for c in range(0, x.shape[1], width)])


def across_lanes(x, op, like):
    return jnp.broadcast_to(op(x, axis=1, keepdims=True), like.shape)


def lowest_block(first_ref, rows):
    return jnp.minimum(jnp.maximum(first_ref[0], 0) // rows, SPAN)


def diagonal_kernel(
    place_ref, lengths_ref, q_ref, do_ref, own_ref,
    first_ref, starts_ref, top_ref, total_ref, out_ref, qt_ref, dot_ref,
):
    rows, width = q_ref.shape
    head = own_ref.shape[1]
    heads = width // head
    lead = SPAN * rows
    lengths = lengths_ref[...].astype(F32)
    docs = lengths.shape[1]
    along = jnp.broadcast_to(lengths, (docs, docs))
    earlier = lax.broadcasted_iota(jnp.int32, (docs, docs), 0)
    later = lax.broadcasted_iota(jnp.int32, (docs, docs), 1)
    ends = jnp.sum(jnp.where(earlier <= later, along.T, 0.0), axis=0, keepdims=True)
    begin = (place_ref[0] * rows).astype(F32)
    positions = begin + lax.broadcasted_iota(jnp.int32, (rows, docs), 0).astype(F32)
    doc_start = jnp.sum(jnp.where(ends <= positions, lengths, 0.0), axis=1, keepdims=True)
    start = (doc_start - begin).astype(jnp.int32)
    starts_ref[...] = jnp.broadcast_to(start, starts_ref.shape)
    first_ref[0] = jnp.min(start) + lead

    column = lax.broadcasted_iota(jnp.int32, (rows, rows), 1)
    row = lax.broadcasted_iota(jnp.int32, (rows, rows), 0)
    allowed = (column >= start) & (column <= row)
    keys = own_ref[pl.ds(0, rows), :]
    values = own_ref[pl.ds(rows, rows), :]
    for h in range(heads):
        cols = pl.ds(h * head, head)
        s = jnp.where(allowed, dot_nt(q_ref[:, cols], keys), -jnp.inf)
        m = jnp.max(s, axis=1, keepdims=True)
        e = jnp.exp2((s - m) * exp2_scale(head))
        top_ref[h] = jnp.broadcast_to(m, (rows, head))
        total_ref[h] = jnp.broadcast_to(jnp.sum(e, axis=1, keepdims=True), (rows, head))
        out_ref[h] = dot_nn(e.astype(BF), values)
        qt_ref[h] = q_ref[:, cols].T
        dot_ref[h] = do_ref[:, cols].T


def second_kernel(
    first_ref, q_ref, starts_ref, top0_ref, total0_ref, out0_ref, block_ref,
    top_ref, total_ref, out_ref, tile_ref,
):
    rows, width = q_ref.shape
    head = block_ref.shape[1]
    heads = width // head
    to_exp2 = exp2_scale(head)
    place = SPAN - 2
    live = lowest_block(first_ref, rows) <= place

    @pl.when(live)
    def _():
        keys = block_ref[pl.ds(0, rows), :]
        values = block_ref[pl.ds(rows, rows), :]
        column = lax.broadcasted_iota(jnp.int32, (rows, rows), 1)
        allowed = column >= wide(starts_ref[...] + (SPAN - place) * rows, rows)
        for h in range(heads):
            s = jnp.where(allowed, dot_nt(q_ref[:, pl.ds(h * head, head)], keys), -jnp.inf)
            top0 = top0_ref[h]
            top = across_lanes(jnp.maximum(folded(s, head, jnp.maximum), top0), jnp.max, top0)
            e = jnp.exp2((s - wide(top, rows)) * to_exp2)
            kept = jnp.exp2((top0 - top) * to_exp2)
            tile_ref[h] = e
            top_ref[h] = top
            total_ref[h] = total0_ref[h] * kept + across_lanes(folded(e, head, jnp.add), jnp.sum, top)
            out_ref[h] = out0_ref[h] * kept + dot_nn(e.astype(BF), values)

    @pl.when(jnp.logical_not(live))
    def _():
        top_ref[...] = top0_ref[...]
        total_ref[...] = total0_ref[...]
        out_ref[...] = out0_ref[...]


def far_kernel(
    place_ref, first_ref, q_ref, do_ref, qt_ref, dot_ref, starts_ref, top0_ref, total0_ref, out0_ref,
    mixed_ref, swapped_ref,
    att_ref, top_ref, inverse_ref, row_dot_ref, second_ref, dq_ref, mixed_part_ref, swapped_part_ref,
    key_window, value_window, key_parts, value_parts, tiles, lanes,
):
    rows, width = q_ref.shape
    head = mixed_ref.shape[1]
    heads = width // head
    to_exp2 = exp2_scale(head)
    scale = score_scale(head)
    odd = lax.rem(place_ref[0], 2)
    mixed_row = pl.multiple_of((1 - odd) * rows, rows)
    swapped_row = pl.multiple_of(odd * rows, rows)
    slots = (
        (mixed_ref, mixed_part_ref, mixed_row),
        (swapped_ref, swapped_part_ref, swapped_row),
    )
    low = lowest_block(first_ref, rows)
    live = (low < SPAN).astype(jnp.int32) + (low < 1).astype(jnp.int32)
    column = lax.broadcasted_iota(jnp.int32, (rows, rows), 1)

    def score_tile(t, carry):
        at = pl.multiple_of(t * rows, rows)
        keys = key_window[pl.ds(at, rows), :]
        allowed = column >= wide(starts_ref[...] + (rows + 2 * at), rows)
        for h in range(heads):
            s = dot_nt(q_ref[:, pl.ds(h * head, head)], keys)
            s = jnp.where(allowed, s, -jnp.inf)
            tiles[h, t] = s
            lanes[h] = jnp.maximum(lanes[h], folded(s, head, jnp.maximum))
        return carry

    def out_tile(t, carry):
        at = pl.multiple_of(t * rows, rows)
        values = value_window[pl.ds(at, rows), :]
        for h in range(heads):
            e = jnp.exp2((tiles[h, t] - wide(top_ref[h], rows)) * to_exp2)
            tiles[h, t] = e
            lanes[h] += folded(e, head, jnp.add)
            dq_ref[h] += dot_nn(e.astype(BF), values)
        return carry

    def grad_tile(t, carry):
        at = pl.multiple_of(t * rows, rows)
        keys = key_window[pl.ds(at, rows), :]
        values = value_window[pl.ds(at, rows), :]
        dv = jnp.zeros((head, rows), F32)
        dk = jnp.zeros((head, rows), F32)
        for h in range(heads):
            dw = dot_nt(do_ref[:, pl.ds(h * head, head)], values)
            w = tiles[h, t] * wide(inverse_ref[h], rows)
            ds = (w * (dw - wide(row_dot_ref[h], rows))).astype(BF)
            dv = dv + dot_nn(dot_ref[h], w.astype(BF))
            dk = dk + dot_nn(qt_ref[h], ds)
            dq_ref[h] += dot_nn(ds, keys)
        key_parts[pl.ds(at, rows), :] = (dk * scale).T.astype(BF)
        value_parts[pl.ds(at, rows), :] = dv.T.astype(BF)
        return carry

    def zero_tile(t, carry):
        at = pl.multiple_of(t * rows, rows)
        key_parts[pl.ds(at, rows), :] = jnp.zeros((rows, head), BF)
        value_parts[pl.ds(at, rows), :] = jnp.zeros((rows, head), BF)
        return carry

    @pl.when(live > 0)
    def _():
        for block, _, at in slots:
            key_window[pl.ds(at, rows), :] = block[pl.ds(0, rows), :]
            value_window[pl.ds(at, rows), :] = block[pl.ds(rows, rows), :]
        lanes[...] = top0_ref[...]
        lax.fori_loop(0, live, score_tile, 0)
        for h in range(heads):
            top = across_lanes(lanes[h], jnp.max, lanes[h])
            top_ref[h] = top
            kept = jnp.exp2((top0_ref[h] - top) * to_exp2)
            second_ref[h] = kept
            inverse_ref[h] = total0_ref[h] * kept
            dq_ref[h] = out0_ref[h] * kept
        lanes[...] = jnp.zeros(lanes.shape, F32)
        lax.fori_loop(0, live, out_tile, 0)
        for h in range(heads):
            inverse_ref[h] += jnp.sum(lanes[h], axis=1, keepdims=True)

    @pl.when(live == 0)
    def _():
        top_ref[...] = top0_ref[...]
        second_ref[...] = jnp.ones(second_ref.shape, F32)
        inverse_ref[...] = total0_ref[...]
        dq_ref[...] = out0_ref[...]

    for h in range(heads):
        cols = pl.ds(h * head, head)
        inverse = 1.0 / inverse_ref[h]
        inverse_ref[h] = inverse
        second_ref[h] = second_ref[h] * inverse
        attended = (dq_ref[h] * inverse).astype(BF)
        att_ref[:, cols] = attended
        row_dot = jnp.sum(do_ref[:, cols].astype(F32) * attended.astype(F32), axis=1, keepdims=True)
        row_dot_ref[h] = jnp.broadcast_to(row_dot, (rows, head))
    dq_ref[...] = jnp.zeros(dq_ref.shape, F32)
    lax.fori_loop(0, live, grad_tile, 0)
    lax.fori_loop(live, 2, zero_tile, 0)
    for _, part, at in slots:
        part[pl.ds(0, rows), :] = key_parts[pl.ds(at, rows), :]
        part[pl.ds(rows, rows), :] = value_parts[pl.ds(at, rows), :]


def second_back_kernel(
    first_ref, do_ref, qt_ref, dot_ref, block_ref, tile_ref, factor_ref, row_dot_ref, far_ref,
    dq_ref, part_ref,
):
    heads, rows, head = far_ref.shape
    scale = score_scale(head)
    live = lowest_block(first_ref, rows) <= SPAN - 2

    @pl.when(live)
    def _():
        keys = block_ref[pl.ds(0, rows), :]
        values = block_ref[pl.ds(rows, rows), :]
        dv = jnp.zeros((head, rows), F32)
        dk = jnp.zeros((head, rows), F32)
        for h in range(heads):
            dw = dot_nt(do_ref[:, pl.ds(h * head, head)], values)
            w = tile_ref[h] * wide(factor_ref[h], rows)
            ds = (w * (dw - wide(row_dot_ref[h], rows))).astype(BF)
            dv = dv + dot_nn(dot_ref[h], w.astype(BF))
            dk = dk + dot_nn(qt_ref[h], ds)
            dq_ref[h] = far_ref[h] + dot_nn(ds, keys)
        part_ref[pl.ds(0, rows), :] = (dk * scale).T.astype(BF)
        part_ref[pl.ds(rows, rows), :] = dv.T.astype(BF)

    @pl.when(jnp.logical_not(live))
    def _():
        dq_ref[...] = far_ref[...]
        part_ref[...] = jnp.zeros(part_ref.shape, BF)


def own_kernel(
    q_ref, do_ref, qt_ref, dot_ref, own_ref, starts_ref, top_ref, inverse_ref, row_dot_ref, earlier_ref,
    attended_ref, dq_ref, part_ref, att_ref,
):
    rows, width = q_ref.shape
    head = own_ref.shape[1]
    heads = width // head
    to_exp2 = exp2_scale(head)
    scale = score_scale(head)
    column = lax.broadcasted_iota(jnp.int32, (rows, rows), 1)
    row = lax.broadcasted_iota(jnp.int32, (rows, rows), 0)
    allowed = (column >= wide(starts_ref[...], rows)) & (column <= row)
    keys = own_ref[pl.ds(0, rows), :]
    values = own_ref[pl.ds(rows, rows), :]
    dv = jnp.zeros((head, rows), F32)
    dk = jnp.zeros((head, rows), F32)
    att_ref[...] = attended_ref[...]
    for h in range(heads):
        cols = pl.ds(h * head, head)
        s = jnp.where(allowed, dot_nt(q_ref[:, cols], keys), -jnp.inf)
        w = jnp.exp2((s - wide(top_ref[h], rows)) * to_exp2) * wide(inverse_ref[h], rows)
        dw = dot_nt(do_ref[:, cols], values)
        ds = (w * (dw - wide(row_dot_ref[h], rows))).astype(BF)
        dv = dv + dot_nn(dot_ref[h], w.astype(BF))
        dk = dk + dot_nn(qt_ref[h], ds)
        dq_ref[:, cols] = ((earlier_ref[h] + dot_nn(ds, keys)) * scale).astype(BF)
    part_ref[pl.ds(0, rows), :] = (dk * scale).T.astype(BF)
    part_ref[pl.ds(rows, rows), :] = dv.T.astype(BF)


def sum_kernel(*refs):
    *terms, out_ref = refs
    out_ref[...] = sum(x[...].astype(F32) for x in terms).astype(BF)


def score_scale(head):
    return 1.0 / math.sqrt(head)


def exp2_scale(head):
    return score_scale(head) * math.log2(math.e)


VMEM = pl.BlockSpec(memory_space=pltpu.VMEM)
SMEM = pl.BlockSpec(memory_space=pltpu.SMEM)


def shape(dims, dtype):
    return jax.ShapeDtypeStruct(dims, dtype)


def on_core(kernel, name, mflop, mib, outs, ins, scratch=(), aliases={}):
    return pl.pallas_call(
        kernel,
        out_shape=tuple(outs),
        in_specs=[SMEM if x.ndim == 1 else VMEM for x in ins],
        out_specs=tuple(SMEM if len(x.shape) == 1 else VMEM for x in outs),
        scratch_shapes=list(scratch),
        input_output_aliases=aliases,
        compiler_params=pltpu.CompilerParams(vmem_limit_bytes=mib << 20),
        cost_estimate=pl.CostEstimate(
            flops=mflop * 1_000_000, bytes_accessed=2 << 20, transcendentals=1 << 19
        ),
        name=name,
    )(*ins)


def sizes(q, own):
    rows, width = q.shape
    head = own.shape[1]
    heads = width // head
    state = shape((heads, rows, head), F32)
    turned = shape((heads, head, rows), BF)
    tile = shape((heads, rows, rows), F32)
    return state, turned, tile, shape(q.shape, BF), shape(own.shape, BF)


def attention_before(place, lengths, q, do, own):
    state, turned, _, _, _ = sizes(q, own)
    starts = shape(state.shape[1:], jnp.int32)
    outs = [shape((1,), jnp.int32), starts, state, state, state, turned, turned]
    return on_core(diagonal_kernel, "diagonal", 1200, 20, outs, (place, lengths, q, do, own))


def attention_second(first, q, starts, top, total, out, two):
    state, _, tile, _, _ = sizes(q, two)
    ins = (first, q, starts, top, total, out, two)
    return on_core(second_kernel, "second", 1200, 20, [state, state, state, tile], ins)


def attention_far(place, first, q, do, qt, dot_, starts, top, total, out, mixed, swapped):
    state, _, tile, like_q, part = sizes(q, mixed)
    rows, head = state.shape[1:]
    return on_core(
        far_kernel,
        "far",
        3000,
        24,
        [like_q] + [state] * 5 + [part] * 2,
        (place, first, q, do, qt, dot_, starts, top, total, out, mixed, swapped),
        [pltpu.VMEM((2 * rows, head), BF)] * 4
        + [pltpu.VMEM((state.shape[0], 2, rows, rows), F32), pltpu.VMEM(state.shape, F32)],
    )


def attention_second_back(first, q, do, qt, dot_, two, tile, factor, row_dot, dq):
    state, _, _, _, part = sizes(q, two)
    ins = (first, do, qt, dot_, two, tile, factor, row_dot, dq)
    return on_core(second_back_kernel, "second_back", 1500, 20, [state, part], ins)


def attention_own(q, do, qt, dot_, own, starts, top, inverse, row_dot, dq, attended):
    _, _, _, like_q, part = sizes(q, own)
    ins = (q, do, qt, dot_, own, starts, top, inverse, row_dot, dq, attended)
    return on_core(own_kernel, "own", 2500, 20, [like_q, part, like_q], ins)


def summed(*terms):
    return on_core(sum_kernel, "sum", 1, 6, [shape(terms[0].shape, BF)], terms)[0]


def pack_kernel(key_ref, value_ref, both_ref, sems):
    rows = key_ref.shape[0]
    copies = [
        pltpu.make_async_copy(key_ref, both_ref.at[pl.ds(0, rows)], sems.at[0]),
        pltpu.make_async_copy(value_ref, both_ref.at[pl.ds(rows, rows)], sems.at[1]),
    ]
    for copy in copies:
        copy.start()
    for copy in copies:
        copy.wait()


def packed(keys, values):
    rows, head = keys.shape
    return pl.pallas_call(
        pack_kernel,
        out_shape=jax.ShapeDtypeStruct((2 * rows, head), BF),
        in_specs=[pl.BlockSpec(memory_space=pltpu.HBM)] * 2,
        out_specs=VMEM,
        scratch_shapes=[pltpu.SemaphoreType.DMA((2,))],
        compiler_params=pltpu.CompilerParams(vmem_limit_bytes=2 << 20),
        name="pack",
    )(keys, values)


def head_sum(part):
    heads = lax.axis_size("head")
    pieces = part.reshape(heads, part.shape[0] // heads, part.shape[1])
    theirs = lax.all_to_all(pieces, "head", split_axis=0, concat_axis=0)
    mine = jnp.sum(theirs.astype(F32), axis=0).astype(BF)
    mine = jnp.broadcast_to(mine[None], pieces.shape)
    return lax.all_to_all(mine, "head", split_axis=0, concat_axis=0).reshape(part.shape)


def moved(value, pairs):
    return lax.ppermute(value, "ctx", pairs)


def on_device(queries, keys, values, d_out, doc_lengths):
    count = lax.axis_size("ctx")
    rows = keys.shape[0]
    place = lax.axis_index("ctx").reshape(1).astype(jnp.int32)
    two_on = [(i, i + 2) for i in range(count - 2)]
    mixed_on = [(i, i + (3 if i % 2 else 1)) for i in range(count) if i + (3 if i % 2 else 1) < count]
    across = [(i, i ^ 1) for i in range(count)]

    def back(pairs):
        return [(there, here) for here, there in pairs]

    lengths = doc_lengths.reshape(1, -1)
    own = packed(keys, values)
    two = moved(own, two_on)
    mixed = moved(own, mixed_on)
    first, starts, top, total, out, qt, dot_ = attention_before(place, lengths, queries, d_out, own)
    two, first = lax.optimization_barrier((two, first))
    swapped = moved(two, across)
    top, total, out, tile = attention_second(first, queries, starts, top, total, out, two)
    attended, top, inverse, row_dot, factor, dq, mixed_part, swapped_part = attention_far(
        place, first, queries, d_out, qt, dot_, starts, top, total, out, mixed, swapped
    )
    from_mixed = moved(mixed_part, back(mixed_on))
    from_core = moved(swapped_part, across)
    dq, two_part = attention_second_back(
        first, queries, d_out, qt, dot_, two, tile, factor, row_dot, dq
    )
    from_two = moved(summed(two_part, from_core), back(two_on))
    d_queries, own_part, attended = attention_own(
        queries, d_out, qt, dot_, own, starts, top, inverse, row_dot, dq, attended
    )
    both = head_sum(summed(own_part, from_two, from_mixed))
    return (attended, d_queries, both[:rows], both[rows:])


def solution(mesh):
    in_specs = (P("ctx", "head"), P("ctx", None), P("ctx", None), P("ctx", "head"), P())
    out_specs = (P("ctx", "head"), P("ctx", "head"), P("ctx", None), P("ctx", None))
    return jax.shard_map(
        on_device, mesh=mesh, in_specs=in_specs, out_specs=out_specs, check_vma=False
    )
```

```python
import functools
import math

import jax
import jax.numpy as jnp
from jax import lax
from jax.experimental import pallas as pl
from jax.experimental.pallas import tpu as pltpu
from jax.sharding import PartitionSpec as P

SPAN = 3
BF = jnp.bfloat16
F32 = jnp.float32


def dot_nt(a, b):
    return lax.dot_general(a, b, (((1,), (1,)), ((), ())), preferred_element_type=F32)


def dot_nn(a, b):
    return jnp.dot(a, b, preferred_element_type=F32)


def wide(x, width):
    return jnp.concatenate([x] * (width // x.shape[1]), axis=1)


def folded(x, width, op):
    return functools.reduce(op, [x[:, c : c + width] for c in range(0, x.shape[1], width)])


def across_lanes(x, op, like):
    return jnp.broadcast_to(op(x, axis=1, keepdims=True), like.shape)


def lowest_block(first_ref, rows):
    return jnp.minimum(jnp.maximum(first_ref[0], 0) // rows, SPAN)


def diagonal_kernel(
    place_ref, lengths_ref, q_ref, do_ref, own_ref,
    first_ref, starts_ref, top_ref, total_ref, out_ref, qt_ref, dot_ref,
):
    rows, width = q_ref.shape
    head = own_ref.shape[1]
    heads = width // head
    lead = SPAN * rows
    lengths = lengths_ref[...].astype(F32)
    docs = lengths.shape[1]
    along = jnp.broadcast_to(lengths, (docs, docs))
    earlier = lax.broadcasted_iota(jnp.int32, (docs, docs), 0)
    later = lax.broadcasted_iota(jnp.int32, (docs, docs), 1)
    ends = jnp.sum(jnp.where(earlier <= later, along.T, 0.0), axis=0, keepdims=True)
    begin = (place_ref[0] * rows).astype(F32)
    positions = begin + lax.broadcasted_iota(jnp.int32, (rows, docs), 0).astype(F32)
    doc_start = jnp.sum(jnp.where(ends <= positions, lengths, 0.0), axis=1, keepdims=True)
    start = (doc_start - begin).astype(jnp.int32)
    starts_ref[...] = jnp.broadcast_to(start, starts_ref.shape)
    first_ref[0] = jnp.min(start) + lead

    column = lax.broadcasted_iota(jnp.int32, (rows, rows), 1)
    row = lax.broadcasted_iota(jnp.int32, (rows, rows), 0)
    allowed = (column >= start) & (column <= row)
    keys = own_ref[pl.ds(0, rows), :]
    values = own_ref[pl.ds(rows, rows), :]
    for h in range(heads):
        cols = pl.ds(h * head, head)
        s = jnp.where(allowed, dot_nt(q_ref[:, cols], keys), -jnp.inf)
        m = jnp.max(s, axis=1, keepdims=True)
        e = jnp.exp2((s - m) * exp2_scale(head))
        top_ref[h] = jnp.broadcast_to(m, (rows, head))
        total_ref[h] = jnp.broadcast_to(jnp.sum(e, axis=1, keepdims=True), (rows, head))
        out_ref[h] = dot_nn(e.astype(BF), values)
        qt_ref[h] = q_ref[:, cols].T
        dot_ref[h] = do_ref[:, cols].T


def second_kernel(
    first_ref, q_ref, starts_ref, top0_ref, total0_ref, out0_ref, block_ref,
    top_ref, total_ref, out_ref, tile_ref,
):
    rows, width = q_ref.shape
    head = block_ref.shape[1]
    heads = width // head
    to_exp2 = exp2_scale(head)
    place = SPAN - 2
    live = lowest_block(first_ref, rows) <= place

    @pl.when(live)
    def _():
        keys = block_ref[pl.ds(0, rows), :]
        values = block_ref[pl.ds(rows, rows), :]
        column = lax.broadcasted_iota(jnp.int32, (rows, rows), 1)
        allowed = column >= wide(starts_ref[...] + (SPAN - place) * rows, rows)
        for h in range(heads):
            s = jnp.where(allowed, dot_nt(q_ref[:, pl.ds(h * head, head)], keys), -jnp.inf)
            top0 = top0_ref[h]
            top = across_lanes(jnp.maximum(folded(s, head, jnp.maximum), top0), jnp.max, top0)
            e = jnp.exp2((s - wide(top, rows)) * to_exp2)
            kept = jnp.exp2((top0 - top) * to_exp2)
            tile_ref[h] = e
            top_ref[h] = top
            total_ref[h] = total0_ref[h] * kept + across_lanes(folded(e, head, jnp.add), jnp.sum, top)
            out_ref[h] = out0_ref[h] * kept + dot_nn(e.astype(BF), values)

    @pl.when(jnp.logical_not(live))
    def _():
        top_ref[...] = top0_ref[...]
        total_ref[...] = total0_ref[...]
        out_ref[...] = out0_ref[...]


def far_kernel(
    place_ref, first_ref, q_ref, do_ref, qt_ref, dot_ref, starts_ref, top0_ref, total0_ref, out0_ref,
    mixed_ref, swapped_ref,
    att_ref, top_ref, inverse_ref, row_dot_ref, second_ref, dq_ref, mixed_part_ref, swapped_part_ref,
    key_window, value_window, key_parts, value_parts, tiles, lanes,
):
    rows, width = q_ref.shape
    head = mixed_ref.shape[1]
    heads = width // head
    to_exp2 = exp2_scale(head)
    scale = score_scale(head)
    odd = lax.rem(place_ref[0], 2)
    mixed_row = pl.multiple_of((1 - odd) * rows, rows)
    swapped_row = pl.multiple_of(odd * rows, rows)
    slots = (
        (mixed_ref, mixed_part_ref, mixed_row),
        (swapped_ref, swapped_part_ref, swapped_row),
    )
    low = lowest_block(first_ref, rows)
    live = (low < SPAN).astype(jnp.int32) + (low < 1).astype(jnp.int32)
    column = lax.broadcasted_iota(jnp.int32, (rows, rows), 1)

    def score_tile(t, carry):
        at = pl.multiple_of(t * rows, rows)
        keys = key_window[pl.ds(at, rows), :]
        allowed = column >= wide(starts_ref[...] + (rows + 2 * at), rows)
        for h in range(heads):
            s = dot_nt(q_ref[:, pl.ds(h * head, head)], keys)
            s = jnp.where(allowed, s, -jnp.inf)
            tiles[h, t] = s
            lanes[h] = jnp.maximum(lanes[h], folded(s, head, jnp.maximum))
        return carry

    def out_tile(t, carry):
        at = pl.multiple_of(t * rows, rows)
        values = value_window[pl.ds(at, rows), :]
        for h in range(heads):
            e = jnp.exp2((tiles[h, t] - wide(top_ref[h], rows)) * to_exp2)
            tiles[h, t] = e
            lanes[h] += folded(e, head, jnp.add)
            dq_ref[h] += dot_nn(e.astype(BF), values)
        return carry

    def grad_tile(t, carry):
        at = pl.multiple_of(t * rows, rows)
        keys = key_window[pl.ds(at, rows), :]
        values = value_window[pl.ds(at, rows), :]
        dv = jnp.zeros((head, rows), F32)
        dk = jnp.zeros((head, rows), F32)
        for h in range(heads):
            dw = dot_nt(do_ref[:, pl.ds(h * head, head)], values)
            w = tiles[h, t] * wide(inverse_ref[h], rows)
            ds = (w * (dw - wide(row_dot_ref[h], rows))).astype(BF)
            dv = dv + dot_nn(dot_ref[h], w.astype(BF))
            dk = dk + dot_nn(qt_ref[h], ds)
            dq_ref[h] += dot_nn(ds, keys)
        key_parts[pl.ds(at, rows), :] = (dk * scale).T.astype(BF)
        value_parts[pl.ds(at, rows), :] = dv.T.astype(BF)
        return carry

    def zero_tile(t, carry):
        at = pl.multiple_of(t * rows, rows)
        key_parts[pl.ds(at, rows), :] = jnp.zeros((rows, head), BF)
        value_parts[pl.ds(at, rows), :] = jnp.zeros((rows, head), BF)
        return carry

    @pl.when(live > 0)
    def _():
        for block, _, at in slots:
            key_window[pl.ds(at, rows), :] = block[pl.ds(0, rows), :]
            value_window[pl.ds(at, rows), :] = block[pl.ds(rows, rows), :]
        lanes[...] = top0_ref[...]
        lax.fori_loop(0, live, score_tile, 0)
        for h in range(heads):
            top = across_lanes(lanes[h], jnp.max, lanes[h])
            top_ref[h] = top
            kept = jnp.exp2((top0_ref[h] - top) * to_exp2)
            second_ref[h] = kept
            inverse_ref[h] = total0_ref[h] * kept
            dq_ref[h] = out0_ref[h] * kept
        lanes[...] = jnp.zeros(lanes.shape, F32)
        lax.fori_loop(0, live, out_tile, 0)
        for h in range(heads):
            inverse_ref[h] += jnp.sum(lanes[h], axis=1, keepdims=True)

    @pl.when(live == 0)
    def _():
        top_ref[...] = top0_ref[...]
        second_ref[...] = jnp.ones(second_ref.shape, F32)
        inverse_ref[...] = total0_ref[...]
        dq_ref[...] = out0_ref[...]

    for h in range(heads):
        cols = pl.ds(h * head, head)
        inverse = 1.0 / inverse_ref[h]
        inverse_ref[h] = inverse
        second_ref[h] = second_ref[h] * inverse
        attended = (dq_ref[h] * inverse).astype(BF)
        att_ref[:, cols] = attended
        row_dot = jnp.sum(do_ref[:, cols].astype(F32) * attended.astype(F32), axis=1, keepdims=True)
        row_dot_ref[h] = jnp.broadcast_to(row_dot, (rows, head))
    dq_ref[...] = jnp.zeros(dq_ref.shape, F32)
    lax.fori_loop(0, live, grad_tile, 0)
    lax.fori_loop(live, 2, zero_tile, 0)
    for _, part, at in slots:
        part[pl.ds(0, rows), :] = key_parts[pl.ds(at, rows), :]
        part[pl.ds(rows, rows), :] = value_parts[pl.ds(at, rows), :]


def second_back_kernel(
    first_ref, do_ref, qt_ref, dot_ref, block_ref, tile_ref, factor_ref, row_dot_ref, far_ref,
    dq_ref, part_ref,
):
    heads, rows, head = far_ref.shape
    scale = score_scale(head)
    live = lowest_block(first_ref, rows) <= SPAN - 2

    @pl.when(live)
    def _():
        keys = block_ref[pl.ds(0, rows), :]
        values = block_ref[pl.ds(rows, rows), :]
        dv = jnp.zeros((head, rows), F32)
        dk = jnp.zeros((head, rows), F32)
        for h in range(heads):
            dw = dot_nt(do_ref[:, pl.ds(h * head, head)], values)
            w = tile_ref[h] * wide(factor_ref[h], rows)
            ds = (w * (dw - wide(row_dot_ref[h], rows))).astype(BF)
            dv = dv + dot_nn(dot_ref[h], w.astype(BF))
            dk = dk + dot_nn(qt_ref[h], ds)
            dq_ref[h] = far_ref[h] + dot_nn(ds, keys)
        part_ref[pl.ds(0, rows), :] = (dk * scale).T.astype(BF)
        part_ref[pl.ds(rows, rows), :] = dv.T.astype(BF)

    @pl.when(jnp.logical_not(live))
    def _():
        dq_ref[...] = far_ref[...]
        part_ref[...] = jnp.zeros(part_ref.shape, BF)


def own_kernel(
    q_ref, do_ref, qt_ref, dot_ref, own_ref, starts_ref, top_ref, inverse_ref, row_dot_ref, earlier_ref,
    attended_ref, dq_ref, part_ref, att_ref,
):
    rows, width = q_ref.shape
    head = own_ref.shape[1]
    heads = width // head
    to_exp2 = exp2_scale(head)
    scale = score_scale(head)
    column = lax.broadcasted_iota(jnp.int32, (rows, rows), 1)
    row = lax.broadcasted_iota(jnp.int32, (rows, rows), 0)
    allowed = (column >= wide(starts_ref[...], rows)) & (column <= row)
    keys = own_ref[pl.ds(0, rows), :]
    values = own_ref[pl.ds(rows, rows), :]
    dv = jnp.zeros((head, rows), F32)
    dk = jnp.zeros((head, rows), F32)
    att_ref[...] = attended_ref[...]
    for h in range(heads):
        cols = pl.ds(h * head, head)
        s = jnp.where(allowed, dot_nt(q_ref[:, cols], keys), -jnp.inf)
        w = jnp.exp2((s - wide(top_ref[h], rows)) * to_exp2) * wide(inverse_ref[h], rows)
        dw = dot_nt(do_ref[:, cols], values)
        ds = (w * (dw - wide(row_dot_ref[h], rows))).astype(BF)
        dv = dv + dot_nn(dot_ref[h], w.astype(BF))
        dk = dk + dot_nn(qt_ref[h], ds)
        dq_ref[:, cols] = ((earlier_ref[h] + dot_nn(ds, keys)) * scale).astype(BF)
    part_ref[pl.ds(0, rows), :] = (dk * scale).T.astype(BF)
    part_ref[pl.ds(rows, rows), :] = dv.T.astype(BF)


def sum_kernel(*refs):
    *terms, out_ref = refs
    out_ref[...] = sum(x[...].astype(F32) for x in terms).astype(BF)


def score_scale(head):
    return 1.0 / math.sqrt(head)


def exp2_scale(head):
    return score_scale(head) * math.log2(math.e)


VMEM = pl.BlockSpec(memory_space=pltpu.VMEM)
SMEM = pl.BlockSpec(memory_space=pltpu.SMEM)


def shape(dims, dtype):
    return jax.ShapeDtypeStruct(dims, dtype)


def on_core(kernel, name, mflop, mib, outs, ins, scratch=(), aliases={}):
    return pl.pallas_call(
        kernel,
        out_shape=tuple(outs),
        in_specs=[SMEM if x.ndim == 1 else VMEM for x in ins],
        out_specs=tuple(SMEM if len(x.shape) == 1 else VMEM for x in outs),
        scratch_shapes=list(scratch),
        input_output_aliases=aliases,
        compiler_params=pltpu.CompilerParams(vmem_limit_bytes=mib << 20),
        cost_estimate=pl.CostEstimate(
            flops=mflop * 1_000_000, bytes_accessed=2 << 20, transcendentals=1 << 19
        ),
        name=name,
    )(*ins)


def sizes(q, own):
    rows, width = q.shape
    head = own.shape[1]
    heads = width // head
    state = shape((heads, rows, head), F32)
    turned = shape((heads, head, rows), BF)
    tile = shape((heads, rows, rows), F32)
    return state, turned, tile, shape(q.shape, BF), shape(own.shape, BF)


def attention_before(place, lengths, q, do, own):
    state, turned, _, _, _ = sizes(q, own)
    starts = shape(state.shape[1:], jnp.int32)
    outs = [shape((1,), jnp.int32), starts, state, state, state, turned, turned]
    return on_core(diagonal_kernel, "diagonal", 1200, 20, outs, (place, lengths, q, do, own))


def attention_second(first, q, starts, top, total, out, two):
    state, _, tile, _, _ = sizes(q, two)
    ins = (first, q, starts, top, total, out, two)
    return on_core(second_kernel, "second", 1200, 20, [state, state, state, tile], ins)


def attention_far(place, first, q, do, qt, dot_, starts, top, total, out, mixed, swapped):
    state, _, tile, like_q, part = sizes(q, mixed)
    rows, head = state.shape[1:]
    return on_core(
        far_kernel,
        "far",
        3000,
        24,
        [like_q] + [state] * 5 + [part] * 2,
        (place, first, q, do, qt, dot_, starts, top, total, out, mixed, swapped),
        [pltpu.VMEM((2 * rows, head), BF)] * 4
        + [pltpu.VMEM((state.shape[0], 2, rows, rows), F32), pltpu.VMEM(state.shape, F32)],
    )


def attention_second_back(first, q, do, qt, dot_, two, tile, factor, row_dot, dq):
    state, _, _, _, part = sizes(q, two)
    ins = (first, do, qt, dot_, two, tile, factor, row_dot, dq)
    return on_core(second_back_kernel, "second_back", 1500, 20, [state, part], ins)


def attention_own(q, do, qt, dot_, own, starts, top, inverse, row_dot, dq, attended):
    _, _, _, like_q, part = sizes(q, own)
    ins = (q, do, qt, dot_, own, starts, top, inverse, row_dot, dq, attended)
    return on_core(own_kernel, "own", 2500, 20, [like_q, part, like_q], ins)


def summed(*terms):
    return on_core(sum_kernel, "sum", 1, 6, [shape(terms[0].shape, BF)], terms)[0]


def pack_kernel(key_ref, value_ref, both_ref, sems):
    rows = key_ref.shape[0]
    copies = [
        pltpu.make_async_copy(key_ref, both_ref.at[pl.ds(0, rows)], sems.at[0]),
        pltpu.make_async_copy(value_ref, both_ref.at[pl.ds(rows, rows)], sems.at[1]),
    ]
    for copy in copies:
        copy.start()
    for copy in copies:
        copy.wait()


def packed(keys, values):
    rows, head = keys.shape
    return pl.pallas_call(
        pack_kernel,
        out_shape=jax.ShapeDtypeStruct((2 * rows, head), BF),
        in_specs=[pl.BlockSpec(memory_space=pltpu.HBM)] * 2,
        out_specs=VMEM,
        scratch_shapes=[pltpu.SemaphoreType.DMA((2,))],
        compiler_params=pltpu.CompilerParams(vmem_limit_bytes=2 << 20),
        name="pack",
    )(keys, values)


def head_sum(part):
    heads = lax.axis_size("head")
    pieces = part.reshape(heads, part.shape[0] // heads, part.shape[1])
    theirs = lax.all_to_all(pieces, "head", split_axis=0, concat_axis=0)
    mine = jnp.sum(theirs.astype(F32), axis=0).astype(BF)
    mine = jnp.broadcast_to(mine[None], pieces.shape)
    return lax.all_to_all(mine, "head", split_axis=0, concat_axis=0).reshape(part.shape)


def moved(value, pairs):
    return lax.ppermute(value, "ctx", pairs)


def on_device(queries, keys, values, d_out, doc_lengths):
    count = lax.axis_size("ctx")
    rows = keys.shape[0]
    place = lax.axis_index("ctx").reshape(1).astype(jnp.int32)
    two_on = [(i, i + 2) for i in range(count - 2)]
    mixed_on = [(i, i + (3 if i % 2 else 1)) for i in range(count) if i + (3 if i % 2 else 1) < count]
    across = [(i, i ^ 1) for i in range(count)]

    def back(pairs):
        return [(there, here) for here, there in pairs]

    lengths = doc_lengths.reshape(1, -1)
    two_keys = moved(keys, two_on)
    two_values = moved(values, two_on)
    own = packed(keys, values)
    mixed = moved(own, mixed_on)
    first, starts, top, total, out, qt, dot_ = attention_before(place, lengths, queries, d_out, own)
    two = packed(two_keys, two_values)
    two, first = lax.optimization_barrier((two, first))
    swapped = moved(two, across)
    top, total, out, tile = attention_second(first, queries, starts, top, total, out, two)
    attended, top, inverse, row_dot, factor, dq, mixed_part, swapped_part = attention_far(
        place, first, queries, d_out, qt, dot_, starts, top, total, out, mixed, swapped
    )
    from_mixed = moved(mixed_part, back(mixed_on))
    from_core = moved(swapped_part, across)
    dq, two_part = attention_second_back(
        first, queries, d_out, qt, dot_, two, tile, factor, row_dot, dq
    )
    from_two = moved(summed(two_part, from_core), back(two_on))
    d_queries, own_part, attended = attention_own(
        queries, d_out, qt, dot_, own, starts, top, inverse, row_dot, dq, attended
    )
    both = head_sum(summed(own_part, from_two, from_mixed))
    return (attended, d_queries, both[:rows], both[rows:])


def solution(mesh):
    in_specs = (P("ctx", "head"), P("ctx", None), P("ctx", None), P("ctx", "head"), P())
    out_specs = (P("ctx", "head"), P("ctx", "head"), P("ctx", None), P("ctx", None))
    return jax.shard_map(
        on_device, mesh=mesh, in_specs=in_specs, out_specs=out_specs, check_vma=False
    )
```

```python
import functools
import math

import jax
import jax.numpy as jnp
from jax import lax
from jax.experimental import pallas as pl
from jax.experimental.pallas import tpu as pltpu
from jax.sharding import PartitionSpec as P

SPAN = 3
BF = jnp.bfloat16
F32 = jnp.float32


def dot_nt(a, b):
    return lax.dot_general(a, b, (((1,), (1,)), ((), ())), preferred_element_type=F32)


def dot_nn(a, b):
    return jnp.dot(a, b, preferred_element_type=F32)


def wide(x, width):
    return jnp.concatenate([x] * (width // x.shape[1]), axis=1)


def folded(x, width, op):
    return functools.reduce(op, [x[:, c : c + width] for c in range(0, x.shape[1], width)])


def across_lanes(x, op, like):
    return jnp.broadcast_to(op(x, axis=1, keepdims=True), like.shape)


def lowest_block(first_ref, rows):
    return jnp.minimum(jnp.maximum(first_ref[0], 0) // rows, SPAN)


def diagonal_kernel(
    place_ref, lengths_ref, q_ref, do_ref, own_ref,
    first_ref, starts_ref, top_ref, total_ref, out_ref, qt_ref, dot_ref,
):
    rows, width = q_ref.shape
    head = own_ref.shape[1]
    heads = width // head
    lead = SPAN * rows
    lengths = lengths_ref[...].astype(F32)
    docs = lengths.shape[1]
    along = jnp.broadcast_to(lengths, (docs, docs))
    earlier = lax.broadcasted_iota(jnp.int32, (docs, docs), 0)
    later = lax.broadcasted_iota(jnp.int32, (docs, docs), 1)
    ends = jnp.sum(jnp.where(earlier <= later, along.T, 0.0), axis=0, keepdims=True)
    begin = (place_ref[0] * rows).astype(F32)
    positions = begin + lax.broadcasted_iota(jnp.int32, (rows, docs), 0).astype(F32)
    doc_start = jnp.sum(jnp.where(ends <= positions, lengths, 0.0), axis=1, keepdims=True)
    start = (doc_start - begin).astype(jnp.int32)
    starts_ref[...] = jnp.broadcast_to(start, starts_ref.shape)
    first_ref[0] = jnp.min(start) + lead

    column = lax.broadcasted_iota(jnp.int32, (rows, rows), 1)
    row = lax.broadcasted_iota(jnp.int32, (rows, rows), 0)
    allowed = (column >= start) & (column <= row)
    keys = own_ref[pl.ds(0, rows), :]
    values = own_ref[pl.ds(rows, rows), :]
    for h in range(heads):
        cols = pl.ds(h * head, head)
        s = jnp.where(allowed, dot_nt(q_ref[:, cols], keys), -jnp.inf)
        m = jnp.max(s, axis=1, keepdims=True)
        e = jnp.exp2((s - m) * exp2_scale(head))
        top_ref[h] = jnp.broadcast_to(m, (rows, head))
        total_ref[h] = jnp.broadcast_to(jnp.sum(e, axis=1, keepdims=True), (rows, head))
        out_ref[h] = dot_nn(e.astype(BF), values)
        qt_ref[h] = q_ref[:, cols].T
        dot_ref[h] = do_ref[:, cols].T


def second_kernel(
    first_ref, q_ref, starts_ref, top0_ref, total0_ref, out0_ref, block_ref,
    top_ref, total_ref, out_ref, tile_ref,
):
    rows, width = q_ref.shape
    head = block_ref.shape[1]
    heads = width // head
    to_exp2 = exp2_scale(head)
    place = SPAN - 2
    live = lowest_block(first_ref, rows) <= place

    @pl.when(live)
    def _():
        keys = block_ref[pl.ds(0, rows), :]
        values = block_ref[pl.ds(rows, rows), :]
        column = lax.broadcasted_iota(jnp.int32, (rows, rows), 1)
        allowed = column >= wide(starts_ref[...] + (SPAN - place) * rows, rows)
        for h in range(heads):
            s = jnp.where(allowed, dot_nt(q_ref[:, pl.ds(h * head, head)], keys), -jnp.inf)
            top0 = top0_ref[h]
            top = across_lanes(jnp.maximum(folded(s, head, jnp.maximum), top0), jnp.max, top0)
            e = jnp.exp2((s - wide(top, rows)) * to_exp2)
            kept = jnp.exp2((top0 - top) * to_exp2)
            tile_ref[h] = e
            top_ref[h] = top
            total_ref[h] = total0_ref[h] * kept + across_lanes(folded(e, head, jnp.add), jnp.sum, top)
            out_ref[h] = out0_ref[h] * kept + dot_nn(e.astype(BF), values)

    @pl.when(jnp.logical_not(live))
    def _():
        top_ref[...] = top0_ref[...]
        total_ref[...] = total0_ref[...]
        out_ref[...] = out0_ref[...]


def far_kernel(
    place_ref, first_ref, q_ref, do_ref, qt_ref, dot_ref, starts_ref, top0_ref, total0_ref, out0_ref,
    mixed_ref, swapped_ref,
    att_ref, top_ref, inverse_ref, row_dot_ref, second_ref, dq_ref, mixed_part_ref, swapped_part_ref,
    key_window, value_window, key_parts, value_parts, tiles, lanes,
):
    rows, width = q_ref.shape
    head = mixed_ref.shape[1]
    heads = width // head
    to_exp2 = exp2_scale(head)
    scale = score_scale(head)
    odd = lax.rem(place_ref[0], 2)
    mixed_row = pl.multiple_of((1 - odd) * rows, rows)
    swapped_row = pl.multiple_of(odd * rows, rows)
    slots = (
        (mixed_ref, mixed_part_ref, mixed_row),
        (swapped_ref, swapped_part_ref, swapped_row),
    )
    low = lowest_block(first_ref, rows)
    live = (low < SPAN).astype(jnp.int32) + (low < 1).astype(jnp.int32)
    column = lax.broadcasted_iota(jnp.int32, (rows, rows), 1)

    def score_tile(t, carry):
        at = pl.multiple_of(t * rows, rows)
        keys = key_window[pl.ds(at, rows), :]
        allowed = column >= wide(starts_ref[...] + (rows + 2 * at), rows)
        for h in range(heads):
            s = dot_nt(q_ref[:, pl.ds(h * head, head)], keys)
            s = jnp.where(allowed, s, -jnp.inf)
            tiles[h, t] = s
            lanes[h] = jnp.maximum(lanes[h], folded(s, head, jnp.maximum))
        return carry

    def out_tile(t, carry):
        at = pl.multiple_of(t * rows, rows)
        values = value_window[pl.ds(at, rows), :]
        for h in range(heads):
            e = jnp.exp2((tiles[h, t] - wide(top_ref[h], rows)) * to_exp2)
            tiles[h, t] = e
            lanes[h] += folded(e, head, jnp.add)
            dq_ref[h] += dot_nn(e.astype(BF), values)
        return carry

    def grad_tile(t, carry):
        at = pl.multiple_of(t * rows, rows)
        keys = key_window[pl.ds(at, rows), :]
        values = value_window[pl.ds(at, rows), :]
        dv = jnp.zeros((head, rows), F32)
        dk = jnp.zeros((head, rows), F32)
        for h in range(heads):
            dw = dot_nt(do_ref[:, pl.ds(h * head, head)], values)
            w = tiles[h, t] * wide(inverse_ref[h], rows)
            ds = (w * (dw - wide(row_dot_ref[h], rows))).astype(BF)
            dv = dv + dot_nn(dot_ref[h], w.astype(BF))
            dk = dk + dot_nn(qt_ref[h], ds)
            dq_ref[h] += dot_nn(ds, keys)
        key_parts[pl.ds(at, rows), :] = (dk * scale).T.astype(BF)
        value_parts[pl.ds(at, rows), :] = dv.T.astype(BF)
        return carry

    def zero_tile(t, carry):
        at = pl.multiple_of(t * rows, rows)
        key_parts[pl.ds(at, rows), :] = jnp.zeros((rows, head), BF)
        value_parts[pl.ds(at, rows), :] = jnp.zeros((rows, head), BF)
        return carry

    @pl.when(live > 0)
    def _():
        for block, _, at in slots:
            key_window[pl.ds(at, rows), :] = block[pl.ds(0, rows), :]
            value_window[pl.ds(at, rows), :] = block[pl.ds(rows, rows), :]
        lanes[...] = top0_ref[...]
        lax.fori_loop(0, live, score_tile, 0)
        for h in range(heads):
            top = across_lanes(lanes[h], jnp.max, lanes[h])
            top_ref[h] = top
            kept = jnp.exp2((top0_ref[h] - top) * to_exp2)
            second_ref[h] = kept
            inverse_ref[h] = total0_ref[h] * kept
            dq_ref[h] = out0_ref[h] * kept
        lanes[...] = jnp.zeros(lanes.shape, F32)
        lax.fori_loop(0, live, out_tile, 0)
        for h in range(heads):
            inverse_ref[h] += jnp.sum(lanes[h], axis=1, keepdims=True)

    @pl.when(live == 0)
    def _():
        top_ref[...] = top0_ref[...]
        second_ref[...] = jnp.ones(second_ref.shape, F32)
        inverse_ref[...] = total0_ref[...]
        dq_ref[...] = out0_ref[...]

    for h in range(heads):
        cols = pl.ds(h * head, head)
        inverse = 1.0 / inverse_ref[h]
        inverse_ref[h] = inverse
        second_ref[h] = second_ref[h] * inverse
        attended = (dq_ref[h] * inverse).astype(BF)
        att_ref[:, cols] = attended
        row_dot = jnp.sum(do_ref[:, cols].astype(F32) * attended.astype(F32), axis=1, keepdims=True)
        row_dot_ref[h] = jnp.broadcast_to(row_dot, (rows, head))
    dq_ref[...] = jnp.zeros(dq_ref.shape, F32)
    lax.fori_loop(0, live, grad_tile, 0)
    lax.fori_loop(live, 2, zero_tile, 0)
    for _, part, at in slots:
        part[pl.ds(0, rows), :] = key_parts[pl.ds(at, rows), :]
        part[pl.ds(rows, rows), :] = value_parts[pl.ds(at, rows), :]


def second_back_kernel(
    first_ref, do_ref, qt_ref, dot_ref, block_ref, tile_ref, factor_ref, row_dot_ref, far_ref,
    dq_ref, part_ref,
):
    heads, rows, head = far_ref.shape
    scale = score_scale(head)
    live = lowest_block(first_ref, rows) <= SPAN - 2

    @pl.when(live)
    def _():
        keys = block_ref[pl.ds(0, rows), :]
        values = block_ref[pl.ds(rows, rows), :]
        dv = jnp.zeros((head, rows), F32)
        dk = jnp.zeros((head, rows), F32)
        for h in range(heads):
            dw = dot_nt(do_ref[:, pl.ds(h * head, head)], values)
            w = tile_ref[h] * wide(factor_ref[h], rows)
            ds = (w * (dw - wide(row_dot_ref[h], rows))).astype(BF)
            dv = dv + dot_nn(dot_ref[h], w.astype(BF))
            dk = dk + dot_nn(qt_ref[h], ds)
            dq_ref[h] = far_ref[h] + dot_nn(ds, keys)
        part_ref[pl.ds(0, rows), :] = (dk * scale).T.astype(BF)
        part_ref[pl.ds(rows, rows), :] = dv.T.astype(BF)

    @pl.when(jnp.logical_not(live))
    def _():
        dq_ref[...] = far_ref[...]
        part_ref[...] = jnp.zeros(part_ref.shape, BF)


def own_kernel(
    q_ref, do_ref, qt_ref, dot_ref, own_ref, starts_ref, top_ref, inverse_ref, row_dot_ref, earlier_ref,
    attended_ref, dq_ref, part_ref, att_ref,
):
    rows, width = q_ref.shape
    head = own_ref.shape[1]
    heads = width // head
    to_exp2 = exp2_scale(head)
    scale = score_scale(head)
    column = lax.broadcasted_iota(jnp.int32, (rows, rows), 1)
    row = lax.broadcasted_iota(jnp.int32, (rows, rows), 0)
    allowed = (column >= wide(starts_ref[...], rows)) & (column <= row)
    keys = own_ref[pl.ds(0, rows), :]
    values = own_ref[pl.ds(rows, rows), :]
    dv = jnp.zeros((head, rows), F32)
    dk = jnp.zeros((head, rows), F32)
    att_ref[...] = attended_ref[...]
    for h in range(heads):
        cols = pl.ds(h * head, head)
        s = jnp.where(allowed, dot_nt(q_ref[:, cols], keys), -jnp.inf)
        w = jnp.exp2((s - wide(top_ref[h], rows)) * to_exp2) * wide(inverse_ref[h], rows)
        dw = dot_nt(do_ref[:, cols], values)
        ds = (w * (dw - wide(row_dot_ref[h], rows))).astype(BF)
        dv = dv + dot_nn(dot_ref[h], w.astype(BF))
        dk = dk + dot_nn(qt_ref[h], ds)
        dq_ref[:, cols] = ((earlier_ref[h] + dot_nn(ds, keys)) * scale).astype(BF)
    part_ref[pl.ds(0, rows), :] = (dk * scale).T.astype(BF)
    part_ref[pl.ds(rows, rows), :] = dv.T.astype(BF)


def stack_kernel(two_ref, core_ref, own_ref, mixed_ref, out_ref):
    pieces, _, rows, _ = out_ref.shape
    for slot, (a, b) in enumerate(((two_ref, core_ref), (own_ref, mixed_ref))):
        for piece in range(pieces):
            at = pl.ds(piece * rows, rows)
            out_ref[piece, slot] = (a[at, :].astype(F32) + b[at, :].astype(F32)).astype(BF)


def score_scale(head):
    return 1.0 / math.sqrt(head)


def exp2_scale(head):
    return score_scale(head) * math.log2(math.e)


VMEM = pl.BlockSpec(memory_space=pltpu.VMEM)
SMEM = pl.BlockSpec(memory_space=pltpu.SMEM)


def shape(dims, dtype):
    return jax.ShapeDtypeStruct(dims, dtype)


def on_core(kernel, name, mflop, mib, outs, ins, scratch=(), aliases={}):
    return pl.pallas_call(
        kernel,
        out_shape=tuple(outs),
        in_specs=[SMEM if x.ndim == 1 else VMEM for x in ins],
        out_specs=tuple(SMEM if len(x.shape) == 1 else VMEM for x in outs),
        scratch_shapes=list(scratch),
        input_output_aliases=aliases,
        compiler_params=pltpu.CompilerParams(vmem_limit_bytes=mib << 20),
        cost_estimate=pl.CostEstimate(
            flops=mflop * 1_000_000, bytes_accessed=2 << 20, transcendentals=1 << 19
        ),
        name=name,
    )(*ins)


def sizes(q, own):
    rows, width = q.shape
    head = own.shape[1]
    heads = width // head
    state = shape((heads, rows, head), F32)
    turned = shape((heads, head, rows), BF)
    tile = shape((heads, rows, rows), F32)
    return state, turned, tile, shape(q.shape, BF), shape(own.shape, BF)


def attention_before(place, lengths, q, do, own):
    state, turned, _, _, _ = sizes(q, own)
    starts = shape(state.shape[1:], jnp.int32)
    outs = [shape((1,), jnp.int32), starts, state, state, state, turned, turned]
    return on_core(diagonal_kernel, "diagonal", 1200, 20, outs, (place, lengths, q, do, own))


def attention_second(first, q, starts, top, total, out, two):
    state, _, tile, _, _ = sizes(q, two)
    ins = (first, q, starts, top, total, out, two)
    return on_core(second_kernel, "second", 1200, 20, [state, state, state, tile], ins)


def attention_far(place, first, q, do, qt, dot_, starts, top, total, out, mixed, swapped):
    state, _, tile, like_q, part = sizes(q, mixed)
    rows, head = state.shape[1:]
    return on_core(
        far_kernel,
        "far",
        3000,
        24,
        [like_q] + [state] * 5 + [part] * 2,
        (place, first, q, do, qt, dot_, starts, top, total, out, mixed, swapped),
        [pltpu.VMEM((2 * rows, head), BF)] * 4
        + [pltpu.VMEM((state.shape[0], 2, rows, rows), F32), pltpu.VMEM(state.shape, F32)],
    )


def attention_second_back(first, q, do, qt, dot_, two, tile, factor, row_dot, dq):
    state, _, _, _, part = sizes(q, two)
    ins = (first, do, qt, dot_, two, tile, factor, row_dot, dq)
    return on_core(second_back_kernel, "second_back", 1500, 20, [state, part], ins)


def attention_own(q, do, qt, dot_, own, starts, top, inverse, row_dot, dq, attended):
    _, _, _, like_q, part = sizes(q, own)
    ins = (q, do, qt, dot_, own, starts, top, inverse, row_dot, dq, attended)
    return on_core(own_kernel, "own", 2500, 20, [like_q, part, like_q], ins)


def stacked(pieces, two, core, own, mixed):
    rows, head = own.shape
    out = shape((pieces, 2, rows // pieces, head), BF)
    return on_core(stack_kernel, "stack", 1, 6, [out], (two, core, own, mixed))[0]


def pack_kernel(key_ref, value_ref, both_ref, sems):
    rows = key_ref.shape[0]
    copies = [
        pltpu.make_async_copy(key_ref, both_ref.at[pl.ds(0, rows)], sems.at[0]),
        pltpu.make_async_copy(value_ref, both_ref.at[pl.ds(rows, rows)], sems.at[1]),
    ]
    for copy in copies:
        copy.start()
    for copy in copies:
        copy.wait()


def packed(keys, values):
    rows, head = keys.shape
    return pl.pallas_call(
        pack_kernel,
        out_shape=jax.ShapeDtypeStruct((2 * rows, head), BF),
        in_specs=[pl.BlockSpec(memory_space=pltpu.HBM)] * 2,
        out_specs=VMEM,
        scratch_shapes=[pltpu.SemaphoreType.DMA((2,))],
        compiler_params=pltpu.CompilerParams(vmem_limit_bytes=2 << 20),
        name="pack",
    )(keys, values)


def exchanged(pieces):
    return lax.all_to_all(pieces, "head", split_axis=0, concat_axis=0)


def moved(value, pairs):
    return lax.ppermute(value, "ctx", pairs)


def on_device(queries, keys, values, d_out, doc_lengths):
    count = lax.axis_size("ctx")
    rows = keys.shape[0]
    place = lax.axis_index("ctx").reshape(1).astype(jnp.int32)
    two_on = [(i, i + 2) for i in range(count - 2)]
    mixed_on = [(i, i + (3 if i % 2 else 1)) for i in range(count) if i + (3 if i % 2 else 1) < count]
    across = [(i, i ^ 1) for i in range(count)]

    def back(pairs):
        return [(there, here) for here, there in pairs]

    lengths = doc_lengths.reshape(1, -1)
    own = packed(keys, values)
    two = moved(own, two_on)
    mixed = moved(own, mixed_on)
    first, starts, top, total, out, qt, dot_ = attention_before(place, lengths, queries, d_out, own)
    two, first = lax.optimization_barrier((two, first))
    swapped = moved(two, across)
    top, total, out, tile = attention_second(first, queries, starts, top, total, out, two)
    attended, top, inverse, row_dot, factor, dq, mixed_part, swapped_part = attention_far(
        place, first, queries, d_out, qt, dot_, starts, top, total, out, mixed, swapped
    )
    from_mixed = moved(mixed_part, back(mixed_on))
    from_core = moved(swapped_part, across)
    dq, two_part = attention_second_back(
        first, queries, d_out, qt, dot_, two, tile, factor, row_dot, dq
    )
    d_queries, own_part, attended = attention_own(
        queries, d_out, qt, dot_, own, starts, top, inverse, row_dot, dq, attended
    )
    heads = lax.axis_size("head")
    quarters = exchanged(stacked(heads, two_part, from_core, own_part, from_mixed))
    passed, mine = jnp.sum(quarters.astype(F32), axis=0)
    from_two = moved(passed.astype(BF), back(two_on))
    mine = (mine + from_two.astype(F32)).astype(BF)
    both = exchanged(jnp.broadcast_to(mine[None], (heads,) + mine.shape)).reshape(own.shape)
    return (attended, d_queries, both[:rows], both[rows:])


def solution(mesh):
    in_specs = (P("ctx", "head"), P("ctx", None), P("ctx", None), P("ctx", "head"), P())
    out_specs = (P("ctx", "head"), P("ctx", "head"), P("ctx", None), P("ctx", None))
    return jax.shard_map(
        on_device, mesh=mesh, in_specs=in_specs, out_specs=out_specs, check_vma=False
    )
```

```python
import functools
import math

import jax
import jax.numpy as jnp
from jax import lax
from jax.experimental import pallas as pl
from jax.experimental.pallas import tpu as pltpu
from jax.sharding import PartitionSpec as P

SPAN = 3
BF = jnp.bfloat16
F32 = jnp.float32


def dot_nt(a, b):
    return lax.dot_general(a, b, (((1,), (1,)), ((), ())), preferred_element_type=F32)


def dot_nn(a, b):
    return jnp.dot(a, b, preferred_element_type=F32)


def wide(x, width):
    return jnp.concatenate([x] * (width // x.shape[1]), axis=1)


def folded(x, width, op):
    return functools.reduce(op, [x[:, c : c + width] for c in range(0, x.shape[1], width)])


def across_lanes(x, op, like):
    return jnp.broadcast_to(op(x, axis=1, keepdims=True), like.shape)


def lowest_block(first_ref, rows):
    return jnp.minimum(jnp.maximum(first_ref[0], 0) // rows, SPAN)


def diagonal_kernel(
    place_ref, lengths_ref, q_ref, do_ref, own_ref,
    first_ref, starts_ref, top_ref, total_ref, out_ref, qt_ref, dot_ref,
):
    rows, width = q_ref.shape
    head = own_ref.shape[1]
    heads = width // head
    lead = SPAN * rows
    lengths = lengths_ref[...].astype(F32)
    docs = lengths.shape[1]
    along = jnp.broadcast_to(lengths, (docs, docs))
    earlier = lax.broadcasted_iota(jnp.int32, (docs, docs), 0)
    later = lax.broadcasted_iota(jnp.int32, (docs, docs), 1)
    ends = jnp.sum(jnp.where(earlier <= later, along.T, 0.0), axis=0, keepdims=True)
    begin = (place_ref[0] * rows).astype(F32)
    positions = begin + lax.broadcasted_iota(jnp.int32, (rows, docs), 0).astype(F32)
    doc_start = jnp.sum(jnp.where(ends <= positions, lengths, 0.0), axis=1, keepdims=True)
    start = (doc_start - begin).astype(jnp.int32)
    starts_ref[...] = jnp.broadcast_to(start, starts_ref.shape)
    first_ref[0] = jnp.min(start) + lead

    column = lax.broadcasted_iota(jnp.int32, (rows, rows), 1)
    row = lax.broadcasted_iota(jnp.int32, (rows, rows), 0)
    allowed = (column >= start) & (column <= row)
    keys = own_ref[pl.ds(0, rows), :]
    values = own_ref[pl.ds(rows, rows), :]
    for h in range(heads):
        cols = pl.ds(h * head, head)
        s = jnp.where(allowed, dot_nt(q_ref[:, cols], keys), -jnp.inf)
        m = jnp.max(s, axis=1, keepdims=True)
        e = jnp.exp2((s - m) * exp2_scale(head))
        top_ref[h] = jnp.broadcast_to(m, (rows, head))
        total_ref[h] = jnp.broadcast_to(jnp.sum(e, axis=1, keepdims=True), (rows, head))
        out_ref[h] = dot_nn(e.astype(BF), values)
        qt_ref[h] = q_ref[:, cols].T
        dot_ref[h] = do_ref[:, cols].T


def second_kernel(
    first_ref, q_ref, starts_ref, top0_ref, total0_ref, out0_ref, block_ref,
    top_ref, total_ref, out_ref, tile_ref,
):
    rows, width = q_ref.shape
    head = block_ref.shape[1]
    heads = width // head
    to_exp2 = exp2_scale(head)
    place = SPAN - 2
    live = lowest_block(first_ref, rows) <= place

    @pl.when(live)
    def _():
        keys = block_ref[pl.ds(0, rows), :]
        values = block_ref[pl.ds(rows, rows), :]
        column = lax.broadcasted_iota(jnp.int32, (rows, rows), 1)
        allowed = column >= wide(starts_ref[...] + (SPAN - place) * rows, rows)
        for h in range(heads):
            s = jnp.where(allowed, dot_nt(q_ref[:, pl.ds(h * head, head)], keys), -jnp.inf)
            top0 = top0_ref[h]
            top = across_lanes(jnp.maximum(folded(s, head, jnp.maximum), top0), jnp.max, top0)
            e = jnp.exp2((s - wide(top, rows)) * to_exp2)
            kept = jnp.exp2((top0 - top) * to_exp2)
            tile_ref[h] = e
            top_ref[h] = top
            total_ref[h] = total0_ref[h] * kept + across_lanes(folded(e, head, jnp.add), jnp.sum, top)
            out_ref[h] = out0_ref[h] * kept + dot_nn(e.astype(BF), values)

    @pl.when(jnp.logical_not(live))
    def _():
        top_ref[...] = top0_ref[...]
        total_ref[...] = total0_ref[...]
        out_ref[...] = out0_ref[...]


def far_kernel(
    place_ref, first_ref, q_ref, do_ref, qt_ref, dot_ref, starts_ref, top0_ref, total0_ref, out0_ref,
    mixed_ref, swapped_ref,
    att_ref, top_ref, inverse_ref, row_dot_ref, second_ref, dq_ref, mixed_part_ref, swapped_part_ref,
    window, parts,
):
    rows, width = q_ref.shape
    head = mixed_ref.shape[1]
    heads = width // head
    to_exp2 = exp2_scale(head)
    scale = score_scale(head)
    odd = lax.rem(place_ref[0], 2)
    slots = ((mixed_ref, mixed_part_ref, 1 - odd), (swapped_ref, swapped_part_ref, odd))
    low = lowest_block(first_ref, rows)
    live = (low < SPAN).astype(jnp.int32) + (low < 1).astype(jnp.int32)
    def on_rows(r0, n, blocks):
        row = pl.ds(r0, n)
        keys = [window[b, pl.ds(k0, m), :] for b, k0, m in blocks]
        values = [window[b, pl.ds(rows + k0, m), :] for b, k0, m in blocks]
        allowed = [
            lax.broadcasted_iota(jnp.int32, (n, m), 1)
            >= wide(starts_ref[row, :] + ((1 + 2 * b) * rows - k0), m)
            for b, k0, m in blocks
        ]
        dv = [jnp.zeros((head, m), F32) for _, _, m in blocks]
        dk = [jnp.zeros((head, m), F32) for _, _, m in blocks]
        for h in range(heads):
            cols = pl.ds(h * head, head)
            top = top0 = top0_ref[h, row, :]
            total = total0_ref[h, row, :]
            out = out0_ref[h, row, :]
            kept = 1.0
            e = []
            if blocks:
                s = [
                    jnp.where(ok, dot_nt(q_ref[row, cols], k), -jnp.inf)
                    for ok, k in zip(allowed, keys)
                ]
                for x in s:
                    top = jnp.maximum(top, folded(x, head, jnp.maximum))
                top = across_lanes(top, jnp.max, top)
                kept = jnp.exp2((top0 - top) * to_exp2)
                e = [jnp.exp2((x - wide(top, x.shape[1])) * to_exp2) for x in s]
                sums = functools.reduce(jnp.add, [folded(x, head, jnp.add) for x in e])
                total = total * kept + across_lanes(sums, jnp.sum, top)
                out = out * kept
                for x, v in zip(e, values):
                    out = out + dot_nn(x.astype(BF), v)
            inverse = 1.0 / total
            attended = (out * inverse).astype(BF)
            products = do_ref[row, cols].astype(F32) * attended.astype(F32)
            row_dot = across_lanes(products, jnp.sum, top)
            att_ref[row, cols] = attended
            top_ref[h, row, :] = top
            inverse_ref[h, row, :] = inverse
            row_dot_ref[h, row, :] = row_dot
            second_ref[h, row, :] = kept * inverse
            dq = jnp.zeros((n, head), F32)
            for i, (x, k, v) in enumerate(zip(e, keys, values)):
                m = x.shape[1]
                dw = dot_nt(do_ref[row, cols], v)
                w = x * wide(inverse, m)
                ds = (w * (dw - wide(row_dot, m))).astype(BF)
                dv[i] = dv[i] + dot_nn(dot_ref[h, :, row], w.astype(BF))
                dk[i] = dk[i] + dot_nn(qt_ref[h, :, row], ds)
                dq = dq + dot_nn(ds, k)
            dq_ref[h, row, :] = dq
        for (b, k0, m), a, c in zip(blocks, dk, dv):
            parts[b, pl.ds(k0, m), :] = (a * scale).T.astype(BF)
            parts[b, pl.ds(rows + k0, m), :] = c.T.astype(BF)

    for block, _, at in slots:
        @pl.when(at < live)
        def _():
            window[at] = block[...]

    half = rows // 2
    near, far = (0, 0, rows), (1, 0, rows)
    low_half = first_ref[0] < half

    @pl.when(live < 2)
    def _():
        parts[1] = jnp.zeros(parts.shape[1:], BF)

    @pl.when(live == 0)
    def _():
        parts[0] = jnp.zeros(parts.shape[1:], BF)
        on_rows(0, rows, [])

    @pl.when(live == 1)
    def _():
        on_rows(0, rows, [near])

    @pl.when((live == 2) & low_half)
    def _():
        on_rows(0, half, [near, far])
        on_rows(half, half, [])

    @pl.when((live == 2) & jnp.logical_not(low_half))
    def _():
        parts[1] = jnp.zeros(parts.shape[1:], BF)
        on_rows(0, rows, [near, (1, half, half)])

    for _, part, at in slots:
        part[...] = parts[at]


def second_back_kernel(
    first_ref, do_ref, qt_ref, dot_ref, block_ref, tile_ref, factor_ref, row_dot_ref, far_ref,
    dq_ref, part_ref,
):
    heads, rows, head = far_ref.shape
    scale = score_scale(head)
    live = lowest_block(first_ref, rows) <= SPAN - 2

    @pl.when(live)
    def _():
        keys = block_ref[pl.ds(0, rows), :]
        values = block_ref[pl.ds(rows, rows), :]
        dv = jnp.zeros((head, rows), F32)
        dk = jnp.zeros((head, rows), F32)
        for h in range(heads):
            dw = dot_nt(do_ref[:, pl.ds(h * head, head)], values)
            w = tile_ref[h] * wide(factor_ref[h], rows)
            ds = (w * (dw - wide(row_dot_ref[h], rows))).astype(BF)
            dv = dv + dot_nn(dot_ref[h], w.astype(BF))
            dk = dk + dot_nn(qt_ref[h], ds)
            dq_ref[h] = far_ref[h] + dot_nn(ds, keys)
        part_ref[pl.ds(0, rows), :] = (dk * scale).T.astype(BF)
        part_ref[pl.ds(rows, rows), :] = dv.T.astype(BF)

    @pl.when(jnp.logical_not(live))
    def _():
        dq_ref[...] = far_ref[...]
        part_ref[...] = jnp.zeros(part_ref.shape, BF)


def own_kernel(
    q_ref, do_ref, qt_ref, dot_ref, own_ref, starts_ref, top_ref, inverse_ref, row_dot_ref, earlier_ref,
    attended_ref, dq_ref, part_ref, att_ref,
):
    rows, width = q_ref.shape
    head = own_ref.shape[1]
    heads = width // head
    to_exp2 = exp2_scale(head)
    scale = score_scale(head)
    column = lax.broadcasted_iota(jnp.int32, (rows, rows), 1)
    row = lax.broadcasted_iota(jnp.int32, (rows, rows), 0)
    allowed = (column >= wide(starts_ref[...], rows)) & (column <= row)
    keys = own_ref[pl.ds(0, rows), :]
    values = own_ref[pl.ds(rows, rows), :]
    dv = jnp.zeros((head, rows), F32)
    dk = jnp.zeros((head, rows), F32)
    att_ref[...] = attended_ref[...]
    for h in range(heads):
        cols = pl.ds(h * head, head)
        s = jnp.where(allowed, dot_nt(q_ref[:, cols], keys), -jnp.inf)
        w = jnp.exp2((s - wide(top_ref[h], rows)) * to_exp2) * wide(inverse_ref[h], rows)
        dw = dot_nt(do_ref[:, cols], values)
        ds = (w * (dw - wide(row_dot_ref[h], rows))).astype(BF)
        dv = dv + dot_nn(dot_ref[h], w.astype(BF))
        dk = dk + dot_nn(qt_ref[h], ds)
        dq_ref[:, cols] = ((earlier_ref[h] + dot_nn(ds, keys)) * scale).astype(BF)
    part_ref[pl.ds(0, rows), :] = (dk * scale).T.astype(BF)
    part_ref[pl.ds(rows, rows), :] = dv.T.astype(BF)


def sum_kernel(*refs):
    *terms, out_ref = refs
    out_ref[...] = sum(x[...].astype(F32) for x in terms).astype(BF)


def score_scale(head):
    return 1.0 / math.sqrt(head)


def exp2_scale(head):
    return score_scale(head) * math.log2(math.e)


VMEM = pl.BlockSpec(memory_space=pltpu.VMEM)
SMEM = pl.BlockSpec(memory_space=pltpu.SMEM)


def shape(dims, dtype):
    return jax.ShapeDtypeStruct(dims, dtype)


def on_core(kernel, name, mflop, mib, outs, ins, scratch=(), aliases={}):
    return pl.pallas_call(
        kernel,
        out_shape=tuple(outs),
        in_specs=[SMEM if x.ndim == 1 else VMEM for x in ins],
        out_specs=tuple(SMEM if len(x.shape) == 1 else VMEM for x in outs),
        scratch_shapes=list(scratch),
        input_output_aliases=aliases,
        compiler_params=pltpu.CompilerParams(vmem_limit_bytes=mib << 20),
        cost_estimate=pl.CostEstimate(
            flops=mflop * 1_000_000, bytes_accessed=2 << 20, transcendentals=1 << 19
        ),
        name=name,
    )(*ins)


def sizes(q, own):
    rows, width = q.shape
    head = own.shape[1]
    heads = width // head
    state = shape((heads, rows, head), F32)
    turned = shape((heads, head, rows), BF)
    tile = shape((heads, rows, rows), F32)
    return state, turned, tile, shape(q.shape, BF), shape(own.shape, BF)


def attention_before(place, lengths, q, do, own):
    state, turned, _, _, _ = sizes(q, own)
    starts = shape(state.shape[1:], jnp.int32)
    outs = [shape((1,), jnp.int32), starts, state, state, state, turned, turned]
    return on_core(diagonal_kernel, "diagonal", 1200, 20, outs, (place, lengths, q, do, own))


def attention_second(first, q, starts, top, total, out, two):
    state, _, tile, _, _ = sizes(q, two)
    ins = (first, q, starts, top, total, out, two)
    return on_core(second_kernel, "second", 1200, 20, [state, state, state, tile], ins)


def attention_far(place, first, q, do, qt, dot_, starts, top, total, out, mixed, swapped):
    state, _, tile, like_q, part = sizes(q, mixed)
    rows, head = state.shape[1:]
    return on_core(
        far_kernel,
        "far",
        3000,
        24,
        [like_q] + [state] * 5 + [part] * 2,
        (place, first, q, do, qt, dot_, starts, top, total, out, mixed, swapped),
        [pltpu.VMEM((2, 2 * rows, head), BF)] * 2,
    )


def attention_second_back(first, q, do, qt, dot_, two, tile, factor, row_dot, dq):
    state, _, _, _, part = sizes(q, two)
    ins = (first, do, qt, dot_, two, tile, factor, row_dot, dq)
    return on_core(second_back_kernel, "second_back", 1500, 20, [state, part], ins)


def attention_own(q, do, qt, dot_, own, starts, top, inverse, row_dot, dq, attended):
    _, _, _, like_q, part = sizes(q, own)
    ins = (q, do, qt, dot_, own, starts, top, inverse, row_dot, dq, attended)
    return on_core(own_kernel, "own", 2500, 20, [like_q, part, like_q], ins)


def summed(*terms):
    return on_core(sum_kernel, "sum", 1, 6, [shape(terms[0].shape, BF)], terms)[0]


def pack_kernel(key_ref, value_ref, both_ref, sems):
    rows = key_ref.shape[0]
    copies = [
        pltpu.make_async_copy(key_ref, both_ref.at[pl.ds(0, rows)], sems.at[0]),
        pltpu.make_async_copy(value_ref, both_ref.at[pl.ds(rows, rows)], sems.at[1]),
    ]
    for copy in copies:
        copy.start()
    for copy in copies:
        copy.wait()


def packed(keys, values):
    rows, head = keys.shape
    return pl.pallas_call(
        pack_kernel,
        out_shape=jax.ShapeDtypeStruct((2 * rows, head), BF),
        in_specs=[pl.BlockSpec(memory_space=pltpu.HBM)] * 2,
        out_specs=VMEM,
        scratch_shapes=[pltpu.SemaphoreType.DMA((2,))],
        compiler_params=pltpu.CompilerParams(vmem_limit_bytes=2 << 20),
        name="pack",
    )(keys, values)


def head_sum(part):
    heads = lax.axis_size("head")
    pieces = part.reshape(heads, part.shape[0] // heads, part.shape[1])
    theirs = lax.all_to_all(pieces, "head", split_axis=0, concat_axis=0)
    mine = jnp.sum(theirs.astype(F32), axis=0).astype(BF)
    mine = jnp.broadcast_to(mine[None], pieces.shape)
    return lax.all_to_all(mine, "head", split_axis=0, concat_axis=0).reshape(part.shape)


def moved(value, pairs):
    return lax.ppermute(value, "ctx", pairs)


def on_device(queries, keys, values, d_out, doc_lengths):
    count = lax.axis_size("ctx")
    rows = keys.shape[0]
    place = lax.axis_index("ctx").reshape(1).astype(jnp.int32)
    two_on = [(i, i + 2) for i in range(count - 2)]
    mixed_on = [(i, i + (3 if i % 2 else 1)) for i in range(count) if i + (3 if i % 2 else 1) < count]
    across = [(i, i ^ 1) for i in range(count)]

    def back(pairs):
        return [(there, here) for here, there in pairs]

    lengths = doc_lengths.reshape(1, -1)
    own = packed(keys, values)
    two = moved(own, two_on)
    mixed = moved(own, mixed_on)
    first, starts, top, total, out, qt, dot_ = attention_before(place, lengths, queries, d_out, own)
    two, first = lax.optimization_barrier((two, first))
    swapped = moved(two, across)
    top, total, out, tile = attention_second(first, queries, starts, top, total, out, two)
    attended, top, inverse, row_dot, factor, dq, mixed_part, swapped_part = attention_far(
        place, first, queries, d_out, qt, dot_, starts, top, total, out, mixed, swapped
    )
    from_mixed = moved(mixed_part, back(mixed_on))
    from_core = moved(swapped_part, across)
    dq, two_part = attention_second_back(
        first, queries, d_out, qt, dot_, two, tile, factor, row_dot, dq
    )
    from_two = moved(summed(two_part, from_core), back(two_on))
    d_queries, own_part, attended = attention_own(
        queries, d_out, qt, dot_, own, starts, top, inverse, row_dot, dq, attended
    )
    both = head_sum(summed(own_part, from_two, from_mixed))
    return (attended, d_queries, both[:rows], both[rows:])


def solution(mesh):
    in_specs = (P("ctx", "head"), P("ctx", None), P("ctx", None), P("ctx", "head"), P())
    out_specs = (P("ctx", "head"), P("ctx", "head"), P("ctx", None), P("ctx", None))
    return jax.shard_map(
        on_device, mesh=mesh, in_specs=in_specs, out_specs=out_specs, check_vma=False
    )
```

```python
import functools
import math

import jax
import jax.numpy as jnp
from jax import lax
from jax.experimental import pallas as pl
from jax.experimental.pallas import tpu as pltpu
from jax.sharding import PartitionSpec as P

SPAN = 3
BF = jnp.bfloat16
F32 = jnp.float32


def dot_nt(a, b):
    return lax.dot_general(a, b, (((1,), (1,)), ((), ())), preferred_element_type=F32)


def dot_nn(a, b):
    return jnp.dot(a, b, preferred_element_type=F32)


def wide(x, width):
    return jnp.concatenate([x] * (width // x.shape[1]), axis=1)


def folded(x, width, op):
    return functools.reduce(op, [x[:, c : c + width] for c in range(0, x.shape[1], width)])


def across_lanes(x, op, like):
    return jnp.broadcast_to(op(x, axis=1, keepdims=True), like.shape)


def lowest_block(first_ref, rows):
    return jnp.minimum(jnp.maximum(first_ref[0], 0) // rows, SPAN)


def diagonal_kernel(
    place_ref, lengths_ref, q_ref, do_ref, own_ref,
    first_ref, starts_ref, top_ref, total_ref, out_ref, qt_ref, dot_ref,
):
    rows, width = q_ref.shape
    head = own_ref.shape[1]
    heads = width // head
    lead = SPAN * rows
    lengths = lengths_ref[...].astype(F32)
    docs = lengths.shape[1]
    along = jnp.broadcast_to(lengths, (docs, docs))
    earlier = lax.broadcasted_iota(jnp.int32, (docs, docs), 0)
    later = lax.broadcasted_iota(jnp.int32, (docs, docs), 1)
    ends = jnp.sum(jnp.where(earlier <= later, along.T, 0.0), axis=0, keepdims=True)
    begin = (place_ref[0] * rows).astype(F32)
    positions = begin + lax.broadcasted_iota(jnp.int32, (rows, docs), 0).astype(F32)
    doc_start = jnp.sum(jnp.where(ends <= positions, lengths, 0.0), axis=1, keepdims=True)
    start = (doc_start - begin).astype(jnp.int32)
    starts_ref[...] = jnp.broadcast_to(start, starts_ref.shape)
    first_ref[0] = jnp.min(start) + lead
    first_ref[1] = jnp.sum(jnp.where(start < 0, 1, 0))

    column = lax.broadcasted_iota(jnp.int32, (rows, rows), 1)
    row = lax.broadcasted_iota(jnp.int32, (rows, rows), 0)
    allowed = (column >= start) & (column <= row)
    keys = own_ref[pl.ds(0, rows), :]
    values = own_ref[pl.ds(rows, rows), :]
    for h in range(heads):
        cols = pl.ds(h * head, head)
        s = jnp.where(allowed, dot_nt(q_ref[:, cols], keys), -jnp.inf)
        m = jnp.max(s, axis=1, keepdims=True)
        e = jnp.exp2((s - m) * exp2_scale(head))
        top_ref[h] = jnp.broadcast_to(m, (rows, head))
        total_ref[h] = jnp.broadcast_to(jnp.sum(e, axis=1, keepdims=True), (rows, head))
        out_ref[h] = dot_nn(e.astype(BF), values)
        qt_ref[h] = q_ref[:, cols].T
        dot_ref[h] = do_ref[:, cols].T


def second_kernel(
    first_ref, q_ref, starts_ref, top0_ref, total0_ref, out0_ref, block_ref,
    top_ref, total_ref, out_ref, tile_ref,
):
    rows, width = q_ref.shape
    head = block_ref.shape[1]
    heads = width // head
    to_exp2 = exp2_scale(head)
    place = SPAN - 2
    live = lowest_block(first_ref, rows) <= place
    reached = first_ref[1]
    half = rows // 2

    def on_rows(n):
        row = pl.ds(0, n)
        keys = block_ref[pl.ds(0, rows), :]
        values = block_ref[pl.ds(rows, rows), :]
        column = lax.broadcasted_iota(jnp.int32, (n, rows), 1)
        allowed = column >= wide(starts_ref[row, :] + (SPAN - place) * rows, rows)
        for h in range(heads):
            s = jnp.where(allowed, dot_nt(q_ref[row, pl.ds(h * head, head)], keys), -jnp.inf)
            top0 = top0_ref[h, row, :]
            top = across_lanes(jnp.maximum(folded(s, head, jnp.maximum), top0), jnp.max, top0)
            e = jnp.exp2((s - wide(top, rows)) * to_exp2)
            kept = jnp.exp2((top0 - top) * to_exp2)
            tile_ref[h, row, :] = e
            top_ref[h, row, :] = top
            sums = across_lanes(folded(e, head, jnp.add), jnp.sum, top)
            total_ref[h, row, :] = total0_ref[h, row, :] * kept + sums
            out_ref[h, row, :] = out0_ref[h, row, :] * kept + dot_nn(e.astype(BF), values)

    def keep_rows(r0):
        row = pl.ds(r0, rows - r0)
        for h in range(heads):
            top_ref[h, row, :] = top0_ref[h, row, :]
            total_ref[h, row, :] = total0_ref[h, row, :]
            out_ref[h, row, :] = out0_ref[h, row, :]

    @pl.when(live & (reached <= half))
    def _():
        on_rows(half)
        keep_rows(half)

    @pl.when(live & (reached > half))
    def _():
        on_rows(rows)

    @pl.when(jnp.logical_not(live))
    def _():
        keep_rows(0)


def far_kernel(
    place_ref, first_ref, q_ref, do_ref, qt_ref, dot_ref, starts_ref, top0_ref, total0_ref, out0_ref,
    mixed_ref, swapped_ref,
    att_ref, top_ref, inverse_ref, row_dot_ref, second_ref, dq_ref, mixed_part_ref, swapped_part_ref,
    window, parts,
):
    rows, width = q_ref.shape
    head = mixed_ref.shape[1]
    heads = width // head
    to_exp2 = exp2_scale(head)
    scale = score_scale(head)
    odd = lax.rem(place_ref[0], 2)
    slots = ((mixed_ref, mixed_part_ref, 1 - odd), (swapped_ref, swapped_part_ref, odd))
    low = lowest_block(first_ref, rows)
    live = (low < SPAN).astype(jnp.int32) + (low < 1).astype(jnp.int32)
    def on_rows(r0, n, blocks):
        row = pl.ds(r0, n)
        keys = [window[b, pl.ds(k0, m), :] for b, k0, m in blocks]
        values = [window[b, pl.ds(rows + k0, m), :] for b, k0, m in blocks]
        allowed = [
            lax.broadcasted_iota(jnp.int32, (n, m), 1)
            >= wide(starts_ref[row, :] + ((1 + 2 * b) * rows - k0), m)
            for b, k0, m in blocks
        ]
        dv = [jnp.zeros((head, m), F32) for _, _, m in blocks]
        dk = [jnp.zeros((head, m), F32) for _, _, m in blocks]
        for h in range(heads):
            cols = pl.ds(h * head, head)
            top = top0 = top0_ref[h, row, :]
            total = total0_ref[h, row, :]
            out = out0_ref[h, row, :]
            kept = 1.0
            e = []
            if blocks:
                s = [
                    jnp.where(ok, dot_nt(q_ref[row, cols], k), -jnp.inf)
                    for ok, k in zip(allowed, keys)
                ]
                for x in s:
                    top = jnp.maximum(top, folded(x, head, jnp.maximum))
                top = across_lanes(top, jnp.max, top)
                kept = jnp.exp2((top0 - top) * to_exp2)
                e = [jnp.exp2((x - wide(top, x.shape[1])) * to_exp2) for x in s]
                sums = functools.reduce(jnp.add, [folded(x, head, jnp.add) for x in e])
                total = total * kept + across_lanes(sums, jnp.sum, top)
                out = out * kept
                for x, v in zip(e, values):
                    out = out + dot_nn(x.astype(BF), v)
            inverse = 1.0 / total
            attended = (out * inverse).astype(BF)
            products = do_ref[row, cols].astype(F32) * attended.astype(F32)
            row_dot = across_lanes(products, jnp.sum, top)
            att_ref[row, cols] = attended
            top_ref[h, row, :] = top
            inverse_ref[h, row, :] = inverse
            row_dot_ref[h, row, :] = row_dot
            second_ref[h, row, :] = kept * inverse
            dq = jnp.zeros((n, head), F32)
            for i, (x, k, v) in enumerate(zip(e, keys, values)):
                m = x.shape[1]
                dw = dot_nt(do_ref[row, cols], v)
                w = x * wide(inverse, m)
                ds = (w * (dw - wide(row_dot, m))).astype(BF)
                dv[i] = dv[i] + dot_nn(dot_ref[h, :, row], w.astype(BF))
                dk[i] = dk[i] + dot_nn(qt_ref[h, :, row], ds)
                dq = dq + dot_nn(ds, k)
            dq_ref[h, row, :] = dq
        for (b, k0, m), a, c in zip(blocks, dk, dv):
            parts[b, pl.ds(k0, m), :] = (a * scale).T.astype(BF)
            parts[b, pl.ds(rows + k0, m), :] = c.T.astype(BF)

    for block, _, at in slots:
        @pl.when(at < live)
        def _():
            window[at] = block[...]

    half, quarter = rows // 2, rows // 4
    near, far = (0, 0, rows), (1, 0, rows)
    reached = first_ref[1]

    for block, _, at in slots:
        @pl.when(at < live)
        def _():
            window[at] = block[...]

    half = rows // 2
    near, far = (0, 0, rows), (1, 0, rows)
    low_half = first_ref[0] < half

    @pl.when(live < 2)
    def _():
        parts[1] = jnp.zeros(parts.shape[1:], BF)

    @pl.when(live == 0)
    def _():
        parts[0] = jnp.zeros(parts.shape[1:], BF)
        on_rows(0, rows, [])

    @pl.when((live == 1) & (reached <= half))
    def _():
        on_rows(0, half, [near])
        on_rows(half, half, [])

    @pl.when((live == 1) & (reached > half))
    def _():
        on_rows(0, rows, [near])

    @pl.when((live == 2) & (reached <= half))
    def _():
        on_rows(0, half, [near, far])
        on_rows(half, half, [])

    @pl.when((live == 2) & (reached > half) & (reached <= rows - quarter))
    def _():
        parts[1] = jnp.zeros(parts.shape[1:], BF)
        on_rows(0, rows - quarter, [near, (1, half, half)])
        on_rows(rows - quarter, quarter, [])

    @pl.when((live == 2) & (reached > rows - quarter))
    def _():
        parts[1] = jnp.zeros(parts.shape[1:], BF)
        on_rows(0, rows, [near, (1, rows - quarter, quarter)])

    for _, part, at in slots:
        part[...] = parts[at]


def second_back_kernel(
    first_ref, do_ref, qt_ref, dot_ref, block_ref, tile_ref, factor_ref, row_dot_ref, far_ref,
    dq_ref, part_ref,
):
    heads, rows, head = far_ref.shape
    scale = score_scale(head)
    live = lowest_block(first_ref, rows) <= SPAN - 2
    reached = first_ref[1]
    half = rows // 2

    def on_rows(n):
        row = pl.ds(0, n)
        keys = block_ref[pl.ds(0, rows), :]
        values = block_ref[pl.ds(rows, rows), :]
        dv = jnp.zeros((head, rows), F32)
        dk = jnp.zeros((head, rows), F32)
        for h in range(heads):
            dw = dot_nt(do_ref[row, pl.ds(h * head, head)], values)
            w = tile_ref[h, row, :] * wide(factor_ref[h, row, :], rows)
            ds = (w * (dw - wide(row_dot_ref[h, row, :], rows))).astype(BF)
            dv = dv + dot_nn(dot_ref[h, :, row], w.astype(BF))
            dk = dk + dot_nn(qt_ref[h, :, row], ds)
            dq_ref[h, row, :] = far_ref[h, row, :] + dot_nn(ds, keys)
        part_ref[pl.ds(0, rows), :] = (dk * scale).T.astype(BF)
        part_ref[pl.ds(rows, rows), :] = dv.T.astype(BF)

    @pl.when(live & (reached <= half))
    def _():
        on_rows(half)
        for h in range(heads):
            dq_ref[h, pl.ds(half, half), :] = far_ref[h, pl.ds(half, half), :]

    @pl.when(live & (reached > half))
    def _():
        on_rows(rows)

    @pl.when(jnp.logical_not(live))
    def _():
        dq_ref[...] = far_ref[...]
        part_ref[...] = jnp.zeros(part_ref.shape, BF)


def own_kernel(
    q_ref, do_ref, qt_ref, dot_ref, own_ref, starts_ref, top_ref, inverse_ref, row_dot_ref, earlier_ref,
    attended_ref, dq_ref, part_ref, att_ref,
):
    rows, width = q_ref.shape
    head = own_ref.shape[1]
    heads = width // head
    to_exp2 = exp2_scale(head)
    scale = score_scale(head)
    column = lax.broadcasted_iota(jnp.int32, (rows, rows), 1)
    row = lax.broadcasted_iota(jnp.int32, (rows, rows), 0)
    allowed = (column >= wide(starts_ref[...], rows)) & (column <= row)
    keys = own_ref[pl.ds(0, rows), :]
    values = own_ref[pl.ds(rows, rows), :]
    dv = jnp.zeros((head, rows), F32)
    dk = jnp.zeros((head, rows), F32)
    att_ref[...] = attended_ref[...]
    for h in range(heads):
        cols = pl.ds(h * head, head)
        s = jnp.where(allowed, dot_nt(q_ref[:, cols], keys), -jnp.inf)
        w = jnp.exp2((s - wide(top_ref[h], rows)) * to_exp2) * wide(inverse_ref[h], rows)
        dw = dot_nt(do_ref[:, cols], values)
        ds = (w * (dw - wide(row_dot_ref[h], rows))).astype(BF)
        dv = dv + dot_nn(dot_ref[h], w.astype(BF))
        dk = dk + dot_nn(qt_ref[h], ds)
        dq_ref[:, cols] = ((earlier_ref[h] + dot_nn(ds, keys)) * scale).astype(BF)
    part_ref[pl.ds(0, rows), :] = (dk * scale).T.astype(BF)
    part_ref[pl.ds(rows, rows), :] = dv.T.astype(BF)


def sum_kernel(*refs):
    *terms, out_ref = refs
    out_ref[...] = sum(x[...].astype(F32) for x in terms).astype(BF)


def score_scale(head):
    return 1.0 / math.sqrt(head)


def exp2_scale(head):
    return score_scale(head) * math.log2(math.e)


VMEM = pl.BlockSpec(memory_space=pltpu.VMEM)
SMEM = pl.BlockSpec(memory_space=pltpu.SMEM)


def shape(dims, dtype):
    return jax.ShapeDtypeStruct(dims, dtype)


def on_core(kernel, name, mflop, mib, outs, ins, scratch=(), aliases={}):
    return pl.pallas_call(
        kernel,
        out_shape=tuple(outs),
        in_specs=[SMEM if x.ndim == 1 else VMEM for x in ins],
        out_specs=tuple(SMEM if len(x.shape) == 1 else VMEM for x in outs),
        scratch_shapes=list(scratch),
        input_output_aliases=aliases,
        compiler_params=pltpu.CompilerParams(vmem_limit_bytes=mib << 20),
        cost_estimate=pl.CostEstimate(
            flops=mflop * 1_000_000, bytes_accessed=2 << 20, transcendentals=1 << 19
        ),
        name=name,
    )(*ins)


def sizes(q, own):
    rows, width = q.shape
    head = own.shape[1]
    heads = width // head
    state = shape((heads, rows, head), F32)
    turned = shape((heads, head, rows), BF)
    tile = shape((heads, rows, rows), F32)
    return state, turned, tile, shape(q.shape, BF), shape(own.shape, BF)


def attention_before(place, lengths, q, do, own):
    state, turned, _, _, _ = sizes(q, own)
    starts = shape(state.shape[1:], jnp.int32)
    outs = [shape((2,), jnp.int32), starts, state, state, state, turned, turned]
    return on_core(diagonal_kernel, "diagonal", 1200, 20, outs, (place, lengths, q, do, own))


def attention_second(first, q, starts, top, total, out, two):
    state, _, tile, _, _ = sizes(q, two)
    ins = (first, q, starts, top, total, out, two)
    return on_core(second_kernel, "second", 1200, 20, [state, state, state, tile], ins)


def attention_far(place, first, q, do, qt, dot_, starts, top, total, out, mixed, swapped):
    state, _, tile, like_q, part = sizes(q, mixed)
    rows, head = state.shape[1:]
    return on_core(
        far_kernel,
        "far",
        3000,
        24,
        [like_q] + [state] * 5 + [part] * 2,
        (place, first, q, do, qt, dot_, starts, top, total, out, mixed, swapped),
        [pltpu.VMEM((2, 2 * rows, head), BF)] * 2,
    )


def attention_second_back(first, q, do, qt, dot_, two, tile, factor, row_dot, dq):
    state, _, _, _, part = sizes(q, two)
    ins = (first, do, qt, dot_, two, tile, factor, row_dot, dq)
    return on_core(second_back_kernel, "second_back", 1500, 20, [state, part], ins)


def attention_own(q, do, qt, dot_, own, starts, top, inverse, row_dot, dq, attended):
    _, _, _, like_q, part = sizes(q, own)
    ins = (q, do, qt, dot_, own, starts, top, inverse, row_dot, dq, attended)
    return on_core(own_kernel, "own", 2500, 20, [like_q, part, like_q], ins)


def summed(*terms):
    return on_core(sum_kernel, "sum", 1, 6, [shape(terms[0].shape, BF)], terms)[0]


def pack_kernel(key_ref, value_ref, both_ref, sems):
    rows = key_ref.shape[0]
    copies = [
        pltpu.make_async_copy(key_ref, both_ref.at[pl.ds(0, rows)], sems.at[0]),
        pltpu.make_async_copy(value_ref, both_ref.at[pl.ds(rows, rows)], sems.at[1]),
    ]
    for copy in copies:
        copy.start()
    for copy in copies:
        copy.wait()


def packed(keys, values):
    rows, head = keys.shape
    return pl.pallas_call(
        pack_kernel,
        out_shape=jax.ShapeDtypeStruct((2 * rows, head), BF),
        in_specs=[pl.BlockSpec(memory_space=pltpu.HBM)] * 2,
        out_specs=VMEM,
        scratch_shapes=[pltpu.SemaphoreType.DMA((2,))],
        compiler_params=pltpu.CompilerParams(vmem_limit_bytes=2 << 20),
        name="pack",
    )(keys, values)


def head_sum(part):
    heads = lax.axis_size("head")
    pieces = part.reshape(heads, part.shape[0] // heads, part.shape[1])
    theirs = lax.all_to_all(pieces, "head", split_axis=0, concat_axis=0)
    mine = jnp.sum(theirs.astype(F32), axis=0).astype(BF)
    mine = jnp.broadcast_to(mine[None], pieces.shape)
    return lax.all_to_all(mine, "head", split_axis=0, concat_axis=0).reshape(part.shape)


def moved(value, pairs):
    return lax.ppermute(value, "ctx", pairs)


def on_device(queries, keys, values, d_out, doc_lengths):
    count = lax.axis_size("ctx")
    rows = keys.shape[0]
    place = lax.axis_index("ctx").reshape(1).astype(jnp.int32)
    two_on = [(i, i + 2) for i in range(count - 2)]
    mixed_on = [(i, i + (3 if i % 2 else 1)) for i in range(count) if i + (3 if i % 2 else 1) < count]
    across = [(i, i ^ 1) for i in range(count)]

    def back(pairs):
        return [(there, here) for here, there in pairs]

    lengths = doc_lengths.reshape(1, -1)
    own = packed(keys, values)
    two = moved(own, two_on)
    mixed = moved(own, mixed_on)
    first, starts, top, total, out, qt, dot_ = attention_before(place, lengths, queries, d_out, own)
    two, first = lax.optimization_barrier((two, first))
    swapped = moved(two, across)
    top, total, out, tile = attention_second(first, queries, starts, top, total, out, two)
    attended, top, inverse, row_dot, factor, dq, mixed_part, swapped_part = attention_far(
        place, first, queries, d_out, qt, dot_, starts, top, total, out, mixed, swapped
    )
    from_mixed = moved(mixed_part, back(mixed_on))
    from_core = moved(swapped_part, across)
    dq, two_part = attention_second_back(
        first, queries, d_out, qt, dot_, two, tile, factor, row_dot, dq
    )
    from_two = moved(summed(two_part, from_core), back(two_on))
    d_queries, own_part, attended = attention_own(
        queries, d_out, qt, dot_, own, starts, top, inverse, row_dot, dq, attended
    )
    both = head_sum(summed(own_part, from_two, from_mixed))
    return (attended, d_queries, both[:rows], both[rows:])


def solution(mesh):
    in_specs = (P("ctx", "head"), P("ctx", None), P("ctx", None), P("ctx", "head"), P())
    out_specs = (P("ctx", "head"), P("ctx", "head"), P("ctx", None), P("ctx", None))
    return jax.shard_map(
        on_device, mesh=mesh, in_specs=in_specs, out_specs=out_specs, check_vma=False
    )
```
